256 devices in a mesh: frame: 8 (over z), space: 4 (over y_lo, core), tensor: 8 (over y_hi, x).
Axes of the slice: x: 4, y: 4 (y_hi: 2, y_lo: 2; y = y_hi * 2 + y_lo), z: 8, core: 2. Of those that a mesh axis runs over, the one named last changes fastest.
Arguments:
- inputs: bfloat16 [2, 16, 576, 2048], P(None, 'frame', 'space'), may hold values from -6 to 6
- upstream: bfloat16 [2, 16, 576, 2048], P(None, 'frame', 'space'), may hold values from -6 to 6
- action_ids: int32 [2, 16], P(None, 'frame'), may hold values from 0 to 7
- frame_time: int32 [2, 16], replicated, may hold values from 0 to 15, each once within a row
- action_table: float32 [8, 2048], replicated, may hold values from -3 to 3
- gain: float32 [2048], replicated, may hold values from 0.5 to 1.5
- w_qkv: bfloat16 [2048, 3, 2048], P(('frame', 'space'), None, 'tensor'), may hold values from -1 to 1
- w_out: bfloat16 [2048, 2048], P(('frame', 'space'), 'tensor'), may hold values from -0.125 to 0.125
Outputs:
- grad_inputs: bfloat16 [2, 16, 576, 2048], P(None, 'frame', 'space')
- grad_qkv: float32 [2048, 3, 2048], P(('frame', 'space'), None, 'tensor')
- grad_out_proj: float32 [2048, 2048], P(('frame', 'space'), 'tensor')
- grad_gain: float32 [2048], replicated
- grad_actions: float32 [8, 2048], replicated
The draws below stay inside these ranges and needn't reach their ends.
All inputs are finite; a program needn't handle non-finite values.
Results may differ from the reference program's by a relative error of at most 0.018.
The reference program's roundings to bfloat16 on the way (of `normed`, `merged_qkv`, `grad_heads`, `rounded`, `mixed_out` and `grad_merged`) count: a program that leaves them out, or rounds other values in their place, can miss the bound.
Values may be sent and summed in bfloat16 or wider, within the bound.
A program may use at most 128 MiB of HBM per device.

```python
import math
import jax
import jax.numpy as jnp
from jax import lax

D = 2048
HEADS = 16
HEAD = 128
ACTIONS = 8
BATCH = 2
FRAMES = 16
SPATIAL = 576


def draw_w_qkv(key, part):
    key = jax.random.fold_in(key, 7)
    base_key = jax.random.fold_in(key, 0)
    bound = 6.0 * D ** (-0.5)
    base = jax.random.normal(base_key, (D, 3, HEADS * HEAD), jnp.float32) * D ** (-0.5)
    base = jnp.clip(base, -bound, bound)
    base = jnp.clip(base, -1.0, 1.0)
    return base.astype(jnp.bfloat16)


def place_ends(entries, stream_key, low, top_value):
    longest = entries.shape.index(max(entries.shape))
    spots = []
    for shift in (0, 1):
        where = [jax.random.randint(jax.random.fold_in(stream_key, axis), (), 0, length) for axis, length in enumerate(entries.shape)]
        where[longest] = (where[longest] + shift) % entries.shape[longest]
        spots.append(tuple(where))
    return entries.at[spots[0]].set(low).at[spots[1]].set(top_value)


def spiked(drawn, own_key, source, target, parts, factor):
    owner, partner = [(jnp.arange(drawn.shape[axis_at]) // (drawn.shape[axis_at] // parts)).reshape([-1 if axis == axis_at else 1 for axis in range(drawn.ndim)]) for axis_at in (source, target)]
    chosen = jax.random.permutation(own_key, parts)[partner]
    strong = (owner == chosen) | (owner == (partner + parts // 2) % parts)
    return jnp.where(strong, factor * drawn, drawn)


def levels(own_key, extent, pieces, low, largest):
    def one(position, blocks):
        draws = jax.random.uniform(jax.random.fold_in(jax.random.fold_in(own_key, 6), position), (blocks,), jnp.float32, low / len(pieces), largest / len(pieces))
        return jnp.repeat(jnp.exp(draws), extent[position] // blocks).reshape((-1,) + (1,) * (len(extent) - position - 1))

    level = one(*pieces[0])
    for cut in pieces[1:]:
        level = level * one(*cut)
    return level


def centred(key, shape, spread, most, shards=(), kind=jnp.bfloat16):
    result = jax.random.normal(key, shape, jnp.float32) * spread
    if len(shards) > 0:
        result = levels(key, shape, shards, -0.22, 0.18) * result
    return jnp.clip(result, min=-most, max=most).astype(kind)


def gaussian_with(own_key, dims, spread, reach, cuts, heavy, kind=jnp.bfloat16):
    drawn = spread * jax.random.normal(own_key, dims, jnp.float32)
    if cuts:
        drawn = drawn * levels(own_key, dims, cuts, -0.22, 0.18)
    return jnp.clip(spiked(drawn, jax.random.fold_in(own_key, 3), *heavy), -reach, reach).astype(kind)


def setup_inputs(seed: int = 0) -> dict:
    arg_keys = jax.random.split(jax.random.key(seed), 9)
    inputs = gaussian_with(arg_keys[0], (BATCH, FRAMES, SPATIAL, D), 1.0, 6.0, ((1, 8), (2, 4)), (2, 3, 4, 2.0))
    upstream = gaussian_with(arg_keys[1], (BATCH, FRAMES, SPATIAL, D), 1.0, 6.0, ((1, 8), (2, 4)), (1, 3, 8, 2.0))
    action_ids = place_ends(jax.random.randint(arg_keys[2], (BATCH, FRAMES), 0, ACTIONS), jax.random.fold_in(arg_keys[2], 1), 0, ACTIONS - 1).astype(jnp.int32)
    frame_time = jax.vmap(lambda own: jax.random.permutation(own, FRAMES))(jax.random.split(arg_keys[3], BATCH)).reshape((BATCH, FRAMES)).astype(jnp.int32)
    action_table = centred(arg_keys[4], (ACTIONS, D), 0.5, 3.0, (), jnp.float32)
    gain = jnp.clip(1.0 + 0.1 * jax.random.normal(arg_keys[5], (D,), jnp.float32), 0.5, 1.5)
    w_qkv = draw_w_qkv(jax.random.fold_in(arg_keys[8], 71), 0)
    w_out = centred(arg_keys[7], (D, HEADS * HEAD), (HEADS * HEAD) ** -0.5, 0.125, ((0, 32), (1, 8)))
    return {"inputs": inputs, "upstream": upstream, "action_ids": action_ids, "frame_time": frame_time, "action_table": action_table, "gain": gain, "w_qkv": w_qkv, "w_out": w_out}


NORM_EPSILON = 1e-06

def normalize(inputs, action_ids, action_table, gain):
    action_count = action_table.shape[0]
    onehot = (action_ids[..., None] == jnp.arange(action_count, dtype=jnp.int32)).astype(jnp.float32)
    embedded = jnp.einsum('bfa,ad->bfd', onehot, action_table, precision=lax.Precision.HIGHEST)
    hidden = inputs.astype(jnp.float32) + embedded[:, :, None, :]
    inverse = lax.rsqrt(lax.optimization_barrier(jnp.mean(hidden * hidden, -1, keepdims=True)) + NORM_EPSILON)
    unit_rows = hidden * inverse
    normed = (unit_rows * gain).astype(jnp.bfloat16)
    return (onehot, inverse, unit_rows, normed)

def temporal_attention(merged_qkv, grad_heads, frame_time, head_size):
    batch_count, frame_count, space_count, channel_count = merged_qkv.shape
    head_width = channel_count // 3
    head_count = head_width // head_size
    split_parts = merged_qkv.reshape(batch_count, frame_count, space_count, 3, head_count, head_size).astype(jnp.float32)
    queries = split_parts[:, :, :, 0]
    key_rows = split_parts[:, :, :, 1]
    value_rows = split_parts[:, :, :, 2]
    score_scale = 1.0 / math.sqrt(head_size)
    scores = jnp.einsum('bqshd,bkshd->bshqk', queries, key_rows) * score_scale
    allowed = frame_time[:, None, None, None, :] <= frame_time[:, None, None, :, None]
    scores = jnp.where(allowed, scores, -1e+30)
    row_maxima = lax.optimization_barrier(jnp.max(scores, -1, keepdims=True))
    exponent = jnp.exp(scores - row_maxima)
    probabilities = exponent / lax.optimization_barrier(jnp.sum(exponent, -1, keepdims=True))
    rounded = lax.optimization_barrier(probabilities.astype(jnp.bfloat16)).astype(jnp.float32)
    mixed_out = jnp.einsum('bshqk,bkshd->bqshd', rounded, value_rows)
    mixed_out = mixed_out.reshape(batch_count, frame_count, space_count, head_width).astype(jnp.bfloat16)
    grad_rows = grad_heads.reshape(batch_count, frame_count, space_count, head_count, head_size).astype(jnp.float32)
    grad_probs = jnp.einsum('bqshd,bkshd->bshqk', grad_rows, value_rows)
    grad_values = jnp.einsum('bshqk,bqshd->bkshd', rounded, grad_rows)
    grad_scores = probabilities * (grad_probs - lax.optimization_barrier(jnp.sum(grad_probs * probabilities, -1, keepdims=True)))
    grad_queries = jnp.einsum('bshqk,bkshd->bqshd', grad_scores, key_rows) * score_scale
    grad_keys = jnp.einsum('bshqk,bqshd->bkshd', grad_scores, queries) * score_scale
    grad_merged = jnp.stack([grad_queries, grad_keys, grad_values], 3)
    grad_merged = grad_merged.reshape(batch_count, frame_count, space_count, channel_count).astype(jnp.bfloat16)
    return (mixed_out, grad_merged)

def norm_backward(grad_norm, unit_rows, inverse, upstream_rows, row_onehot, gain):
    scaled = grad_norm * gain
    grad_hidden = upstream_rows.astype(jnp.float32) + inverse * (scaled - unit_rows * lax.optimization_barrier(jnp.mean(scaled * unit_rows, -1, keepdims=True)))
    gain_term = lax.optimization_barrier(jnp.sum(grad_norm * unit_rows, 0))
    action_term = jnp.einsum('ra,rd->ad', row_onehot, grad_hidden, precision=lax.Precision.HIGHEST)
    return (grad_hidden, gain_term, action_term)

def reference(inputs, upstream, action_ids, frame_time, action_table, gain, w_qkv, w_out):
    batch_count, frame_count, space_count, feature_count = inputs.shape
    row_count = batch_count * frame_count * space_count
    channel_count = w_out.shape[1]
    onehot, inverse, unit_rows, normed = normalize(inputs, action_ids, action_table, gain)
    flat_norm = normed.reshape(row_count, feature_count)
    flat_up = upstream.reshape(row_count, feature_count)
    weight_flat = w_qkv.reshape(feature_count, 3 * channel_count)
    merged_qkv = jnp.dot(flat_norm, weight_flat, preferred_element_type=jnp.float32).astype(jnp.bfloat16)
    merged_qkv = merged_qkv.reshape(batch_count, frame_count, space_count, 3 * channel_count)
    grad_heads = jnp.dot(flat_up, w_out, preferred_element_type=jnp.float32).astype(jnp.bfloat16)
    grad_heads = grad_heads.reshape(batch_count, frame_count, space_count, channel_count)
    mixed_out, grad_merged = temporal_attention(merged_qkv, grad_heads, frame_time, HEAD)
    flat_mixed = mixed_out.reshape(row_count, channel_count)
    flat_grads = grad_merged.reshape(row_count, 3 * channel_count)
    grad_out_proj = jnp.dot(flat_up.T, flat_mixed, preferred_element_type=jnp.float32)
    grad_qkv = jnp.dot(flat_norm.T, flat_grads, preferred_element_type=jnp.float32).reshape(feature_count, 3, channel_count)
    grad_norm = jnp.dot(flat_grads, weight_flat.T, preferred_element_type=jnp.float32)
    row_onehot = jnp.broadcast_to(onehot[:, :, None, :], (batch_count, frame_count, space_count, onehot.shape[2])).reshape(row_count, onehot.shape[2])
    grad_hidden, grad_gain, grad_actions = norm_backward(grad_norm, unit_rows.reshape(row_count, feature_count), inverse.reshape(row_count, 1), flat_up, row_onehot, gain)
    grad_inputs = grad_hidden.astype(jnp.bfloat16).reshape(inputs.shape)
    return (grad_inputs, grad_qkv, grad_out_proj, grad_gain, grad_actions)
```

```python
import math

import jax
import jax.numpy as jnp
from jax import lax
from jax.experimental import pallas as pl
from jax.experimental.pallas import tpu as pltpu
from jax.sharding import PartitionSpec as P

HEAD = 128
NORM_EPSILON = 1e-06
MESH = pl.DeviceIdType.MESH
BF16 = jnp.bfloat16
F32 = jnp.float32

NZ, NX = 8, 4
SITES = 36
ROWS = 72
TOKENS = NZ * ROWS
SLICE = 256
VMEM_BYTES = 56 * 1024 * 1024


def position():
    f = lax.axis_index("frame")
    s = lax.axis_index("space")
    t = lax.axis_index("tensor")
    return f, s // 2, s % 2, t // NX, t % NX


def barrier(peers):
    sem = pltpu.get_barrier_semaphore()
    for peer in peers:
        pl.semaphore_signal(sem, inc=1, device_id=peer, device_id_type=MESH)
    pl.semaphore_wait(sem, len(peers))


class Copies:
    def __init__(self, send_sems, recv_sems):
        self.send_sems, self.recv_sems = send_sems, recv_sems
        self.started = []

    def send(self, slot, src, dst, device):
        copy = pltpu.make_async_remote_copy(
            src_ref=src,
            dst_ref=dst,
            send_sem=self.send_sems.at[slot],
            recv_sem=self.recv_sems.at[slot],
            device_id=device,
            device_id_type=MESH,
        )
        copy.start()
        self.started.append(copy)

    def arrived(self, slot, dst, device):
        pltpu.make_async_remote_copy(
            src_ref=dst,
            dst_ref=dst,
            send_sem=self.send_sems.at[slot],
            recv_sem=self.recv_sems.at[slot],
            device_id=device,
            device_id_type=MESH,
        ).wait_recv()

    def drain(self):
        for copy in self.started:
            copy.wait_send()


def mod(value, n):
    return lax.rem(value + 2 * n, n)


GATHER_SLOTS = 6 * NZ + 18


def gather_kernel(xu, w, tok, wts, send_sems, recv_sems, local_sems):
    f, yl, c, yh, x = position()
    right = {"tensor": yh * NX + mod(x + 1, NX)}
    left = {"tensor": yh * NX + mod(x - 1, NX)}
    other = {"tensor": (1 - yh) * NX + x}
    up, down = {"frame": mod(f + 1, NZ)}, {"frame": mod(f - 1, NZ)}
    ypeer = {"space": (1 - yl) * 2 + c}
    cpeer = {"space": yl * 2 + 1 - c}
    barrier([{"frame": mod(f + k, NZ)} for k in range(1, NZ)] + [right, left, other, ypeer, cpeer])

    cp = Copies(send_sems, recv_sems)
    xl, xr, xo = mod(x - 1, NX), mod(x + 1, NX), mod(x + 2, NX)
    W0 = 6 * NZ
    own_w = pltpu.make_async_copy(w, wts.at[f, yl, c], local_sems.at[1])
    own_w.start()
    cp.send(W0, w, wts.at[f, yl, c], ypeer)
    own = pltpu.make_async_copy(xu.at[f], tok.at[yh, x, f], local_sems.at[0])
    own.start()
    for k in range(1, NZ):
        j = mod(f + k, NZ)
        cp.send(6 * k, xu.at[j], tok.at[yh, x, f], {"frame": j})

    def stage_y(k):
        j = mod(f - k, NZ)
        if k == 0:
            own.wait()
        else:
            cp.arrived(6 * k, tok.at[yh, x, j], other)
        cp.send(6 * k + 1, tok.at[yh, x, j], tok.at[yh, x, j], other)

    def stage_x(k):
        j = mod(f - k, NZ)
        cp.arrived(6 * k + 1, tok.at[1 - yh, x, j], other)
        cp.send(6 * k + 2, tok.at[:, x, j], tok.at[:, x, j], right)
        cp.send(6 * k + 3, tok.at[:, x, j], tok.at[:, x, j], left)

    def stage_forward(k):
        j = mod(f - k, NZ)
        cp.arrived(6 * k + 2, tok.at[:, xl, j], left)
        cp.send(6 * k + 4, tok.at[:, xl, j, 0], tok.at[:, xl, j, 0], right)
        cp.arrived(6 * k + 3, tok.at[:, xr, j], right)
        cp.send(6 * k + 5, tok.at[:, xr, j, 1], tok.at[:, xr, j, 1], left)

    def ring(step):
        if step == 0:
            own_w.wait()
            cp.arrived(W0, wts.at[f, 1 - yl, c], ypeer)
            cp.send(W0 + 1, wts.at[f, :, c], wts.at[f, :, c], up)
            cp.send(W0 + 2, wts.at[f, :, c], wts.at[f, :, c], down)
            cp.send(W0 + 9, wts.at[f, :, c], wts.at[f, :, c], cpeer)
            return
        lo, hi = mod(f - step, NZ), mod(f + step, NZ)
        if step < 4:
            cp.arrived(W0 + 2 * step - 1, wts.at[lo, :, c], down)
            cp.arrived(W0 + 2 * step, wts.at[hi, :, c], up)
            if step < 3:
                cp.send(W0 + 2 * step + 1, wts.at[lo, :, c], wts.at[lo, :, c], up)
                cp.send(W0 + 2 * step + 2, wts.at[hi, :, c], wts.at[hi, :, c], down)
            else:
                cp.send(W0 + 7, wts.at[lo, 0, c], wts.at[lo, 0, c], up)
                cp.send(W0 + 8, wts.at[hi, 1, c], wts.at[hi, 1, c], down)
            cp.send(W0 + 9 + step, wts.at[lo, :, c], wts.at[lo, :, c], cpeer)
            cp.send(W0 + 12 + step, wts.at[hi, :, c], wts.at[hi, :, c], cpeer)
        else:
            cp.arrived(W0 + 7, wts.at[lo, 0, c], down)
            cp.arrived(W0 + 8, wts.at[lo, 1, c], up)
            cp.send(W0 + 16, wts.at[lo, :, c], wts.at[lo, :, c], cpeer)

    for k in range(NZ + 2):
        if k < NZ:
            stage_y(k)
        if 1 <= k <= NZ:
            stage_x(k - 1)
        if k >= 2:
            stage_forward(k - 2)
        if k in (0, 2, 4, 6, 8):
            ring(k // 2)
    for k in range(NZ):
        j = mod(f - k, NZ)
        cp.arrived(6 * k + 4, tok.at[:, xo, j, 0], left)
        cp.arrived(6 * k + 5, tok.at[:, xo, j, 1], right)
    for step in range(5):
        lo, hi = mod(f - step, NZ), mod(f + step, NZ)
        if step == 0:
            cp.arrived(W0 + 9, wts.at[f, :, 1 - c], cpeer)
        elif step < 4:
            cp.arrived(W0 + 9 + step, wts.at[lo, :, 1 - c], cpeer)
            cp.arrived(W0 + 12 + step, wts.at[hi, :, 1 - c], cpeer)
        else:
            cp.arrived(W0 + 16, wts.at[lo, :, 1 - c], cpeer)
    cp.drain()


def gather(xu, w):
    any_spec = pl.BlockSpec(memory_space=pl.ANY)
    return pl.pallas_call(
        gather_kernel,
        out_shape=(
            jax.ShapeDtypeStruct((2, NX, NZ, 2, ROWS, SLICE), BF16),
            jax.ShapeDtypeStruct((NZ, 2, 2, 64, 1024), BF16),
        ),
        in_specs=[any_spec, any_spec],
        out_specs=(any_spec, any_spec),
        scratch_shapes=[
            pltpu.SemaphoreType.DMA((GATHER_SLOTS,)),
            pltpu.SemaphoreType.DMA((GATHER_SLOTS,)),
            pltpu.SemaphoreType.DMA((2,)),
        ],
        compiler_params=pltpu.CompilerParams(
            collective_id=0, has_side_effects=True, vmem_limit_bytes=VMEM_BYTES
        ),
    )(xu, w)


def nt(a, b):
    return lax.dot_general(a, b, (((1,), (1,)), ((), ())), preferred_element_type=F32)


def tn(a, b):
    return lax.dot_general(a, b, (((0,), (0,)), ((), ())), preferred_element_type=F32)


def local_kernel(tok, wts, bias, gn, gw, normed, up, qkv, mixed, grads, probs, dscore):
    scale = 1.0 / math.sqrt(HEAD)
    for t in range(8):
        cols = slice(t * SLICE, (t + 1) * SLICE)
        for arr, out in ((0, normed), (1, up)):
            out[:, cols] = jnp.concatenate(
                [tok[t // NX, t % NX, j, arr].astype(F32) for j in range(NZ)], 0
            ).astype(BF16)

    @pl.loop(0, 4)
    def _(n):
        at = pl.ds(pl.multiple_of(n * 256, 256), 256)

        @pl.when(n < 3)
        def _():
            qkv[:, at] = jnp.dot(
                normed[...], wts[:, at], preferred_element_type=F32
            ).astype(BF16)

        @pl.when(n == 3)
        def _():
            qkv[:, at] = jnp.dot(up[...], wts[:, at], preferred_element_type=F32).astype(BF16)

    half = TOKENS // 2
    for h in range(2):
        q, k, v, g = (qkv[:, n * 256 + h * HEAD : n * 256 + (h + 1) * HEAD] for n in range(4))
        for part in range(2):
            rows = slice(part * half, (part + 1) * half)
            scores = nt(q[rows], k) * scale + bias[rows]
            exponent = jnp.exp(scores - jnp.max(scores, -1, keepdims=True))
            p = exponent / jnp.sum(exponent, -1, keepdims=True)
            probs[rows] = p.astype(BF16)
            gp = nt(g[rows], v)
            ds = p * (gp - jnp.sum(gp * p, -1, keepdims=True))
            dscore[rows] = ds.astype(BF16)
        lanes = slice(h * HEAD, (h + 1) * HEAD)
        pb, db = probs[...], dscore[...]
        mixed[:, lanes] = jnp.dot(pb, v, preferred_element_type=F32).astype(BF16)
        grads[:, h * HEAD : (h + 1) * HEAD] = (
            jnp.dot(db, k, preferred_element_type=F32) * scale
        ).astype(BF16)
        grads[:, 256 + h * HEAD : 256 + (h + 1) * HEAD] = (tn(db, q) * scale).astype(BF16)
        grads[:, 512 + h * HEAD : 512 + (h + 1) * HEAD] = tn(pb, g).astype(BF16)

    @pl.loop(0, 8)
    def _(t):
        at = pl.ds(pl.multiple_of(t * SLICE, SLICE), SLICE)
        back = nt(grads[...], wts[at, 0:768])
        for j in range(NZ):
            gn[t // NX, t % NX, j] = back[j * ROWS : (j + 1) * ROWS].astype(BF16)
        term = tn(normed[:, at], grads[...]).astype(BF16)
        term_out = tn(up[:, at], mixed[...]).astype(BF16)
        for r in range(4):
            gw[t, r // 2, r % 2, :, 0:768] = term[64 * r : 64 * r + 64]
            gw[t, r // 2, r % 2, :, 768:1024] = term_out[64 * r : 64 * r + 64]


def local(tok, wts, bias):
    spec = pl.BlockSpec(memory_space=pltpu.VMEM)
    return pl.pallas_call(
        local_kernel,
        out_shape=(
            jax.ShapeDtypeStruct((2, NX, NZ, ROWS, SLICE), BF16),
            jax.ShapeDtypeStruct((NZ, 2, 2, 64, 1024), BF16),
        ),
        in_specs=[spec] * 3,
        out_specs=(spec, spec),
        scratch_shapes=[
            pltpu.VMEM((TOKENS, 2048), BF16),
            pltpu.VMEM((TOKENS, 2048), BF16),
            pltpu.VMEM((TOKENS, 1024), BF16),
            pltpu.VMEM((TOKENS, 256), BF16),
            pltpu.VMEM((TOKENS, 768), BF16),
            pltpu.VMEM((TOKENS, TOKENS), BF16),
            pltpu.VMEM((TOKENS, TOKENS), BF16),
        ],
        compiler_params=pltpu.CompilerParams(vmem_limit_bytes=VMEM_BYTES),
    )(tok, wts.reshape(2048, 1024), bias)


BACK_SLOTS = 10 * NZ + 12


def back_kernel(
    gn, gw, full, wsum, part_l, part_r, sum_l, sum_r, in_l, in_r, ysend, yin, zsend,
    cin, rs_up, rs_down, ri_up, ri_down, psend, pin, send_sems, recv_sems, local_sems,
):
    f, yl, c, yh, x = position()
    right = {"tensor": yh * NX + mod(x + 1, NX)}
    left = {"tensor": yh * NX + mod(x - 1, NX)}
    other = {"tensor": (1 - yh) * NX + x}
    up, down = {"frame": mod(f + 1, NZ)}, {"frame": mod(f - 1, NZ)}
    ypeer = {"space": (1 - yl) * 2 + c}
    cpeer = {"space": yl * 2 + 1 - c}
    barrier([{"frame": mod(f + k, NZ)} for k in range(1, NZ)] + [right, left, other, ypeer, cpeer])

    cp = Copies(send_sems, recv_sems)
    xl, xr, xo = mod(x - 1, NX), mod(x + 1, NX), mod(x + 2, NX)
    lo_lanes, hi_lanes = pl.ds(0, 128), pl.ds(128, 128)
    W0 = 10 * NZ

    for k in range(NZ):
        j = mod(f + k, NZ)
        cp.send(10 * k, gn.at[:, xo, j, :, lo_lanes], part_l.at[k], right)
        cp.send(10 * k + 1, gn.at[:, xo, j, :, hi_lanes], part_r.at[k], left)
        if k == 0:
            cp.send(W0, gw.at[:, :, 1 - c], cin, cpeer)

    def stage_sum(k):
        j = mod(f + k, NZ)
        cp.arrived(10 * k, part_l.at[k], left)
        sum_r[k, :, :, 0:128] = (
            gn[:, xr, j, :, 0:128].astype(F32) + part_l[k].astype(F32)
        ).astype(BF16)
        sum_r[k, :, :, 128:256] = gn[:, xr, j, :, 128:256]
        cp.send(10 * k + 2, sum_r.at[k], in_l.at[k], right)
        cp.arrived(10 * k + 1, part_r.at[k], right)
        sum_l[k, :, :, 0:128] = gn[:, xl, j, :, 0:128]
        sum_l[k, :, :, 128:256] = (
            gn[:, xl, j, :, 128:256].astype(F32) + part_r[k].astype(F32)
        ).astype(BF16)
        cp.send(10 * k + 3, sum_l.at[k], in_r.at[k], left)

    def stage_y(k):
        j = mod(f + k, NZ)
        cp.arrived(10 * k + 2, in_l.at[k], left)
        cp.arrived(10 * k + 3, in_r.at[k], right)
        theirs = (
            gn[1 - yh, x, j].astype(F32)
            + in_l[k, 1 - yh].astype(F32)
            + in_r[k, 1 - yh].astype(F32)
        )
        ysend[k] = theirs.astype(BF16)
        cp.send(10 * k + 4, ysend.at[k], yin.at[k], other)

    def stage_z(k):
        j = mod(f + k, NZ)
        cp.arrived(10 * k + 4, yin.at[k], other)
        mine = (
            gn[yh, x, j].astype(F32)
            + in_l[k, yh].astype(F32)
            + in_r[k, yh].astype(F32)
            + yin[k].astype(F32)
        )
        zsend[k] = mine.astype(BF16)
        if k == 0:
            pltpu.make_async_copy(zsend.at[0], full.at[yh, x, f], local_sems.at[0]).start()
        else:
            cp.send(10 * k + 5, zsend.at[k], full.at[yh, x, f], {"frame": j})

    def gather_y(k):
        j = mod(f - k, NZ)
        if k == 0:
            pltpu.make_async_copy(zsend.at[0], full.at[yh, x, f], local_sems.at[0]).wait()
        else:
            cp.arrived(10 * k + 5, full.at[yh, x, j], other)
        cp.send(10 * k + 6, full.at[yh, x, j], full.at[yh, x, j], other)

    def gather_x(k):
        j = mod(f - k, NZ)
        cp.arrived(10 * k + 6, full.at[1 - yh, x, j], other)
        cp.send(10 * k + 7, full.at[:, x, j], full.at[:, x, j], right)
        cp.send(10 * k + 8, full.at[:, x, j], full.at[:, x, j], left)

    def gather_forward(k):
        j = mod(f - k, NZ)
        cp.arrived(10 * k + 7, full.at[:, xl, j], left)
        here = full.at[:, xl, j, :, lo_lanes]
        cp.send(10 * k + 9, here, here, right)
        cp.arrived(10 * k + 8, full.at[:, xr, j], right)
        here = full.at[:, xr, j, :, hi_lanes]
        cp.send(W0 + 12 + k, here, here, left)

    def block(j, row):
        return gw[j, row, c].astype(F32) + cin[j, row].astype(F32)

    def ring(step):
        if step == 0:
            cp.arrived(W0, cin, cpeer)
            far = mod(f + 4, NZ)
            rs_up[0, 0] = block(far, 0).astype(BF16)
            cp.send(W0 + 1, rs_up.at[0, 0], ri_up.at[0, 0], up)
            rs_down[0, 0] = block(far, 1).astype(BF16)
            cp.send(W0 + 2, rs_down.at[0, 0], ri_down.at[0, 0], down)
            return
        if step < 4:
            ahead, behind = mod(f + 4 - step, NZ), mod(f - 4 + step, NZ)
            if step == 1:
                cp.arrived(W0 + 1, ri_up.at[0, 0], down)
                rs_up[1, 0] = (block(ahead, 0) + ri_up[0, 0].astype(F32)).astype(BF16)
                rs_up[1, 1] = block(ahead, 1).astype(BF16)
                cp.send(W0 + 3, rs_up.at[1], ri_up.at[1], up)
                cp.arrived(W0 + 2, ri_down.at[0, 0], up)
                rs_down[1, 0] = block(behind, 0).astype(BF16)
                rs_down[1, 1] = (block(behind, 1) + ri_down[0, 0].astype(F32)).astype(BF16)
                cp.send(W0 + 4, rs_down.at[1], ri_down.at[1], down)
            else:
                cp.arrived(W0 + 2 * step - 1, ri_up.at[step - 1], down)
                for r in range(2):
                    rs_up[step, r] = (
                        block(ahead, r) + ri_up[step - 1, r].astype(F32)
                    ).astype(BF16)
                cp.send(W0 + 2 * step + 1, rs_up.at[step], ri_up.at[step], up)
                cp.arrived(W0 + 2 * step, ri_down.at[step - 1], up)
                for r in range(2):
                    rs_down[step, r] = (
                        block(behind, r) + ri_down[step - 1, r].astype(F32)
                    ).astype(BF16)
                cp.send(W0 + 2 * step + 2, rs_down.at[step], ri_down.at[step], down)
            return
        if step == 4:
            cp.arrived(W0 + 7, ri_up.at[3], down)
            cp.arrived(W0 + 8, ri_down.at[3], up)
            theirs = (
                block(f, 1 - yl)
                + ri_up[3, 1 - yl].astype(F32)
                + ri_down[3, 1 - yl].astype(F32)
            )
            psend[...] = theirs.astype(BF16)
            cp.send(W0 + 9, psend, pin, ypeer)
            return
        cp.arrived(W0 + 9, pin, ypeer)
        wsum[...] = (
            block(f, yl)
            + ri_up[3, yl].astype(F32)
            + ri_down[3, yl].astype(F32)
            + pin[...].astype(F32)
        )

    stages = [stage_sum, stage_y, stage_z, gather_y, gather_x, gather_forward]
    for k in range(NZ + len(stages) - 1):
        for lag, stage in enumerate(stages):
            if 0 <= k - lag < NZ:
                stage(k - lag)
        if k % 2 == 1 and k // 2 < 6:
            ring(k // 2)
    for k in range(NZ):
        j = mod(f - k, NZ)
        cp.arrived(10 * k + 9, full.at[:, xo, j, :, lo_lanes], left)
        cp.arrived(W0 + 12 + k, full.at[:, xo, j, :, hi_lanes], right)
    cp.drain()


def back(gn, gw):
    spec = pl.BlockSpec(memory_space=pltpu.VMEM)
    any_spec = pl.BlockSpec(memory_space=pl.ANY)
    slots = BACK_SLOTS + NZ
    block = (2, ROWS, SLICE)
    return pl.pallas_call(
        back_kernel,
        out_shape=(
            jax.ShapeDtypeStruct((2, NX, NZ, ROWS, SLICE), BF16),
            jax.ShapeDtypeStruct((64, 1024), F32),
        ),
        in_specs=[spec, spec],
        out_specs=(any_spec, spec),
        scratch_shapes=[
            pltpu.VMEM((NZ, 2, ROWS, 128), BF16),
            pltpu.VMEM((NZ, 2, ROWS, 128), BF16),
            pltpu.VMEM((NZ,) + block, BF16),
            pltpu.VMEM((NZ,) + block, BF16),
            pltpu.VMEM((NZ,) + block, BF16),
            pltpu.VMEM((NZ,) + block, BF16),
            pltpu.VMEM((NZ, ROWS, SLICE), BF16),
            pltpu.VMEM((NZ, ROWS, SLICE), BF16),
            pltpu.VMEM((NZ, ROWS, SLICE), BF16),
            pltpu.VMEM((NZ, 2, 64, 1024), BF16),
            pltpu.VMEM((4, 2, 64, 1024), BF16),
            pltpu.VMEM((4, 2, 64, 1024), BF16),
            pltpu.VMEM((4, 2, 64, 1024), BF16),
            pltpu.VMEM((4, 2, 64, 1024), BF16),
            pltpu.VMEM((64, 1024), BF16),
            pltpu.VMEM((64, 1024), BF16),
            pltpu.SemaphoreType.DMA((slots,)),
            pltpu.SemaphoreType.DMA((slots,)),
            pltpu.SemaphoreType.DMA((1,)),
        ],
        compiler_params=pltpu.CompilerParams(
            collective_id=1, has_side_effects=True, vmem_limit_bytes=VMEM_BYTES
        ),
    )(gn, gw)


def small_kernel(term, out, zin, sent, sin, total, send_sems, recv_sems):
    f, yl, c, yh, x = position()
    s, t = yl * 2 + c, yh * NX + x
    frames = [{"frame": mod(f + k, NZ)} for k in range(1, NZ)]
    spaces = [{"space": mod(s + k, 4)} for k in range(1, 4)]
    tensors = [{"tensor": mod(t + k, 8)} for k in range(1, 8)]
    barrier(frames + spaces + tensors)
    cp = Copies(send_sems, recv_sems)
    zin[f] = term[t]
    for k in range(1, NZ):
        cp.send(k - 1, term.at[t], zin.at[f], frames[k - 1])
    for k in range(1, NZ):
        cp.arrived(k - 1, zin.at[mod(f - k, NZ)], frames[k - 1])
    acc = zin[0]
    for k in range(1, NZ):
        acc = acc + zin[k]
    sent[...] = acc
    sin[s] = acc
    for k in range(1, 4):
        cp.send(6 + k, sent, sin.at[s], spaces[k - 1])
    for k in range(1, 4):
        cp.arrived(6 + k, sin.at[mod(s - k, 4)], spaces[k - 1])
    acc = sin[0]
    for k in range(1, 4):
        acc = acc + sin[k]
    total[...] = acc
    out[t] = acc
    for k in range(1, 8):
        cp.send(9 + k, total, out.at[t], tensors[k - 1])
    for k in range(1, 8):
        cp.arrived(9 + k, out.at[mod(t - k, 8)], tensors[k - 1])
    cp.drain()


def small_sum(term):
    spec = pl.BlockSpec(memory_space=pltpu.VMEM)
    return pl.pallas_call(
        small_kernel,
        out_shape=jax.ShapeDtypeStruct((8, 16, SLICE), F32),
        in_specs=[spec],
        out_specs=spec,
        scratch_shapes=[
            pltpu.VMEM((NZ, 16, SLICE), F32),
            pltpu.VMEM((16, SLICE), F32),
            pltpu.VMEM((4, 16, SLICE), F32),
            pltpu.VMEM((16, SLICE), F32),
            pltpu.SemaphoreType.DMA((17,)),
            pltpu.SemaphoreType.DMA((17,)),
        ],
        compiler_params=pltpu.CompilerParams(collective_id=2, has_side_effects=True),
    )(term)


def score_bias(frame_time):
    rollout = lax.axis_index("frame") // 4
    times = lax.dynamic_index_in_dim(frame_time, rollout, 0, keepdims=False)
    times = jnp.broadcast_to(times[:, None], (2 * NZ, SITES)).reshape(TOKENS)
    sites = jnp.broadcast_to(jnp.arange(SITES)[None, :], (2 * NZ, SITES)).reshape(TOKENS)
    allowed = (sites[:, None] == sites[None, :]) & (times[None, :] <= times[:, None])
    return jnp.where(allowed, 0.0, -1e30).astype(F32)


def by_site(rows):
    n = rows.shape[-1]
    return rows.reshape(2, 2, 4, SITES, n).transpose(0, 2, 1, 3, 4).reshape(NZ, ROWS, n)


def on_device(inputs, upstream, action_ids, frame_time, action_table, gain, w_qkv, w_out):
    t = lax.axis_index("tensor")
    actions = action_table.shape[0]
    onehot = (action_ids[..., None] == jnp.arange(actions, dtype=jnp.int32)).astype(F32)
    embedded = jnp.einsum("bfa,ad->bfd", onehot, action_table, precision=lax.Precision.HIGHEST)
    hidden = inputs.astype(F32) + embedded[:, :, None, :]
    inverse = lax.rsqrt(jnp.mean(hidden * hidden, -1, keepdims=True) + NORM_EPSILON)

    def mine(a):
        return lax.dynamic_slice_in_dim(a, t * SLICE, SLICE, axis=a.ndim - 1)

    normed = (mine(inputs).astype(F32) + mine(embedded)[:, :, None, :]) * inverse * mine(gain)
    xu = jnp.stack([by_site(normed.astype(BF16)), by_site(mine(upstream))], 1)
    w = jnp.concatenate([w_qkv.reshape(64, 768), w_out], 1)

    tok, wts = gather(xu, w)
    gn, gw = local(tok, wts, score_bias(frame_time))
    full, wsum = back(gn, gw)

    grad_norm = full.reshape(8, 2, 4, 2, SITES, SLICE).transpose(1, 3, 2, 4, 0, 5)
    grad_norm = grad_norm.reshape(inputs.shape).astype(F32)
    unit_rows = hidden * inverse
    scaled = grad_norm * gain
    grad_hidden = upstream.astype(F32) + inverse * (
        scaled - unit_rows * jnp.mean(scaled * unit_rows, -1, keepdims=True)
    )
    gain_term = jnp.sum(grad_norm * unit_rows, (0, 1, 2))
    frame_sums = jnp.sum(grad_hidden, 2)
    action_term = jnp.einsum("bfa,bfd->ad", onehot, frame_sums, precision=lax.Precision.HIGHEST)
    term = jnp.concatenate([jnp.broadcast_to(gain_term[None], (8, 2048)), action_term], 0)
    sums = small_sum(term.reshape(16, 8, SLICE).transpose(1, 0, 2))
    sums = sums.transpose(1, 0, 2).reshape(16, 2048)
    return (
        grad_hidden.astype(BF16),
        wsum[:, :768].reshape(64, 3, 256),
        wsum[:, 768:],
        sums[0],
        sums[8:],
    )


def solution(mesh):
    return jax.shard_map(
        on_device,
        mesh=mesh,
        in_specs=(
            P(None, "frame", "space", None),
            P(None, "frame", "space", None),
            P(None, "frame"),
            P(),
            P(),
            P(),
            P(("frame", "space"), None, "tensor"),
            P(("frame", "space"), "tensor"),
        ),
        out_specs=(
            P(None, "frame", "space", None),
            P(("frame", "space"), None, "tensor"),
            P(("frame", "space"), "tensor"),
            P(),
            P(),
        ),
        check_vma=False,
    )
```

```python
import math

import jax
import jax.numpy as jnp
from jax import lax
from jax.experimental import pallas as pl
from jax.experimental.pallas import tpu as pltpu
from jax.sharding import PartitionSpec as P

HEAD = 128
NORM_EPSILON = 1e-06
MESH = pl.DeviceIdType.MESH
BF16 = jnp.bfloat16
F32 = jnp.float32

NZ, NX, NT = 8, 4, 8
SITES = 36
ROWS = 72
TOKENS = NZ * ROWS
SLICE = 256
WIDTH = 2048
VMEM_BYTES = 58 * 1024 * 1024
ORDER = (0, 1, 7, 2, 6, 3, 5, 4)
SLOTS = 320


def mod(value, n):
    return lax.rem(value + 2 * n, n)


def nt(a, b):
    return lax.dot_general(a, b, (((1,), (1,)), ((), ())), preferred_element_type=F32)


def tn(a, b):
    return lax.dot_general(a, b, (((0,), (0,)), ((), ())), preferred_element_type=F32)


def nn(a, b):
    return jnp.dot(a, b, preferred_element_type=F32)


class Copies:
    def __init__(self, send_sems, recv_sems):
        self.send_sems, self.recv_sems = send_sems, recv_sems
        self.slots, self.started = {}, []

    def slot(self, name):
        return self.slots.setdefault(name, len(self.slots))

    def send(self, name, src, dst, device):
        slot = self.slot(name)
        copy = pltpu.make_async_remote_copy(
            src_ref=src,
            dst_ref=dst,
            send_sem=self.send_sems.at[slot],
            recv_sem=self.recv_sems.at[slot],
            device_id=device,
            device_id_type=MESH,
        )
        copy.start()
        self.started.append(copy)

    def arrived(self, name, dst, device):
        slot = self.slot(name)
        pltpu.make_async_remote_copy(
            src_ref=dst,
            dst_ref=dst,
            send_sem=self.send_sems.at[slot],
            recv_sem=self.recv_sems.at[slot],
            device_id=device,
            device_id_type=MESH,
        ).wait_recv()

    def drain(self):
        for copy in self.started:
            copy.wait_send()


def kernel(
    inputs, upstream, w3, wo, embedded, ids, gain, code_col, code_row,
    out, wq_sum, wo_sum, small_out,
    in_v, up_v, xu, meta, meta_in, tok, wts, normed, up, bias, qkv, mixed, grads, probs, dscore,
    m_part, m_in, m_sum, gn, gw, part_l, part_r, sum_l, sum_r, in_l, in_r, ysend, yin, zsend,
    cin, rs_up, rs_down, ri_up, ri_down, psend, pin, full,
    act, gterm, small, zin, sent, sin, total,
    send_sems, recv_sems, local_sems,
):
    f = lax.axis_index("frame")
    s = lax.axis_index("space")
    t = lax.axis_index("tensor")
    yl, c, yh, x = s // 2, s % 2, t // NX, t % NX
    xl, xr, xo = mod(x - 1, NX), mod(x + 1, NX), mod(x + 2, NX)
    right, left = {"tensor": yh * NX + xr}, {"tensor": yh * NX + xl}
    other = {"tensor": (1 - yh) * NX + x}
    z_up, z_down = {"frame": mod(f + 1, NZ)}, {"frame": mod(f - 1, NZ)}
    ypeer = {"space": (1 - yl) * 2 + c}
    cpeer = {"space": yl * 2 + 1 - c}
    frames = [{"frame": mod(f + k, NZ)} for k in range(1, NZ)]
    spaces = [{"space": mod(s + k, 4)} for k in range(1, 4)]
    tensors = [{"tensor": mod(t + k, NT)} for k in range(1, NT)]
    peers = frames + spaces + tensors
    my_cols = pl.ds(pl.multiple_of(t * SLICE, SLICE), SLICE)

    greeted = pltpu.get_barrier_semaphore()
    for peer in peers:
        pl.semaphore_signal(greeted, inc=1, device_id=peer, device_id_type=MESH)

    cp = Copies(send_sems, recv_sems)

    def w_rows(z, row, plane):
        return wts.at[pl.ds(pl.multiple_of((z * 4 + row * 2 + plane) * 64, 64), 64), :]

    def local(src, dst, n):
        copy = pltpu.make_async_copy(src, dst, local_sems.at[n])
        copy.start()
        return copy

    load_in = local(inputs, in_v, 0)
    load_up = local(upstream.at[:, :, my_cols], up_v, 1)
    own_rows = pl.ds(pl.multiple_of((f * 4 + s) * 64, 64), 64)
    load_w = [
        local(w3.at[n], wts.at[own_rows, n * 256 : (n + 1) * 256], 2 + n) for n in range(3)
    ] + [local(wo, wts.at[own_rows, 768:1024], 5)]
    load_in.wait()

    lane = lax.broadcasted_iota(jnp.int32, (ROWS, 128), 1)
    eye = (lane == lax.broadcasted_iota(jnp.int32, (ROWS, 128), 0)).astype(F32)

    def to_row(column):
        return jnp.sum(eye * column, 0, keepdims=True)

    def to_column(row):
        return jnp.sum(eye * row, 1, keepdims=True)

    gain_t = gain[0:1, my_cols]
    gain_inv = 1.0 / gain_t
    pieces, inverses = [], []
    for i in range(4):
        squares = jnp.zeros((144, SLICE), F32)
        for n in range(NT):
            cols = slice(n * SLICE, (n + 1) * SLICE)
            hidden = in_v[i, :, cols].astype(F32) + embedded[i : i + 1, cols]
            squares = squares + hidden * hidden
        inverse = lax.rsqrt(jnp.sum(squares, -1, keepdims=True) * (1.0 / WIDTH) + NORM_EPSILON)
        hidden = in_v[i, :, my_cols].astype(F32) + embedded[i : i + 1, my_cols]
        pieces.append(hidden * inverse * gain_t)
        inverses.append(jnp.broadcast_to(inverse, (144, 128)))
    load_up.wait()
    for b in range(2):
        for r in range(4):
            rows = slice(r * SITES, (r + 1) * SITES)

            def chunk(a):
                return jnp.concatenate([a[2 * b][rows], a[2 * b + 1][rows]], 0)

            xu[b * 4 + r, 0] = chunk(pieces).astype(BF16)
            xu[b * 4 + r, 1] = jnp.concatenate(
                [up_v[2 * b].astype(F32)[rows], up_v[2 * b + 1].astype(F32)[rows]], 0
            ).astype(BF16)
            meta[b * 4 + r] = jnp.concatenate(
                [to_row(chunk(inverses)), ids[2 * b : 2 * b + 2], jnp.zeros((5, 128), F32)], 0
            )

    pl.semaphore_wait(greeted, len(peers))

    for p in range(1, NZ):
        j = mod(f + ORDER[p], NZ)
        cp.send(("z", p), xu.at[j], tok.at[yh, x, f], {"frame": j})
        cp.send(("meta", p), meta.at[j], meta_in.at[f], {"frame": j})
    local(xu.at[f], tok.at[yh, x, f], 0).wait()
    meta_in[f] = meta[f]

    def source(p):
        return mod(f - ORDER[p], NZ)

    def tokens_y(p):
        j = source(p)
        if p > 0:
            cp.arrived(("z", p), tok.at[yh, x, j], other)
            cp.arrived(("meta", p), meta_in.at[j], other)
        mine = tok.at[yh, x, j]
        cp.send(("ty", p), mine, mine, other)
        cp.send(("tr", p), mine, mine, right)
        cp.send(("tl", p), mine, mine, left)

    def tokens_x(p):
        j = source(p)
        theirs = tok.at[1 - yh, x, j]
        cp.arrived(("ty", p), theirs, other)
        cp.send(("tor", p), theirs, theirs, right)
        cp.send(("tol", p), theirs, theirs, left)

    def tokens_forward(p):
        j = source(p)
        block = tok.at[yh, xl, j]
        cp.arrived(("tr", p), block, left)
        cp.send(("tfr", p), block, block, right)
        cp.arrived(("tl", p), tok.at[yh, xr, j], right)
        block = tok.at[1 - yh, xr, j]
        cp.arrived(("tol", p), block, right)
        cp.send(("tfl", p), block, block, left)
        cp.arrived(("tor", p), tok.at[1 - yh, xl, j], left)

    def tokens_last(p):
        j = source(p)
        cp.arrived(("tfr", p), tok.at[yh, xo, j], left)
        cp.arrived(("tfl", p), tok.at[1 - yh, xo, j], right)

    def weights(step, o):
        row = yl if o == 0 else 1 - yl
        if step == 0:
            block = w_rows(f, row, c)
            if o == 0:
                for copy in load_w:
                    copy.wait()
                cp.send("wy", block, block, ypeer)
            else:
                cp.arrived("wy", block, ypeer)
            cp.send(("wu", 0, o), block, block, z_up)
            cp.send(("wd", 0, o), block, block, z_down)
            cp.send(("wc", 0, o), block, block, cpeer)
        elif step < 4:
            block = w_rows(mod(f - step, NZ), row, c)
            cp.arrived(("wu", step - 1, o), block, z_down)
            if step < 3 or o == 0:
                cp.send(("wu", step, o), block, block, z_up)
            cp.send(("wc", step, o), block, block, cpeer)
            block = w_rows(mod(f + step, NZ), row, c)
            cp.arrived(("wd", step - 1, o), block, z_up)
            if step < 3 or o == 1:
                cp.send(("wd", step, o), block, block, z_down)
            cp.send(("wc", -step, o), block, block, cpeer)
        else:
            block = w_rows(mod(f + 4, NZ), row, c)
            if o == 0:
                cp.arrived(("wu", 3, o), block, z_down)
            else:
                cp.arrived(("wd", 3, o), block, z_up)
            cp.send(("wc", 4, o), block, block, cpeer)

    def weights_last():
        for step in range(-3, 5):
            for o in range(2):
                row = yl if o == 0 else 1 - yl
                cp.arrived(("wc", step, o), w_rows(mod(f - step, NZ), row, 1 - c), cpeer)

    plan = {
        0: [(0, 0)], 1: [(0, 1)], 2: [(1, 0), (1, 1)], 4: [(2, 0), (2, 1)],
        6: [(3, 0), (3, 1)], 8: [(4, 0), (4, 1)],
    }
    for p in range(NZ + 2):
        if p < NZ:
            tokens_y(p)
        if 1 <= p <= NZ:
            tokens_x(p - 1)
        if p >= 2:
            tokens_forward(p - 2)
        for step, o in plan.get(p, ()):
            weights(step, o)
        if p == 0:
            apart = code_col[:, 0:1] - code_row[0:1, :]
            bias[...] = jnp.where((apart >= 0.0) & (apart <= 15.0), 0.0, -1e30)
    for p in range(NZ):
        tokens_last(p)
    weights_last()

    for n in range(NT):
        cols = slice(n * SLICE, (n + 1) * SLICE)
        for arr, dst in ((0, normed), (1, up)):
            dst[:, cols] = jnp.concatenate(
                [tok[n // NX, n % NX, source(p), arr].astype(F32) for p in range(NZ)], 0
            ).astype(BF16)

    @pl.loop(0, 3)
    def _(n):
        at = pl.ds(pl.multiple_of(n * 256, 256), 256)
        qkv[:, at] = nn(normed[...], wts[:, at]).astype(BF16)

    qkv[:, 768:1024] = nn(up[...], wts[:, 768:1024]).astype(BF16)

    scale = 1.0 / math.sqrt(HEAD)
    half = TOKENS // 2
    for h in range(2):
        q, k, v, g = (qkv[:, n * 256 + h * HEAD : n * 256 + (h + 1) * HEAD] for n in range(4))
        for part in range(2):
            rows = slice(part * half, (part + 1) * half)
            scores = nt(q[rows], k) * scale + bias[rows]
            exponent = jnp.exp(scores - jnp.max(scores, -1, keepdims=True))
            prob = exponent / jnp.sum(exponent, -1, keepdims=True)
            probs[rows] = prob.astype(BF16)
            grad_prob = nt(g[rows], v)
            grad_score = prob * (grad_prob - jnp.sum(grad_prob * prob, -1, keepdims=True))
            dscore[rows] = grad_score.astype(BF16)
        pb, db = probs[...], dscore[...]
        mixed[:, h * HEAD : (h + 1) * HEAD] = nn(pb, v).astype(BF16)
        grads[:, h * HEAD : (h + 1) * HEAD] = (nn(db, k) * scale).astype(BF16)
        grads[:, 256 + h * HEAD : 256 + (h + 1) * HEAD] = (tn(db, q) * scale).astype(BF16)
        grads[:, 512 + h * HEAD : 512 + (h + 1) * HEAD] = tn(pb, g).astype(BF16)

    def norm_part(plane, column):
        feature = pl.ds(pl.multiple_of((plane * NX + column) * SLICE, SLICE), SLICE)
        term = nt(grads[...], wts[feature, 0:768])
        for p in range(NZ):
            gn[plane, column, source(p)] = term[p * ROWS : (p + 1) * ROWS].astype(BF16)

    def target(p):
        return mod(f + ORDER[p], NZ)

    norm_part(0, xo)
    for p in range(NZ):
        cp.send(("a", p), gn.at[0, xo, target(p)], part_l.at[p], right)
    norm_part(1, xo)
    for p in range(NZ):
        cp.send(("b", p), gn.at[1, xo, target(p)], part_r.at[p], left)
    norm_part(1, xr)
    for p in range(NZ):
        cp.send(("c", p), gn.at[1, xr, target(p)], in_l.at[p, 1], right)
    norm_part(0, xl)
    for p in range(NZ):
        cp.send(("d", p), gn.at[0, xl, target(p)], in_r.at[p, 0], left)
    norm_part(0, xr)
    norm_part(1, xl)

    def sum_x(p):
        j = target(p)
        cp.arrived(("a", p), part_l.at[p], left)
        sum_r[p] = (gn[0, xr, j].astype(F32) + part_l[p].astype(F32)).astype(BF16)
        cp.send(("e", p), sum_r.at[p], in_l.at[p, 0], right)
        cp.arrived(("b", p), part_r.at[p], right)
        sum_l[p] = (gn[1, xl, j].astype(F32) + part_r[p].astype(F32)).astype(BF16)
        cp.send(("f", p), sum_l.at[p], in_r.at[p, 1], left)

    product = jnp.zeros((TOKENS, 128), F32)
    for n in range(6):
        cols = slice(n * 128, (n + 1) * 128)
        product = product + grads[:, cols].astype(F32) * qkv[:, cols].astype(F32)
    column = jnp.broadcast_to(jnp.sum(product, -1, keepdims=True), (TOKENS, 128))
    for p in range(NZ):
        m_part[pl.ds(source(p), 1), :] = to_row(column[p * ROWS : (p + 1) * ROWS])
    m_in[t] = m_part[...]
    for k, peer in enumerate(tensors):
        cp.send(("m", k), m_part, m_in.at[t], peer)

    for p in range(2):
        sum_x(p)
    norm_part(0, x)
    norm_part(1, x)
    for p in range(2, NZ):
        sum_x(p)

    for k, peer in enumerate(tensors):
        cp.arrived(("m", k), m_in.at[mod(t - k - 1, NT)], peer)
    row_sum = m_in[0]
    for k in range(1, NT):
        row_sum = row_sum + m_in[k]
    m_sum[...] = row_sum * (1.0 / WIDTH)
    act[...] = jnp.zeros((8, SLICE), F32)
    gterm[...] = jnp.zeros((8, SLICE), F32)

    def weight_terms(n):
        cols = slice(n * SLICE, (n + 1) * SLICE)
        term = tn(normed[:, cols], grads[...]).astype(BF16)
        term_out = tn(up[:, cols], mixed[...]).astype(BF16)
        for r in range(4):
            gw[n, r // 2, r % 2, :, 0:768] = term[64 * r : 64 * r + 64]
            gw[n, r // 2, r % 2, :, 768:1024] = term_out[64 * r : 64 * r + 64]

    def sum_y(p):
        j = target(p)
        cp.arrived(("c", p), in_l.at[p, 1], left)
        cp.arrived(("d", p), in_r.at[p, 0], right)
        cp.arrived(("e", p), in_l.at[p, 0], left)
        cp.arrived(("f", p), in_r.at[p, 1], right)
        theirs = (
            gn[1 - yh, x, j].astype(F32)
            + in_l[p, 1 - yh].astype(F32)
            + in_r[p, 1 - yh].astype(F32)
        )
        ysend[p] = theirs.astype(BF16)
        cp.send(("sy", p), ysend.at[p], yin.at[p], other)

    def to_frames(p):
        j = target(p)
        cp.arrived(("sy", p), yin.at[p], other)
        grad_norm = (
            gn[yh, x, j].astype(F32)
            + in_l[p, yh].astype(F32)
            + in_r[p, yh].astype(F32)
            + yin[p].astype(F32)
        )
        rows = tok[yh, x, j, 0].astype(F32)
        inverse = to_column(meta_in[j, 0:1, :])
        mean = to_column(m_sum[pl.ds(j, 1), :])
        grad_hidden = tok[yh, x, j, 1].astype(F32) + inverse * (
            gain_t * grad_norm - rows * (gain_inv * mean)
        )
        zsend[p] = grad_hidden.astype(BF16)
        if p == 0:
            local(zsend.at[0], full.at[yh, x, f], 0).wait()
        else:
            cp.send(("bz", p), zsend.at[p], full.at[yh, x, f], {"frame": j})
        gterm[0:1] += jnp.sum(grad_norm * rows, 0, keepdims=True)
        names = lax.broadcasted_iota(jnp.int32, (8, SLICE), 0).astype(F32)
        for fr in range(2):
            name = jnp.concatenate([meta_in[j, 1 + fr : 2 + fr, :]] * 2, 1)
            frame_sum = jnp.sum(grad_hidden[fr * SITES : (fr + 1) * SITES], 0, keepdims=True)
            act[...] += jnp.where(names == name, frame_sum, 0.0)

    def back_y(p):
        j = source(p)
        mine = full.at[yh, x, j]
        if p > 0:
            cp.arrived(("bz", p), mine, other)
        cp.send(("by", p), mine, mine, other)
        cp.send(("br", p), mine, mine, right)
        cp.send(("bl", p), mine, mine, left)

    def back_x(p):
        j = source(p)
        theirs = full.at[1 - yh, x, j]
        cp.arrived(("by", p), theirs, other)
        cp.send(("bor", p), theirs, theirs, right)
        cp.send(("bol", p), theirs, theirs, left)

    def back_forward(p):
        j = source(p)
        block = full.at[yh, xl, j]
        cp.arrived(("br", p), block, left)
        cp.send(("bfr", p), block, block, right)
        cp.arrived(("bl", p), full.at[yh, xr, j], right)
        block = full.at[1 - yh, xr, j]
        cp.arrived(("bol", p), block, right)
        cp.send(("bfl", p), block, block, left)
        cp.arrived(("bor", p), full.at[1 - yh, xl, j], left)

    def back_last(p):
        j = source(p)
        cp.arrived(("bfr", p), full.at[yh, xo, j], left)
        cp.arrived(("bfl", p), full.at[1 - yh, xo, j], right)

    def term(j, o):
        row = yl if o == 0 else 1 - yl
        return gw[j, row, c].astype(F32) + cin[j, row].astype(F32)

    def ring(step, o):
        if step == 0:
            far = mod(f + 4, NZ)
            if o == 0:
                rs_up[0, 0] = term(far, 0).astype(BF16)
                cp.send(("ru", 0, 0), rs_up.at[0, 0], ri_up.at[0, 0], z_up)
            else:
                rs_down[0, 1] = term(far, 1).astype(BF16)
                cp.send(("rd", 0, 1), rs_down.at[0, 1], ri_down.at[0, 1], z_down)
        elif step < 4:
            value = term(mod(f + 4 - step, NZ), o)
            if step > 1 or o == 0:
                cp.arrived(("ru", step - 1, o), ri_up.at[step - 1, o], z_down)
                value = value + ri_up[step - 1, o].astype(F32)
            rs_up[step, o] = value.astype(BF16)
            cp.send(("ru", step, o), rs_up.at[step, o], ri_up.at[step, o], z_up)
            value = term(mod(f - 4 + step, NZ), o)
            if step > 1 or o == 1:
                cp.arrived(("rd", step - 1, o), ri_down.at[step - 1, o], z_up)
                value = value + ri_down[step - 1, o].astype(F32)
            rs_down[step, o] = value.astype(BF16)
            cp.send(("rd", step, o), rs_down.at[step, o], ri_down.at[step, o], z_down)
        elif step == 4:
            cp.arrived(("ru", 3, o), ri_up.at[3, o], z_down)
            cp.arrived(("rd", 3, o), ri_down.at[3, o], z_up)
            value = term(f, o) + ri_up[3, o].astype(F32) + ri_down[3, o].astype(F32)
            if o == 1:
                psend[...] = value.astype(BF16)
                cp.send("py", psend, pin, ypeer)
            else:
                total_w = value
                return total_w
        return None

    def small_z_send():
        small[0:8] = act[...]
        small[8:16] = gterm[...] * gain_inv
        zin[f] = small[...]
        for k, peer in enumerate(frames):
            cp.send(("sz", k), small, zin.at[f], peer)

    def small_z_recv():
        for k, peer in enumerate(frames):
            cp.arrived(("sz", k), zin.at[mod(f - k - 1, NZ)], peer)
        acc = zin[0]
        for k in range(1, NZ):
            acc = acc + zin[k]
        sent[...] = acc
        sin[s] = acc
        for k, peer in enumerate(spaces):
            cp.send(("ss", k), sent, sin.at[s], peer)

    def small_s_recv():
        for k, peer in enumerate(spaces):
            cp.arrived(("ss", k), sin.at[mod(s - k - 1, 4)], peer)
        acc = sin[0]
        for k in range(1, 4):
            acc = acc + sin[k]
        total[...] = acc
        small_out[t] = acc
        for k, peer in enumerate(tensors):
            cp.send(("st", k), total, small_out.at[t], peer)

    def small_t_recv():
        for k, peer in enumerate(tensors):
            cp.arrived(("st", k), small_out.at[mod(t - k - 1, NT)], peer)

    def core_send():
        cp.send("core", gw.at[:, :, 1 - c], cin, cpeer)

    def core_recv():
        cp.arrived("core", cin, cpeer)

    stages = [sum_y, to_frames, back_y, back_x, back_forward]
    extra = {
        0: [lambda: [weight_terms(n) for n in (0, 1, 2, 3)]],
        1: [lambda: [weight_terms(n) for n in (4, 5, 6, 7)], core_send],
        2: [core_recv, lambda: ring(0, 0), lambda: ring(0, 1)],
        3: [lambda: ring(1, 1)],
        4: [lambda: ring(1, 0)],
        5: [lambda: ring(2, 1)],
        6: [lambda: ring(2, 0)],
        7: [lambda: ring(3, 1)],
        8: [lambda: ring(3, 0), small_z_send],
        9: [lambda: ring(4, 1), small_z_recv],
        10: [small_s_recv],
        11: [small_t_recv],
    }
    for p in range(NZ + len(stages) - 1):
        for lag, stage in enumerate(stages):
            if 0 <= p - lag < NZ:
                stage(p - lag)
        for action in extra.get(p, ()):
            action()
    own = ring(4, 0)
    cp.arrived("py", pin, ypeer)
    own = own + pin[...].astype(F32)
    for n in range(3):
        wq_sum[n] = own[:, n * 256 : (n + 1) * 256]
    wo_sum[...] = own[:, 768:1024]
    for p in range(NZ):
        back_last(p)

    for n in range(NT):
        cols = slice(n * SLICE, (n + 1) * SLICE)
        for b in range(2):
            blocks = [full[n // NX, n % NX, b * 4 + r].astype(F32) for r in range(4)]
            for fr in range(2):
                rows = slice(fr * SITES, (fr + 1) * SITES)
                out[2 * b + fr, :, cols] = jnp.concatenate(
                    [block[rows] for block in blocks], 0
                ).astype(BF16)
    cp.drain()


def on_device(inputs, upstream, action_ids, frame_time, action_table, gain, w_qkv, w_out):
    f = lax.axis_index("frame")
    actions = action_table.shape[0]
    flat_ids = action_ids.reshape(4)
    onehot = (flat_ids[:, None] == jnp.arange(actions, dtype=jnp.int32)).astype(F32)
    embedded = jnp.einsum("fa,ad->fd", onehot, action_table, precision=lax.Precision.HIGHEST)
    ids = jnp.broadcast_to(flat_ids.astype(F32)[:, None], (4, 128))

    times = lax.dynamic_index_in_dim(frame_time, f // 4, 0, keepdims=False).reshape(NZ, 2)
    times = times[(f - jnp.array(ORDER, jnp.int32)) % NZ]
    code = times[:, :, None] + 64 * jnp.arange(SITES, dtype=jnp.int32)[None, None, :]
    code = code.reshape(TOKENS).astype(F32)
    code_col = jnp.broadcast_to(code[:, None], (TOKENS, 128))
    code_row = jnp.broadcast_to(code[None, :], (8, TOKENS))

    vmem = pl.BlockSpec(memory_space=pltpu.VMEM)
    hbm = pl.BlockSpec(memory_space=pl.ANY)
    chunk = (ROWS, SLICE)
    ring_shape = (4, 2, 64, 1024)
    scratch = [
        ((4, 144, WIDTH), BF16),
        ((4, 144, SLICE), BF16),
        ((NZ, 2) + chunk, BF16),
        ((NZ, 8, 128), F32),
        ((NZ, 8, 128), F32),
        ((2, NX, NZ, 2) + chunk, BF16),
        ((WIDTH, 1024), BF16),
        ((TOKENS, WIDTH), BF16),
        ((TOKENS, WIDTH), BF16),
        ((TOKENS, TOKENS), F32),
        ((TOKENS, 1024), BF16),
        ((TOKENS, 256), BF16),
        ((TOKENS, 768), BF16),
        ((TOKENS, TOKENS), BF16),
        ((TOKENS, TOKENS), BF16),
        ((NZ, 128), F32),
        ((NT, NZ, 128), F32),
        ((NZ, 128), F32),
        ((2, NX, NZ) + chunk, BF16),
        ((NZ, 2, 2, 64, 1024), BF16),
        ((NZ,) + chunk, BF16),
        ((NZ,) + chunk, BF16),
        ((NZ,) + chunk, BF16),
        ((NZ,) + chunk, BF16),
        ((NZ, 2) + chunk, BF16),
        ((NZ, 2) + chunk, BF16),
        ((NZ,) + chunk, BF16),
        ((NZ,) + chunk, BF16),
        ((NZ,) + chunk, BF16),
        ((NZ, 2, 64, 1024), BF16),
        (ring_shape, BF16),
        (ring_shape, BF16),
        (ring_shape, BF16),
        (ring_shape, BF16),
        ((64, 1024), BF16),
        ((64, 1024), BF16),
        ((2, NX, NZ) + chunk, BF16),
        ((8, SLICE), F32),
        ((8, SLICE), F32),
        ((16, SLICE), F32),
        ((NZ, 16, SLICE), F32),
        ((16, SLICE), F32),
        ((4, 16, SLICE), F32),
        ((16, SLICE), F32),
    ]
    grad_inputs, wq_sum, wo_sum, sums = pl.pallas_call(
        kernel,
        out_shape=(
            jax.ShapeDtypeStruct((4, 144, WIDTH), BF16),
            jax.ShapeDtypeStruct((3, 64, 256), F32),
            jax.ShapeDtypeStruct((64, 256), F32),
            jax.ShapeDtypeStruct((NT, 16, SLICE), F32),
        ),
        in_specs=[hbm] * 4 + [vmem] * 5,
        out_specs=(vmem,) * 4,
        scratch_shapes=[pltpu.VMEM(shape, kind) for shape, kind in scratch]
        + [
            pltpu.SemaphoreType.DMA((SLOTS,)),
            pltpu.SemaphoreType.DMA((SLOTS,)),
            pltpu.SemaphoreType.DMA((6,)),
        ],
        compiler_params=pltpu.CompilerParams(
            collective_id=0, has_side_effects=True, vmem_limit_bytes=VMEM_BYTES
        ),
    )(
        inputs.reshape(4, 144, WIDTH),
        upstream.reshape(4, 144, WIDTH),
        w_qkv.transpose(1, 0, 2),
        w_out,
        embedded,
        ids,
        gain.reshape(1, WIDTH),
        code_col,
        code_row,
    )
    sums = sums.transpose(1, 0, 2).reshape(16, WIDTH)
    return (
        grad_inputs.reshape(inputs.shape),
        wq_sum.transpose(1, 0, 2),
        wo_sum,
        sums[8],
        sums[:8],
    )


def solution(mesh):
    return jax.shard_map(
        on_device,
        mesh=mesh,
        in_specs=(
            P(None, "frame", "space", None),
            P(None, "frame", "space", None),
            P(None, "frame"),
            P(),
            P(),
            P(),
            P(("frame", "space"), None, "tensor"),
            P(("frame", "space"), "tensor"),
        ),
        out_specs=(
            P(None, "frame", "space", None),
            P(("frame", "space"), None, "tensor"),
            P(("frame", "space"), "tensor"),
            P(),
            P(),
        ),
        check_vma=False,
    )
```

```python
import math

import jax
import jax.numpy as jnp
from jax import lax
from jax.experimental import pallas as pl
from jax.experimental.pallas import tpu as pltpu
from jax.sharding import PartitionSpec as P

HEAD = 128
NORM_EPSILON = 1e-06
MESH = pl.DeviceIdType.MESH
BF16 = jnp.bfloat16
F32 = jnp.float32

NZ, NX, NT = 8, 4, 8
SITES = 36
ROWS = 72
TOKENS = NZ * ROWS
SLICE = 256
WIDTH = 2048
VMEM_BYTES = 58 * 1024 * 1024
ORDER = (0, 1, 7, 2, 6, 3, 5, 4)
SLOTS = 400
ACROSS = (3, 4, 5, 6, 7)
GATHER = (
    ("w", 0, 0), ("zsend",), ("t0a", 0), ("t1a", 0), ("t1b", 0), ("w", 0, 1), ("w", 1, 0), ("t1c", 0),
    ("t0b", 0), ("t0a", 1), ("t1a", 1), ("t0a", 2), ("t1a", 2), ("t0c", 0), ("t0b", 1), ("t0a", 3),
    ("t1a", 3), ("t0a", 4), ("t1a", 4), ("t1b", 1), ("t1c", 1), ("t0b", 2), ("t1b", 2), ("t0b", 3),
    ("t1c", 2), ("t0b", 4), ("t0a", 5), ("t1a", 5), ("t0a", 6), ("t1a", 6), ("t0c", 1), ("t1b", 3),
    ("t1c", 3), ("t0a", 7), ("t1a", 7), ("t1b", 4), ("t1c", 4), ("w", 1, 1), ("t0c", 2), ("t0b", 5),
    ("t0c", 3), ("t0c", 4), ("t0b", 6), ("w", 2, 0), ("t1b", 5), ("t1c", 5), ("t1b", 6), ("w", 2, 1),
    ("t0b", 7), ("t1c", 6), ("rp", 0), ("w", 3, 0), ("t1b", 7), ("t1c", 7), ("t0c", 5), ("w", 3, 1),
    ("rp", 1), ("t0c", 6), ("w", 4, 0), ("t0c", 7), ("rp", 2), ("w", 4, 1),
)
REDUCE = (
    ("np", 0), ("np0s",), ("np", 1), ("ra", 0), ("ra", 1), ("ra", 2), ("m",), ("wt", 0), ("wt", 1), ("wt", 2),
    ("rx", 0), ("rx", 3), ("wt", 3), ("rg", 0), ("rx", 1), ("wt", 4), ("wt", 5), ("rx", 2), ("rx", 4),
    ("wt", 6), ("sy", 0), ("wt", 7), ("tf", 3), ("rg", 1, 0), ("rg", 1, 1), ("rx", 5), ("sy", 1), ("sy", 2),
    ("tf", 4), ("rx", 6), ("ba", 3), ("tf", 5), ("rx", 7), ("rg", 2, 0), ("tf", 0), ("ba", 0), ("tf", 6),
    ("tf", 1), ("tf", 2), ("bb", 3), ("rg", 2, 1), ("ba", 4), ("tf", 7), ("bb", 0), ("s0",), ("ba", 5),
    ("bc", 3), ("bb", 4), ("bc", 0), ("rg", 3, 0), ("bb", 5), ("ba", 6), ("ba", 1), ("ba", 2), ("bc", 4),
    ("bc", 5), ("bb", 6), ("rg", 3, 1), ("bb", 1), ("bb", 2), ("ba", 7), ("s1",), ("bc", 6), ("bb", 7),
    ("s2",), ("bc", 1), ("bc", 2), ("rg", 4, 1), ("bc", 7), ("rg", 4, 0),
)


def mod(value, n):
    return lax.rem(value + 2 * n, n)


def nt(a, b):
    return lax.dot_general(a, b, (((1,), (1,)), ((), ())), preferred_element_type=F32)


def tn(a, b):
    return lax.dot_general(a, b, (((0,), (0,)), ((), ())), preferred_element_type=F32)


def nn(a, b):
    return jnp.dot(a, b, preferred_element_type=F32)


class Copies:
    def __init__(self, send_sems, recv_sems):
        self.send_sems, self.recv_sems = send_sems, recv_sems
        self.slots, self.started = {}, []

    def slot(self, name):
        return self.slots.setdefault(name, len(self.slots))

    def send(self, name, src, dst, device):
        slot = self.slot(name)
        copy = pltpu.make_async_remote_copy(
            src_ref=src,
            dst_ref=dst,
            send_sem=self.send_sems.at[slot],
            recv_sem=self.recv_sems.at[slot],
            device_id=device,
            device_id_type=MESH,
        )
        copy.start()
        self.started.append(copy)

    def arrived(self, name, dst, device):
        slot = self.slot(name)
        pltpu.make_async_remote_copy(
            src_ref=dst,
            dst_ref=dst,
            send_sem=self.send_sems.at[slot],
            recv_sem=self.recv_sems.at[slot],
            device_id=device,
            device_id_type=MESH,
        ).wait_recv()

    def drain(self):
        for copy in self.started:
            copy.wait_send()


def kernel(
    inputs, upstream, w3, wo, ids, times, table, gain,
    out, wq_sum, wo_sum, gain_out, act_out,
    in_v, up_v, embedded, xu, meta, meta_in, tok, wts, normed, up, bias, qkv, mixed, grads, probs, dscore,
    m_part, m_in, m_sum, gn, gw, part_l, part_r, sum_l, sum_r, in_l, in_r, ysend, yin, zsend,
    cin, rs_up, rs_down, ri_up, ri_down, psend, pin, full, ry, rsend, rin, small_out,
    act, gterm, small, zin, sent, sin, total,
    send_sems, recv_sems, local_sems,
):
    f = lax.axis_index("frame")
    s = lax.axis_index("space")
    t = lax.axis_index("tensor")
    yl, c, yh, x = s // 2, s % 2, t // NX, t % NX
    xl, xr, xo = mod(x - 1, NX), mod(x + 1, NX), mod(x + 2, NX)
    right, left = {"tensor": yh * NX + xr}, {"tensor": yh * NX + xl}
    other = {"tensor": (1 - yh) * NX + x}
    opposite = {"tensor": yh * NX + xo}
    z_up, z_down = {"frame": mod(f + 1, NZ)}, {"frame": mod(f - 1, NZ)}
    ypeer = {"space": (1 - yl) * 2 + c}
    cpeer = {"space": yl * 2 + 1 - c}
    frames = [{"frame": mod(f + k, NZ)} for k in range(1, NZ)]
    spaces = [{"space": mod(s + k, 4)} for k in range(1, 4)]
    tensors = [{"tensor": mod(t + k, NT)} for k in range(1, NT)]
    peers = frames + spaces + tensors
    my_cols = pl.ds(pl.multiple_of(t * SLICE, SLICE), SLICE)

    greeted = pltpu.get_barrier_semaphore()
    for peer in peers:
        pl.semaphore_signal(greeted, inc=1, device_id=peer, device_id_type=MESH)

    cp = Copies(send_sems, recv_sems)

    def w_rows(z, row, plane):
        return wts.at[pl.ds(pl.multiple_of((z * 4 + row * 2 + plane) * 64, 64), 64), :]

    def local(src, dst, n):
        copy = pltpu.make_async_copy(src, dst, local_sems.at[n])
        copy.start()
        return copy

    load_in = local(inputs, in_v, 0)
    load_up = local(upstream.at[:, :, my_cols], up_v, 1)
    own_rows = pl.ds(pl.multiple_of((f * 4 + s) * 64, 64), 64)
    load_w = [
        local(w3.at[n], wts.at[own_rows, n * 256 : (n + 1) * 256], 2 + n) for n in range(3)
    ] + [local(wo, wts.at[own_rows, 768:1024], 5)]

    def source(p):
        return mod(f - ORDER[p], NZ)

    def target(p):
        return mod(f + ORDER[p], NZ)

    spot = lax.broadcasted_iota(jnp.int32, (ROWS, 128), 0)
    lane = lax.broadcasted_iota(jnp.int32, (8, TOKENS), 1)
    columns = []
    time_row = jnp.zeros((8, TOKENS), jnp.int32)
    for p in range(NZ):
        pair = [times[f // 4, 2 * source(p) + fr] for fr in range(2)]
        second = spot >= SITES
        columns.append(jnp.where(second, pair[1] + 64 * (spot - SITES), pair[0] + 64 * spot))
        for fr in range(2):
            start = p * ROWS + fr * SITES
            time_row = jnp.where((lane >= start) & (lane < start + SITES), pair[fr], time_row)
    site_row = lax.rem(lane, SITES)
    code_col = jnp.concatenate(columns, 0)[:, 0:1]
    code_row = (time_row + 64 * site_row)[0:1, :]
    apart = code_col - code_row
    bias[...] = jnp.where((apart >= 0) & (apart <= 15), 0.0, -1e30)

    names = lax.broadcasted_iota(jnp.int32, (8, WIDTH), 0)
    for i in range(4):
        embedded[i : i + 1] = jnp.sum(
            jnp.where(names == ids[i], table[...], 0.0), 0, keepdims=True
        )
    load_in.wait()

    lane = lax.broadcasted_iota(jnp.int32, (ROWS, 128), 1)
    eye = (lane == lax.broadcasted_iota(jnp.int32, (ROWS, 128), 0)).astype(F32)

    def to_row(column):
        return jnp.sum(eye * column, 0, keepdims=True)

    def to_column(row):
        return jnp.sum(eye * row, 1, keepdims=True)

    gain_t = gain[0:1, my_cols]
    gain_inv = 1.0 / gain_t
    pieces, inverses = [], []
    for i in range(4):
        squares = jnp.zeros((144, SLICE), F32)
        for n in range(NT):
            cols = slice(n * SLICE, (n + 1) * SLICE)
            hidden = in_v[i, :, cols].astype(F32) + embedded[i : i + 1, cols]
            squares = squares + hidden * hidden
        inverse = lax.rsqrt(jnp.sum(squares, -1, keepdims=True) * (1.0 / WIDTH) + NORM_EPSILON)
        hidden = in_v[i, :, my_cols].astype(F32) + embedded[i : i + 1, my_cols]
        pieces.append(hidden * inverse * gain_t)
        inverses.append(jnp.broadcast_to(inverse, (144, 128)))
    load_up.wait()
    for b in range(2):
        for r in range(4):
            rows = slice(r * SITES, (r + 1) * SITES)

            def chunk(a):
                return jnp.concatenate([a[2 * b][rows], a[2 * b + 1][rows]], 0)

            xu[b * 4 + r, 0] = chunk(pieces).astype(BF16)
            xu[b * 4 + r, 1] = jnp.concatenate(
                [up_v[2 * b].astype(F32)[rows], up_v[2 * b + 1].astype(F32)[rows]], 0
            ).astype(BF16)
            meta[b * 4 + r] = jnp.concatenate(
                [to_row(chunk(inverses))]
                + [jnp.full((1, 128), ids[2 * b + fr].astype(F32), F32) for fr in range(2)]
                + [jnp.zeros((5, 128), F32)],
                0,
            )

    pl.semaphore_wait(greeted, len(peers))

    def tokens_send():
        for p in range(1, NZ):
            j = target(p)
            cp.send(("z", p), xu.at[j], tok.at[yh, x, f], {"frame": j})
            cp.send(("meta", p), meta.at[j], meta_in.at[f], {"frame": j})
        local(xu.at[f], tok.at[yh, x, f], 0).wait()
        meta_in[f] = meta[f]

    def normed_a(p):
        j = source(p)
        if p > 0:
            cp.arrived(("z", p), tok.at[yh, x, j], other)
            cp.arrived(("meta", p), meta_in.at[j], other)
        mine = tok.at[yh, x, j, 0]
        cp.send(("t0y", p), mine, mine, other)
        cp.send(("t0r", p), mine, mine, right)
        cp.send(("t0l", p), mine, mine, left)

    def normed_b(p):
        theirs = tok.at[1 - yh, x, source(p), 0]
        cp.arrived(("t0y", p), theirs, other)
        cp.send(("t0or", p), theirs, theirs, right)
        cp.send(("t0ol", p), theirs, theirs, left)

    def normed_c(p):
        j = source(p)
        block = tok.at[yh, xl, j, 0]
        cp.arrived(("t0r", p), block, left)
        cp.send(("t0fr", p), block, block, right)
        block = tok.at[1 - yh, xr, j, 0]
        cp.arrived(("t0ol", p), block, right)
        cp.send(("t0fl", p), block, block, left)

    def upstream_a(p):
        mine = tok.at[yh, x, source(p), 1]
        cp.send(("t1r", p), mine, mine, right)
        cp.send(("t1l", p), mine, mine, left)
        cp.send(("t1y", p), mine, mine, other)
        cp.send(("t1o", p), mine, mine, opposite)

    def upstream_b(p):
        j = source(p)
        for name, at, device in ((("t1r", p), xl, left), (("t1l", p), xr, right)):
            block = tok.at[yh, at, j, 1]
            cp.arrived(name, block, device)
            cp.send((name, "y"), block, block, other)

    def upstream_c(p):
        block = tok.at[yh, xo, source(p), 1]
        cp.arrived(("t1o", p), block, opposite)
        cp.send(("t1oy", p), block, block, other)

    def tokens_last(p):
        j = source(p)
        cp.arrived(("t0l", p), tok.at[yh, xr, j, 0], right)
        cp.arrived(("t0or", p), tok.at[1 - yh, xl, j, 0], left)
        cp.arrived(("t0fr", p), tok.at[yh, xo, j, 0], left)
        cp.arrived(("t0fl", p), tok.at[1 - yh, xo, j, 0], right)
        cp.arrived(("t1y", p), tok.at[1 - yh, x, j, 1], other)
        cp.arrived((("t1r", p), "y"), tok.at[1 - yh, xl, j, 1], other)
        cp.arrived((("t1l", p), "y"), tok.at[1 - yh, xr, j, 1], other)
        cp.arrived(("t1oy", p), tok.at[1 - yh, xo, j, 1], other)

    def repack(pair):
        for p in (2 * pair, 2 * pair + 1):
            tokens_last(p)
        rows = slice(pair * 2 * ROWS, (pair + 1) * 2 * ROWS)
        for n in range(NT):
            cols = slice(n * SLICE, (n + 1) * SLICE)
            for arr, dst in ((0, normed), (1, up)):
                dst[rows, cols] = jnp.concatenate(
                    [
                        tok[n // NX, n % NX, source(p), arr].astype(F32)
                        for p in (2 * pair, 2 * pair + 1)
                    ],
                    0,
                ).astype(BF16)

    def weights(step, o):
        row = yl if o == 0 else 1 - yl
        if step == 0:
            block = w_rows(f, row, c)
            if o == 0:
                for copy in load_w:
                    copy.wait()
                cp.send("wy", block, block, ypeer)
            else:
                cp.arrived("wy", block, ypeer)
            cp.send(("wu", 0, o), block, block, z_up)
            cp.send(("wd", 0, o), block, block, z_down)
            cp.send(("wc", 0, o), block, block, cpeer)
        elif step < 4:
            block = w_rows(mod(f - step, NZ), row, c)
            cp.arrived(("wu", step - 1, o), block, z_down)
            if step < 3 or o == 0:
                cp.send(("wu", step, o), block, block, z_up)
            cp.send(("wc", step, o), block, block, cpeer)
            block = w_rows(mod(f + step, NZ), row, c)
            cp.arrived(("wd", step - 1, o), block, z_up)
            if step < 3 or o == 1:
                cp.send(("wd", step, o), block, block, z_down)
            cp.send(("wc", -step, o), block, block, cpeer)
        else:
            block = w_rows(mod(f + 4, NZ), row, c)
            if o == 0:
                cp.arrived(("wu", 3, o), block, z_down)
            else:
                cp.arrived(("wd", 3, o), block, z_up)
            cp.send(("wc", 4, o), block, block, cpeer)

    def weights_last():
        for step in range(-3, 5):
            for o in range(2):
                row = yl if o == 0 else 1 - yl
                cp.arrived(("wc", step, o), w_rows(mod(f - step, NZ), row, 1 - c), cpeer)

    actions = {
        "w": weights, "zsend": tokens_send, "t0a": normed_a, "t0b": normed_b, "t0c": normed_c,
        "t1a": upstream_a, "t1b": upstream_b, "t1c": upstream_c, "rp": repack,
    }
    for name, *where in GATHER:
        actions[name](*where)
    repack(3)
    weights_last()

    @pl.loop(0, 3)
    def _(n):
        at = pl.ds(pl.multiple_of(n * 256, 256), 256)
        qkv[:, at] = nn(normed[...], wts[:, at]).astype(BF16)

    qkv[:, 768:1024] = nn(up[...], wts[:, 768:1024]).astype(BF16)

    scale = 1.0 / math.sqrt(HEAD)
    half = TOKENS // 2
    for h in range(2):
        q, k, v, g = (qkv[:, n * 256 + h * HEAD : n * 256 + (h + 1) * HEAD] for n in range(4))
        for part in range(2):
            rows = slice(part * half, (part + 1) * half)
            scores = nt(q[rows], k) * scale + bias[rows]
            exponent = jnp.exp(scores - jnp.max(scores, -1, keepdims=True))
            prob = exponent / jnp.sum(exponent, -1, keepdims=True)
            probs[rows] = prob.astype(BF16)
            grad_prob = nt(g[rows], v)
            grad_score = prob * (grad_prob - jnp.sum(grad_prob * prob, -1, keepdims=True))
            dscore[rows] = grad_score.astype(BF16)
        pb, db = probs[...], dscore[...]
        mixed[:, h * HEAD : (h + 1) * HEAD] = nn(pb, v).astype(BF16)
        grads[:, h * HEAD : (h + 1) * HEAD] = (nn(db, k) * scale).astype(BF16)
        grads[:, 256 + h * HEAD : 256 + (h + 1) * HEAD] = (tn(db, q) * scale).astype(BF16)
        grads[:, 512 + h * HEAD : 512 + (h + 1) * HEAD] = tn(pb, g).astype(BF16)

    def norm_part(plane, column):
        feature = pl.ds(pl.multiple_of((plane * NX + column) * SLICE, SLICE), SLICE)
        term = nt(grads[...], wts[feature, 0:768])
        for p in range(NZ):
            gn[plane, column, source(p)] = term[p * ROWS : (p + 1) * ROWS].astype(BF16)

    def norm_parts(which):
        plane = 1 - yh if which == 0 else yh
        for column in range(NX):
            norm_part(plane, column)

    def send_across():
        for p in ACROSS:
            cp.send(("ry", p), gn.at[1 - yh, :, target(p)], ry.at[p], other)

    def reduce_a(p):
        j = target(p)
        cp.send(("a", p), gn.at[1 - yh, xo, j], part_l.at[p], right)
        cp.send(("b", p), gn.at[yh, xo, j], part_r.at[p], left)
        cp.send(("c", p), gn.at[yh, xr, j], in_l.at[p, 0], right)
        cp.send(("d", p), gn.at[1 - yh, xl, j], in_r.at[p, 1], left)

    def reduce_x(p):
        j = target(p)
        if p in ACROSS:
            cp.arrived(("ry", p), ry.at[p], other)
            for i, (column, device) in enumerate(((xr, right), (xl, left), (xo, opposite))):
                rsend[p, i] = (
                    gn[yh, column, j].astype(F32) + ry[p, column].astype(F32)
                ).astype(BF16)
                cp.send(("rx", p, i), rsend.at[p, i], rin.at[p, i], device)
            return
        cp.arrived(("a", p), part_l.at[p], left)
        sum_r[p] = (gn[1 - yh, xr, j].astype(F32) + part_l[p].astype(F32)).astype(BF16)
        cp.send(("e", p), sum_r.at[p], in_l.at[p, 1], right)
        cp.arrived(("b", p), part_r.at[p], right)
        sum_l[p] = (gn[yh, xl, j].astype(F32) + part_r[p].astype(F32)).astype(BF16)
        cp.send(("f", p), sum_l.at[p], in_r.at[p, 0], left)

    def send_means():
        product = jnp.zeros((TOKENS, 128), F32)
        for n in range(6):
            cols = slice(n * 128, (n + 1) * 128)
            product = product + grads[:, cols].astype(F32) * qkv[:, cols].astype(F32)
        column = jnp.broadcast_to(jnp.sum(product, -1, keepdims=True), (TOKENS, 128))
        for p in range(NZ):
            m_part[pl.ds(source(p), 1), :] = to_row(column[p * ROWS : (p + 1) * ROWS])
        m_in[t] = m_part[...]
        for k, peer in enumerate(tensors):
            cp.send(("m", k), m_part, m_in.at[t], peer)

    def take_means():
        for k, peer in enumerate(tensors):
            cp.arrived(("m", k), m_in.at[mod(t - k - 1, NT)], peer)
        row_sum = m_in[0]
        for k in range(1, NT):
            row_sum = row_sum + m_in[k]
        m_sum[...] = row_sum * (1.0 / WIDTH)
        act[...] = jnp.zeros((8, SLICE), F32)
        gterm[...] = jnp.zeros((8, SLICE), F32)

    blocks = [mod(f + k, NZ) for k in (4, 3, -3, 2, -2, 1, -1, 0)]
    shared = set()

    def weight_terms(i):
        n = blocks[i]
        cols = pl.ds(pl.multiple_of(n * SLICE, SLICE), SLICE)
        term = tn(normed[:, cols], grads[...]).astype(BF16)
        term_out = tn(up[:, cols], mixed[...]).astype(BF16)
        for r in range(4):
            gw[n, r // 2, r % 2, :, 0:768] = term[64 * r : 64 * r + 64]
            gw[n, r // 2, r % 2, :, 768:1024] = term_out[64 * r : 64 * r + 64]
        cp.send(("core", i), gw.at[n, :, 1 - c], cin.at[n], cpeer)

    def partner_terms(*which):
        for i in which:
            if i not in shared:
                shared.add(i)
                cp.arrived(("core", i), cin.at[blocks[i]], cpeer)

    def sum_y(p):
        j = target(p)
        cp.arrived(("c", p), in_l.at[p, 0], left)
        cp.arrived(("d", p), in_r.at[p, 1], right)
        cp.arrived(("e", p), in_l.at[p, 1], left)
        cp.arrived(("f", p), in_r.at[p, 0], right)
        theirs = (
            gn[1 - yh, x, j].astype(F32) + in_l[p, 1].astype(F32) + in_r[p, 1].astype(F32)
        )
        ysend[p] = theirs.astype(BF16)
        cp.send(("sy", p), ysend.at[p], yin.at[p], other)

    def to_frames(p):
        j = target(p)
        if not shared.issuperset(("mean",)):
            shared.add("mean")
            take_means()
        grad_norm = gn[yh, x, j].astype(F32)
        if p in ACROSS:
            for i, device in enumerate((left, right, opposite)):
                cp.arrived(("rx", p, i), rin.at[p, i], device)
                grad_norm = grad_norm + rin[p, i].astype(F32)
            grad_norm = grad_norm + ry[p, x].astype(F32)
        else:
            cp.arrived(("sy", p), yin.at[p], other)
            grad_norm = (
                grad_norm
                + in_l[p, 0].astype(F32)
                + in_r[p, 0].astype(F32)
                + yin[p].astype(F32)
            )
        rows = tok[yh, x, j, 0].astype(F32)
        inverse = to_column(meta_in[j, 0:1, :])
        mean = to_column(m_sum[pl.ds(j, 1), :])
        grad_hidden = tok[yh, x, j, 1].astype(F32) + inverse * (
            gain_t * grad_norm - rows * (gain_inv * mean)
        )
        zsend[p] = grad_hidden.astype(BF16)
        if p == 0:
            local(zsend.at[0], full.at[yh, x, f], 0).wait()
        else:
            cp.send(("bz", p), zsend.at[p], full.at[yh, x, f], {"frame": j})
        gterm[0:1] += jnp.sum(grad_norm * rows, 0, keepdims=True)
        labels = lax.broadcasted_iota(jnp.int32, (8, SLICE), 0).astype(F32)
        for fr in range(2):
            name = jnp.concatenate([meta_in[j, 1 + fr : 2 + fr, :]] * 2, 1)
            frame_sum = jnp.sum(grad_hidden[fr * SITES : (fr + 1) * SITES], 0, keepdims=True)
            act[...] += jnp.where(labels == name, frame_sum, 0.0)

    def back_y(p):
        j = source(p)
        mine = full.at[yh, x, j]
        if p > 0:
            cp.arrived(("bz", p), mine, other)
        cp.send(("by", p), mine, mine, other)
        cp.send(("br", p), mine, mine, right)
        cp.send(("bl", p), mine, mine, left)

    def back_x(p):
        j = source(p)
        theirs = full.at[1 - yh, x, j]
        cp.arrived(("by", p), theirs, other)
        cp.send(("bor", p), theirs, theirs, right)
        cp.send(("bol", p), theirs, theirs, left)

    def back_forward(p):
        j = source(p)
        block = full.at[yh, xl, j]
        cp.arrived(("br", p), block, left)
        cp.send(("bfr", p), block, block, right)
        block = full.at[1 - yh, xr, j]
        cp.arrived(("bol", p), block, right)
        cp.send(("bfl", p), block, block, left)

    def back_last(p):
        j = source(p)
        cp.arrived(("bl", p), full.at[yh, xr, j], right)
        cp.arrived(("bor", p), full.at[1 - yh, xl, j], left)
        cp.arrived(("bfr", p), full.at[yh, xo, j], left)
        cp.arrived(("bfl", p), full.at[1 - yh, xo, j], right)

    def term(j, o):
        row = yl if o == 0 else 1 - yl
        return gw[j, row, c].astype(F32) + cin[j, row].astype(F32)

    def ring(step, o=None):
        if step == 0:
            partner_terms(0)
            far = blocks[0]
            rs_up[0, 0] = term(far, 0).astype(BF16)
            cp.send(("ru", 0, 0), rs_up.at[0, 0], ri_up.at[0, 0], z_up)
            rs_down[0, 1] = term(far, 1).astype(BF16)
            cp.send(("rd", 0, 1), rs_down.at[0, 1], ri_down.at[0, 1], z_down)
        elif step < 4:
            partner_terms(2 * step - 1, 2 * step)
            value = term(blocks[2 * step - 1], o)
            if step > 1 or o == 0:
                cp.arrived(("ru", step - 1, o), ri_up.at[step - 1, o], z_down)
                value = value + ri_up[step - 1, o].astype(F32)
            rs_up[step, o] = value.astype(BF16)
            cp.send(("ru", step, o), rs_up.at[step, o], ri_up.at[step, o], z_up)
            value = term(blocks[2 * step], o)
            if step > 1 or o == 1:
                cp.arrived(("rd", step - 1, o), ri_down.at[step - 1, o], z_up)
                value = value + ri_down[step - 1, o].astype(F32)
            rs_down[step, o] = value.astype(BF16)
            cp.send(("rd", step, o), rs_down.at[step, o], ri_down.at[step, o], z_down)
        else:
            partner_terms(7)
            cp.arrived(("ru", 3, o), ri_up.at[3, o], z_down)
            cp.arrived(("rd", 3, o), ri_down.at[3, o], z_up)
            value = term(f, o) + ri_up[3, o].astype(F32) + ri_down[3, o].astype(F32)
            if o == 1:
                psend[...] = value.astype(BF16)
                cp.send("py", psend, pin, ypeer)
                return
            cp.arrived("py", pin, ypeer)
            value = value + pin[...].astype(F32)
            for n in range(3):
                wq_sum[n] = value[:, n * 256 : (n + 1) * 256]
            wo_sum[...] = value[:, 768:1024]

    def small_z_send():
        small[0:8] = act[...]
        small[8:16] = gterm[...] * gain_inv
        zin[f] = small[...]
        for k, peer in enumerate(frames):
            cp.send(("sz", k), small, zin.at[f], peer)

    def small_z_recv():
        for k, peer in enumerate(frames):
            cp.arrived(("sz", k), zin.at[mod(f - k - 1, NZ)], peer)
        acc = zin[0]
        for k in range(1, NZ):
            acc = acc + zin[k]
        sent[...] = acc
        sin[s] = acc
        for k, peer in enumerate(spaces):
            cp.send(("ss", k), sent, sin.at[s], peer)

    def small_s_recv():
        for k, peer in enumerate(spaces):
            cp.arrived(("ss", k), sin.at[mod(s - k - 1, 4)], peer)
        acc = sin[0]
        for k in range(1, 4):
            acc = acc + sin[k]
        total[...] = acc
        small_out[t] = acc
        for k, peer in enumerate(tensors):
            cp.send(("st", k), total, small_out.at[t], peer)

    def small_t_recv():
        for k, peer in enumerate(tensors):
            cp.arrived(("st", k), small_out.at[mod(t - k - 1, NT)], peer)

    actions = {
        "np": norm_parts, "np0s": send_across, "ra": reduce_a, "rx": reduce_x, "m": send_means,
        "wt": weight_terms, "rg": ring, "sy": sum_y, "tf": to_frames, "ba": back_y, "bb": back_x,
        "bc": back_forward, "s0": small_z_send, "s1": small_z_recv, "s2": small_s_recv,
    }
    for name, *where in REDUCE:
        actions[name](*where)
    small_t_recv()
    for n in range(NT):
        cols = slice(n * SLICE, (n + 1) * SLICE)
        act_out[:, cols] = small_out[n, 0:8]
        gain_out[:, cols] = small_out[n, 8:9]
    for p in range(NZ):
        back_last(p)

    for n in range(NT):
        cols = slice(n * SLICE, (n + 1) * SLICE)
        for b in range(2):
            blocks = [full[n // NX, n % NX, b * 4 + r].astype(F32) for r in range(4)]
            for fr in range(2):
                rows = slice(fr * SITES, (fr + 1) * SITES)
                out[2 * b + fr, :, cols] = jnp.concatenate(
                    [block[rows] for block in blocks], 0
                ).astype(BF16)
    cp.drain()


def on_device(inputs, upstream, action_ids, frame_time, action_table, gain, w_qkv, w_out):
    vmem = pl.BlockSpec(memory_space=pltpu.VMEM)
    hbm = pl.BlockSpec(memory_space=pl.ANY)
    smem = pl.BlockSpec(memory_space=pltpu.SMEM)
    chunk = (ROWS, SLICE)
    ring_shape = (4, 2, 64, 1024)
    scratch = [
        ((4, 144, WIDTH), BF16),
        ((4, 144, SLICE), BF16),
        ((4, WIDTH), F32),
        ((NZ, 2) + chunk, BF16),
        ((NZ, 8, 128), F32),
        ((NZ, 8, 128), F32),
        ((2, NX, NZ, 2) + chunk, BF16),
        ((WIDTH, 1024), BF16),
        ((TOKENS, WIDTH), BF16),
        ((TOKENS, WIDTH), BF16),
        ((TOKENS, TOKENS), F32),
        ((TOKENS, 1024), BF16),
        ((TOKENS, 256), BF16),
        ((TOKENS, 768), BF16),
        ((TOKENS, TOKENS), BF16),
        ((TOKENS, TOKENS), BF16),
        ((NZ, 128), F32),
        ((NT, NZ, 128), F32),
        ((NZ, 128), F32),
        ((2, NX, NZ) + chunk, BF16),
        ((NZ, 2, 2, 64, 1024), BF16),
        ((NZ,) + chunk, BF16),
        ((NZ,) + chunk, BF16),
        ((NZ,) + chunk, BF16),
        ((NZ,) + chunk, BF16),
        ((NZ, 2) + chunk, BF16),
        ((NZ, 2) + chunk, BF16),
        ((NZ,) + chunk, BF16),
        ((NZ,) + chunk, BF16),
        ((NZ,) + chunk, BF16),
        ((NZ, 2, 64, 1024), BF16),
        (ring_shape, BF16),
        (ring_shape, BF16),
        (ring_shape, BF16),
        (ring_shape, BF16),
        ((64, 1024), BF16),
        ((64, 1024), BF16),
        ((2, NX, NZ) + chunk, BF16),
        ((NZ, NX) + chunk, BF16),
        ((NZ, 3) + chunk, BF16),
        ((NZ, 3) + chunk, BF16),
        ((NT, 16, SLICE), F32),
        ((8, SLICE), F32),
        ((8, SLICE), F32),
        ((16, SLICE), F32),
        ((NZ, 16, SLICE), F32),
        ((16, SLICE), F32),
        ((4, 16, SLICE), F32),
        ((16, SLICE), F32),
    ]
    grad_inputs, wq_sum, wo_sum, grad_gain, grad_actions = pl.pallas_call(
        kernel,
        out_shape=(
            jax.ShapeDtypeStruct((4, 144, WIDTH), BF16),
            jax.ShapeDtypeStruct((3, 64, 256), F32),
            jax.ShapeDtypeStruct((64, 256), F32),
            jax.ShapeDtypeStruct((1, WIDTH), F32),
            jax.ShapeDtypeStruct((8, WIDTH), F32),
        ),
        in_specs=[hbm] * 4 + [smem] * 2 + [vmem] * 2,
        out_specs=(vmem,) * 5,
        scratch_shapes=[pltpu.VMEM(shape, kind) for shape, kind in scratch]
        + [
            pltpu.SemaphoreType.DMA((SLOTS,)),
            pltpu.SemaphoreType.DMA((SLOTS,)),
            pltpu.SemaphoreType.DMA((6,)),
        ],
        compiler_params=pltpu.CompilerParams(
            collective_id=0, has_side_effects=True, vmem_limit_bytes=VMEM_BYTES
        ),
    )(
        inputs.reshape(4, 144, WIDTH),
        upstream.reshape(4, 144, WIDTH),
        w_qkv.transpose(1, 0, 2),
        w_out,
        action_ids.reshape(4),
        frame_time,
        action_table,
        gain.reshape(1, WIDTH),
    )
    return (
        grad_inputs.reshape(inputs.shape),
        wq_sum.transpose(1, 0, 2),
        wo_sum,
        grad_gain.reshape(WIDTH),
        grad_actions,
    )


def solution(mesh):
    return jax.shard_map(
        on_device,
        mesh=mesh,
        in_specs=(
            P(None, "frame", "space", None),
            P(None, "frame", "space", None),
            P(None, "frame"),
            P(),
            P(),
            P(),
            P(("frame", "space"), None, "tensor"),
            P(("frame", "space"), "tensor"),
        ),
        out_specs=(
            P(None, "frame", "space", None),
            P(("frame", "space"), None, "tensor"),
            P(("frame", "space"), "tensor"),
            P(),
            P(),
        ),
        check_vma=False,
    )
```

```python
import math

import jax
import jax.numpy as jnp
from jax import lax
from jax.experimental import pallas as pl
from jax.experimental.pallas import tpu as pltpu
from jax.sharding import PartitionSpec as P

HEAD = 128
NORM_EPSILON = 1e-06
MESH = pl.DeviceIdType.MESH
BF16 = jnp.bfloat16
F32 = jnp.float32

NZ, NX, NT = 8, 4, 8
SITES = 36
ROWS = 72
TOKENS = NZ * ROWS
SLICE = 256
WIDTH = 2048
VMEM_BYTES = 58 * 1024 * 1024
ORDER = (0, 1, 7, 2, 6, 3, 5, 4)
RECEIVED, SENT = 144, 15
ACROSS = (3, 4, 5, 6, 7)
GATHER = (
    ("w", 0, 0), ("zsend",), ("t0a", 0), ("t1a", 0), ("t1b", 0), ("w", 0, 1), ("w", 1, 0), ("t1c", 0),
    ("t0b", 0), ("t0a", 1), ("t1a", 1), ("t0a", 2), ("t1a", 2), ("t0c", 0), ("t0b", 1), ("t0a", 3),
    ("t1a", 3), ("t0a", 4), ("t1a", 4), ("t1b", 1), ("t1c", 1), ("t0b", 2), ("t1b", 2), ("t0b", 3),
    ("t1c", 2), ("t0b", 4), ("t0a", 5), ("t1a", 5), ("t0a", 6), ("t1a", 6), ("t0c", 1), ("t1b", 3),
    ("t1c", 3), ("t0a", 7), ("t1a", 7), ("t1b", 4), ("t1c", 4), ("w", 1, 1), ("t0c", 2), ("t0b", 5),
    ("t0c", 3), ("t0c", 4), ("t0b", 6), ("w", 2, 0), ("t1b", 5), ("t1c", 5), ("t1b", 6), ("w", 2, 1),
    ("t0b", 7), ("t1c", 6), ("rp", 0), ("w", 3, 0), ("t1b", 7), ("t1c", 7), ("t0c", 5), ("w", 3, 1),
    ("rp", 1), ("t0c", 6), ("w", 4, 0), ("t0c", 7), ("rp", 2), ("w", 4, 1),
)
REDUCE = (
    ("np", 0), ("np0s",), ("np", 1), ("ra", 0), ("ra", 1), ("ra", 2), ("m",), ("wt", 0), ("wt", 1), ("wt", 2),
    ("rx", 0), ("rx", 3), ("wt", 3), ("rg", 0), ("rx", 1), ("wt", 4), ("wt", 5), ("rx", 2), ("rx", 4),
    ("wt", 6), ("sy", 0), ("wt", 7), ("tf", 3), ("rg", 1, 0), ("rg", 1, 1), ("rx", 5), ("sy", 1), ("sy", 2),
    ("tf", 4), ("rx", 6), ("ba", 3), ("tf", 5), ("rx", 7), ("rg", 2, 0), ("tf", 0), ("ba", 0), ("tf", 6),
    ("tf", 1), ("tf", 2), ("bb", 3), ("rg", 2, 1), ("ba", 4), ("tf", 7), ("bb", 0), ("s0",), ("ba", 5),
    ("bc", 3), ("bb", 4), ("bc", 0), ("rg", 3, 0), ("bb", 5), ("ba", 6), ("ba", 1), ("ba", 2), ("bc", 4),
    ("bc", 5), ("bb", 6), ("rg", 3, 1), ("bb", 1), ("bb", 2), ("ba", 7), ("s1",), ("bc", 6), ("bb", 7),
    ("s2",), ("bc", 1), ("bc", 2), ("rg", 4, 1), ("bc", 7), ("rg", 4, 0),
)


def mod(value, n):
    return lax.rem(value + 2 * n, n)


def nt(a, b):
    return lax.dot_general(a, b, (((1,), (1,)), ((), ())), preferred_element_type=F32)


def tn(a, b):
    return lax.dot_general(a, b, (((0,), (0,)), ((), ())), preferred_element_type=F32)


def nn(a, b):
    return jnp.dot(a, b, preferred_element_type=F32)


class Copies:
    def __init__(self, send_sems, recv_sems):
        self.send_sems, self.recv_sems = send_sems, recv_sems
        self.names, self.groups = {}, {}

    def copy(self, name, group, src, dst, device):
        return pltpu.make_async_remote_copy(
            src_ref=src,
            dst_ref=dst,
            send_sem=self.send_sems.at[self.groups.setdefault(group, len(self.groups))],
            recv_sem=self.recv_sems.at[self.names.setdefault(name, len(self.names))],
            device_id=device,
            device_id_type=MESH,
        )

    def send(self, name, src, dst, device, group):
        self.copy(name, group, src, dst, device).start()

    def arrived(self, name, landed, device):
        group = next(iter(self.groups))
        self.copy(name, group, landed, landed, device).wait_recv()

    def drain(self, group, sent, device):
        name = next(iter(self.names))
        self.copy(name, group, sent, sent, device).wait_send()


def kernel(
    inputs, upstream, w3, wo, ids, times, table, gain,
    out, wq_sum, wo_sum, gain_out, act_out,
    in_v, up_v, embedded, xu, meta, meta_in, tok, wts, normed, up, bias, qkv, mixed, grads, probs, dscore,
    m_part, m_in, m_sum, gn, gw, part_l, part_r, sum_l, sum_r, in_l, in_r, ysend, yin, zsend,
    cin, rs_up, rs_down, ri_up, ri_down, psend, pin, full, ry, rsend, rin, small_out,
    act, gterm, small, zin, sent, sin, total,
    send_sems, recv_sems, local_sems,
):
    f = lax.axis_index("frame")
    s = lax.axis_index("space")
    t = lax.axis_index("tensor")
    yl, c, yh, x = s // 2, s % 2, t // NX, t % NX
    xl, xr, xo = mod(x - 1, NX), mod(x + 1, NX), mod(x + 2, NX)
    right, left = {"tensor": yh * NX + xr}, {"tensor": yh * NX + xl}
    other = {"tensor": (1 - yh) * NX + x}
    opposite = {"tensor": yh * NX + xo}
    z_up, z_down = {"frame": mod(f + 1, NZ)}, {"frame": mod(f - 1, NZ)}
    ypeer = {"space": (1 - yl) * 2 + c}
    cpeer = {"space": yl * 2 + 1 - c}
    frames = [{"frame": mod(f + k, NZ)} for k in range(1, NZ)]
    spaces = [{"space": mod(s + k, 4)} for k in range(1, 4)]
    tensors = [{"tensor": mod(t + k, NT)} for k in range(1, NT)]
    peers = frames + spaces + tensors
    my_cols = pl.ds(pl.multiple_of(t * SLICE, SLICE), SLICE)

    greeted = pltpu.get_barrier_semaphore()
    for peer in peers:
        pl.semaphore_signal(greeted, inc=1, device_id=peer, device_id_type=MESH)

    cp = Copies(send_sems, recv_sems)

    def w_rows(z, row, plane):
        return wts.at[pl.ds(pl.multiple_of((z * 4 + row * 2 + plane) * 64, 64), 64), :]

    def local(src, dst, n):
        copy = pltpu.make_async_copy(src, dst, local_sems.at[n])
        copy.start()
        return copy

    load_in = local(inputs, in_v, 0)
    load_up = local(upstream.at[:, :, my_cols], up_v, 1)
    own_rows = pl.ds(pl.multiple_of((f * 4 + s) * 64, 64), 64)
    load_w = [
        local(w3.at[n], wts.at[own_rows, n * 256 : (n + 1) * 256], 2 + n) for n in range(3)
    ] + [local(wo, wts.at[own_rows, 768:1024], 5)]

    def source(p):
        return mod(f - ORDER[p], NZ)

    def target(p):
        return mod(f + ORDER[p], NZ)

    spot = lax.broadcasted_iota(jnp.int32, (ROWS, 128), 0)
    lane = lax.broadcasted_iota(jnp.int32, (8, TOKENS), 1)
    columns = []
    time_row = jnp.zeros((8, TOKENS), jnp.int32)
    for p in range(NZ):
        pair = [times[f // 4, 2 * source(p) + fr] for fr in range(2)]
        second = spot >= SITES
        columns.append(jnp.where(second, pair[1] + 64 * (spot - SITES), pair[0] + 64 * spot))
        for fr in range(2):
            start = p * ROWS + fr * SITES
            time_row = jnp.where((lane >= start) & (lane < start + SITES), pair[fr], time_row)
    site_row = lax.rem(lane, SITES)
    code_col = jnp.concatenate(columns, 0)[:, 0:1]
    code_row = (time_row + 64 * site_row)[0:1, :]
    apart = code_col - code_row
    bias[...] = jnp.where((apart >= 0) & (apart <= 15), 0.0, -1e30)

    names = lax.broadcasted_iota(jnp.int32, (8, WIDTH), 0)
    for i in range(4):
        embedded[i : i + 1] = jnp.sum(
            jnp.where(names == ids[i // 2, i % 2], table[...], 0.0), 0, keepdims=True
        )
    load_in.wait()

    lane = lax.broadcasted_iota(jnp.int32, (ROWS, 128), 1)
    eye = (lane == lax.broadcasted_iota(jnp.int32, (ROWS, 128), 0)).astype(F32)

    def to_row(column):
        return jnp.sum(eye * column, 0, keepdims=True)

    def to_column(row):
        return jnp.sum(eye * row, 1, keepdims=True)

    gain_t = gain[0:1, my_cols]
    gain_inv = 1.0 / gain_t
    pieces, inverses = [], []
    for i in range(4):
        squares = jnp.zeros((144, SLICE), F32)
        for n in range(NT):
            cols = slice(n * SLICE, (n + 1) * SLICE)
            hidden = in_v[i, :, cols].astype(F32) + embedded[i : i + 1, cols]
            squares = squares + hidden * hidden
        inverse = lax.rsqrt(jnp.sum(squares, -1, keepdims=True) * (1.0 / WIDTH) + NORM_EPSILON)
        hidden = in_v[i, :, my_cols].astype(F32) + embedded[i : i + 1, my_cols]
        pieces.append(hidden * inverse * gain_t)
        inverses.append(jnp.broadcast_to(inverse, (144, 128)))
    load_up.wait()
    for b in range(2):
        for r in range(4):
            rows = slice(r * SITES, (r + 1) * SITES)

            def chunk(a):
                return jnp.concatenate([a[2 * b][rows], a[2 * b + 1][rows]], 0)

            xu[b * 4 + r, 0] = chunk(pieces).astype(BF16)
            xu[b * 4 + r, 1] = jnp.concatenate(
                [up_v[2 * b].astype(F32)[rows], up_v[2 * b + 1].astype(F32)[rows]], 0
            ).astype(BF16)
            meta[b * 4 + r] = jnp.concatenate(
                [to_row(chunk(inverses))]
                + [jnp.full((1, 128), ids[b, fr].astype(F32), F32) for fr in range(2)]
                + [jnp.zeros((5, 128), F32)],
                0,
            )

    pl.semaphore_wait(greeted, len(peers))

    def tokens_send():
        for p in range(1, NZ):
            j = target(p)
            cp.send(("z", p), xu.at[j], tok.at[yh, x, f], {"frame": j}, "z")
            cp.send("meta", meta.at[j], meta_in.at[f], {"frame": j}, "meta")
        local(xu.at[f], tok.at[yh, x, f], 0).wait()
        meta_in[f] = meta[f]

    def normed_a(p):
        j = source(p)
        if p > 0:
            cp.arrived(("z", p), tok.at[yh, x, j], other)
        mine = tok.at[yh, x, j, 0]
        cp.send(("t0y", p), mine, mine, other, "t")
        cp.send(("t0x", p), mine, mine, right, "t")
        cp.send(("last", p // 2), mine, mine, left, "t")

    def normed_b(p):
        theirs = tok.at[1 - yh, x, source(p), 0]
        cp.arrived(("t0y", p), theirs, other)
        cp.send(("last", p // 2), theirs, theirs, right, "t")
        cp.send(("t0x", p), theirs, theirs, left, "t")

    def normed_c(p):
        j = source(p)
        cp.arrived(("t0x", p), tok.at[0, 0, 0], left)
        block = tok.at[yh, xl, j, 0]
        cp.send(("last", p // 2), block, block, right, "t")
        block = tok.at[1 - yh, xr, j, 0]
        cp.send(("last", p // 2), block, block, left, "t")

    def upstream_a(p):
        mine = tok.at[yh, x, source(p), 1]
        cp.send(("t1x", p), mine, mine, right, "t")
        cp.send(("t1x", p), mine, mine, left, "t")
        cp.send(("last", p // 2), mine, mine, other, "t")
        cp.send(("t1o", p), mine, mine, opposite, "t")

    def upstream_b(p):
        j = source(p)
        cp.arrived(("t1x", p), tok.at[0, 0, 0], left)
        for column in (xl, xr):
            block = tok.at[yh, column, j, 1]
            cp.send(("last", p // 2), block, block, other, "t")

    def upstream_c(p):
        block = tok.at[yh, xo, source(p), 1]
        cp.arrived(("t1o", p), block, opposite)
        cp.send(("last", p // 2), block, block, other, "t")

    def repack(pair):
        cp.arrived(("last", pair), tok.at[:, :, 0:1], other)
        rows = slice(pair * 2 * ROWS, (pair + 1) * 2 * ROWS)
        for n in range(NT):
            cols = slice(n * SLICE, (n + 1) * SLICE)
            for arr, dst in ((0, normed), (1, up)):
                dst[rows, cols] = jnp.concatenate(
                    [
                        tok[n // NX, n % NX, source(p), arr].astype(F32)
                        for p in (2 * pair, 2 * pair + 1)
                    ],
                    0,
                ).astype(BF16)

    def weights(step, o):
        row = yl if o == 0 else 1 - yl
        if step == 0:
            block = w_rows(f, row, c)
            if o == 0:
                for copy in load_w:
                    copy.wait()
                cp.send("wy", block, block, ypeer, "w")
            else:
                cp.arrived("wy", block, ypeer)
            cp.send(("wu", 0, o), block, block, z_up, "w")
            cp.send(("wd", 0, o), block, block, z_down, "w")
            cp.send("wc", block, block, cpeer, "w")
        elif step < 4:
            block = w_rows(mod(f - step, NZ), row, c)
            cp.arrived(("wu", step - 1, o), block, z_down)
            if step < 3 or o == 0:
                cp.send(("wu", step, o), block, block, z_up, "w")
            cp.send("wc", block, block, cpeer, "w")
            block = w_rows(mod(f + step, NZ), row, c)
            cp.arrived(("wd", step - 1, o), block, z_up)
            if step < 3 or o == 1:
                cp.send(("wd", step, o), block, block, z_down, "w")
            cp.send("wc", block, block, cpeer, "w")
        else:
            block = w_rows(mod(f + 4, NZ), row, c)
            if o == 0:
                cp.arrived(("wu", 3, o), block, z_down)
            else:
                cp.arrived(("wd", 3, o), block, z_up)
            cp.send("wc", block, block, cpeer, "w")

    actions = {
        "w": weights, "zsend": tokens_send, "t0a": normed_a, "t0b": normed_b, "t0c": normed_c,
        "t1a": upstream_a, "t1b": upstream_b, "t1c": upstream_c, "rp": repack,
    }
    for name, *where in GATHER:
        actions[name](*where)
    repack(3)
    cp.arrived("wc", wts.at[0:1024], cpeer)

    @pl.loop(0, 3)
    def _(n):
        at = pl.ds(pl.multiple_of(n * 256, 256), 256)
        qkv[:, at] = nn(normed[...], wts[:, at]).astype(BF16)

    qkv[:, 768:1024] = nn(up[...], wts[:, 768:1024]).astype(BF16)

    scale = 1.0 / math.sqrt(HEAD)
    half = TOKENS // 2
    for h in range(2):
        q, k, v, g = (qkv[:, n * 256 + h * HEAD : n * 256 + (h + 1) * HEAD] for n in range(4))
        for part in range(2):
            rows = slice(part * half, (part + 1) * half)
            scores = nt(q[rows], k) * scale + bias[rows]
            exponent = jnp.exp(scores - jnp.max(scores, -1, keepdims=True))
            prob = exponent / jnp.sum(exponent, -1, keepdims=True)
            probs[rows] = prob.astype(BF16)
            grad_prob = nt(g[rows], v)
            grad_score = prob * (grad_prob - jnp.sum(grad_prob * prob, -1, keepdims=True))
            dscore[rows] = grad_score.astype(BF16)
        pb, db = probs[...], dscore[...]
        mixed[:, h * HEAD : (h + 1) * HEAD] = nn(pb, v).astype(BF16)
        grads[:, h * HEAD : (h + 1) * HEAD] = (nn(db, k) * scale).astype(BF16)
        grads[:, 256 + h * HEAD : 256 + (h + 1) * HEAD] = (tn(db, q) * scale).astype(BF16)
        grads[:, 512 + h * HEAD : 512 + (h + 1) * HEAD] = tn(pb, g).astype(BF16)

    def norm_part(plane, column):
        feature = pl.ds(pl.multiple_of((plane * NX + column) * SLICE, SLICE), SLICE)
        term = nt(grads[...], wts[feature, 0:768])
        for p in range(NZ):
            gn[plane, column, source(p)] = term[p * ROWS : (p + 1) * ROWS].astype(BF16)

    def norm_parts(which):
        plane = 1 - yh if which == 0 else yh
        for column in range(NX):
            norm_part(plane, column)

    def send_across():
        for p in ACROSS:
            cp.send(("ry", p), gn.at[1 - yh, :, target(p)], ry.at[p], other, "ry")

    def reduce_a(p):
        j = target(p)
        cp.send(("a", p), gn.at[1 - yh, xo, j], part_l.at[p], right, "r")
        cp.send(("b", p), gn.at[yh, xo, j], part_r.at[p], left, "r")
        cp.send(("in", p), gn.at[yh, xr, j], in_l.at[p, 0], right, "r")
        cp.send(("in", p), gn.at[1 - yh, xl, j], in_r.at[p, 1], left, "r")

    def reduce_x(p):
        j = target(p)
        if p in ACROSS:
            cp.arrived(("ry", p), ry.at[p], other)
            for i, (column, device) in enumerate(((xr, right), (xl, left), (xo, opposite))):
                rsend[p, i] = (
                    gn[yh, column, j].astype(F32) + ry[p, column].astype(F32)
                ).astype(BF16)
                cp.send(("rx", p), rsend.at[p, i], rin.at[p, i], device, "rx")
            return
        cp.arrived(("a", p), part_l.at[p], left)
        sum_r[p] = (gn[1 - yh, xr, j].astype(F32) + part_l[p].astype(F32)).astype(BF16)
        cp.send(("in", p), sum_r.at[p], in_l.at[p, 1], right, "r")
        cp.arrived(("b", p), part_r.at[p], right)
        sum_l[p] = (gn[yh, xl, j].astype(F32) + part_r[p].astype(F32)).astype(BF16)
        cp.send(("in", p), sum_l.at[p], in_r.at[p, 0], left, "r")

    def send_means():
        product = jnp.zeros((TOKENS, 128), F32)
        for n in range(6):
            cols = slice(n * 128, (n + 1) * 128)
            product = product + grads[:, cols].astype(F32) * qkv[:, cols].astype(F32)
        column = jnp.broadcast_to(jnp.sum(product, -1, keepdims=True), (TOKENS, 128))
        for p in range(NZ):
            m_part[pl.ds(source(p), 1), :] = to_row(column[p * ROWS : (p + 1) * ROWS])
        m_in[t] = m_part[...]
        for k, peer in enumerate(tensors):
            cp.send("m", m_part, m_in.at[t], peer, "m")

    def take_means():
        cp.arrived("meta", meta_in.at[0:7], other)
        cp.arrived("m", m_in.at[0:7], other)
        row_sum = m_in[0]
        for k in range(1, NT):
            row_sum = row_sum + m_in[k]
        m_sum[...] = row_sum * (1.0 / WIDTH)
        act[...] = jnp.zeros((8, SLICE), F32)
        gterm[...] = jnp.zeros((8, SLICE), F32)

    blocks = [mod(f + k, NZ) for k in (4, 3, -3, 2, -2, 1, -1, 0)]
    shared = set()

    def weight_terms(i):
        n = blocks[i]
        cols = pl.ds(pl.multiple_of(n * SLICE, SLICE), SLICE)
        term = tn(normed[:, cols], grads[...]).astype(BF16)
        term_out = tn(up[:, cols], mixed[...]).astype(BF16)
        for r in range(4):
            gw[n, r // 2, r % 2, :, 0:768] = term[64 * r : 64 * r + 64]
            gw[n, r // 2, r % 2, :, 768:1024] = term_out[64 * r : 64 * r + 64]
        cp.send(("core", i), gw.at[n, :, 1 - c], cin.at[n], cpeer, "core")

    def partner_terms(*which):
        for i in which:
            if i not in shared:
                shared.add(i)
                cp.arrived(("core", i), cin.at[blocks[i]], cpeer)

    def sum_y(p):
        j = target(p)
        cp.arrived(("in", p), ry.at[0], left)
        theirs = (
            gn[1 - yh, x, j].astype(F32) + in_l[p, 1].astype(F32) + in_r[p, 1].astype(F32)
        )
        ysend[p] = theirs.astype(BF16)
        cp.send(("sy", p), ysend.at[p], yin.at[p], other, "r")

    def to_frames(p):
        j = target(p)
        if not shared.issuperset(("mean",)):
            shared.add("mean")
            take_means()
        grad_norm = gn[yh, x, j].astype(F32)
        if p in ACROSS:
            cp.arrived(("rx", p), rin.at[p], left)
            for i in range(3):
                grad_norm = grad_norm + rin[p, i].astype(F32)
            grad_norm = grad_norm + ry[p, x].astype(F32)
        else:
            cp.arrived(("sy", p), yin.at[p], other)
            grad_norm = (
                grad_norm
                + in_l[p, 0].astype(F32)
                + in_r[p, 0].astype(F32)
                + yin[p].astype(F32)
            )
        rows = tok[yh, x, j, 0].astype(F32)
        inverse = to_column(meta_in[j, 0:1, :])
        mean = to_column(m_sum[pl.ds(j, 1), :])
        grad_hidden = tok[yh, x, j, 1].astype(F32) + inverse * (
            gain_t * grad_norm - rows * (gain_inv * mean)
        )
        zsend[p] = grad_hidden.astype(BF16)
        if p == 0:
            local(zsend.at[0], full.at[yh, x, f], 0).wait()
        else:
            cp.send(("bz", p), zsend.at[p], full.at[yh, x, f], {"frame": j}, "bz")
        gterm[0:1] += jnp.sum(grad_norm * rows, 0, keepdims=True)
        labels = lax.broadcasted_iota(jnp.int32, (8, SLICE), 0).astype(F32)
        for fr in range(2):
            name = jnp.concatenate([meta_in[j, 1 + fr : 2 + fr, :]] * 2, 1)
            frame_sum = jnp.sum(grad_hidden[fr * SITES : (fr + 1) * SITES], 0, keepdims=True)
            act[...] += jnp.where(labels == name, frame_sum, 0.0)

    def back_y(p):
        j = source(p)
        mine = full.at[yh, x, j]
        if p > 0:
            cp.arrived(("bz", p), mine, other)
        cp.send(("by", p), mine, mine, other, "b")
        cp.send(("bx", p), mine, mine, right, "b")
        cp.send("back", mine, mine, left, "b")

    def back_x(p):
        j = source(p)
        theirs = full.at[1 - yh, x, j]
        cp.arrived(("by", p), theirs, other)
        cp.send("back", theirs, theirs, right, "b")
        cp.send(("bx", p), theirs, theirs, left, "b")

    def back_forward(p):
        j = source(p)
        cp.arrived(("bx", p), full.at[0, 0, 0:2], left)
        block = full.at[yh, xl, j]
        cp.send("back", block, block, right, "b")
        block = full.at[1 - yh, xr, j]
        cp.send("back", block, block, left, "b")

    def term(j, o):
        row = yl if o == 0 else 1 - yl
        return gw[j, row, c].astype(F32) + cin[j, row].astype(F32)

    def ring(step, o=None):
        if step == 0:
            partner_terms(0)
            far = blocks[0]
            rs_up[0, 0] = term(far, 0).astype(BF16)
            cp.send(("ru", 0, 0), rs_up.at[0, 0], ri_up.at[0, 0], z_up, "ring")
            rs_down[0, 1] = term(far, 1).astype(BF16)
            cp.send(("rd", 0, 1), rs_down.at[0, 1], ri_down.at[0, 1], z_down, "ring")
        elif step < 4:
            partner_terms(2 * step - 1, 2 * step)
            value = term(blocks[2 * step - 1], o)
            if step > 1 or o == 0:
                cp.arrived(("ru", step - 1, o), ri_up.at[step - 1, o], z_down)
                value = value + ri_up[step - 1, o].astype(F32)
            rs_up[step, o] = value.astype(BF16)
            cp.send(("ru", step, o), rs_up.at[step, o], ri_up.at[step, o], z_up, "ring")
            value = term(blocks[2 * step], o)
            if step > 1 or o == 1:
                cp.arrived(("rd", step - 1, o), ri_down.at[step - 1, o], z_up)
                value = value + ri_down[step - 1, o].astype(F32)
            rs_down[step, o] = value.astype(BF16)
            cp.send(("rd", step, o), rs_down.at[step, o], ri_down.at[step, o], z_down, "ring")
        else:
            partner_terms(7)
            cp.arrived(("ru", 3, o), ri_up.at[3, o], z_down)
            cp.arrived(("rd", 3, o), ri_down.at[3, o], z_up)
            value = term(f, o) + ri_up[3, o].astype(F32) + ri_down[3, o].astype(F32)
            if o == 1:
                psend[...] = value.astype(BF16)
                cp.send("py", psend, pin, ypeer, "ring")
                return
            cp.arrived("py", pin, ypeer)
            value = value + pin[...].astype(F32)
            for n in range(3):
                wq_sum[n] = value[:, n * 256 : (n + 1) * 256]
            wo_sum[...] = value[:, 768:1024]

    def small_z_send():
        small[0:8] = act[...]
        small[8:16] = gterm[...] * gain_inv
        zin[f] = small[...]
        for k, peer in enumerate(frames):
            cp.send("sz", small, zin.at[f], peer, "sz")

    def small_z_recv():
        cp.arrived("sz", zin.at[0:7], other)
        acc = zin[0]
        for k in range(1, NZ):
            acc = acc + zin[k]
        sent[...] = acc
        sin[s] = acc
        for k, peer in enumerate(spaces):
            cp.send("ss", sent, sin.at[s], peer, "ss")

    def small_s_recv():
        cp.arrived("ss", sin.at[0:3], other)
        acc = sin[0]
        for k in range(1, 4):
            acc = acc + sin[k]
        total[...] = acc
        small_out[t] = acc
        for k, peer in enumerate(tensors):
            cp.send("st", total, small_out.at[t], peer, "st")

    def small_t_recv():
        cp.arrived("st", small_out.at[0:7], other)

    actions = {
        "np": norm_parts, "np0s": send_across, "ra": reduce_a, "rx": reduce_x, "m": send_means,
        "wt": weight_terms, "rg": ring, "sy": sum_y, "tf": to_frames, "ba": back_y, "bb": back_x,
        "bc": back_forward, "s0": small_z_send, "s1": small_z_recv, "s2": small_s_recv,
    }
    for name, *where in REDUCE:
        actions[name](*where)
    small_t_recv()
    for n in range(NT):
        cols = slice(n * SLICE, (n + 1) * SLICE)
        act_out[:, cols] = small_out[n, 0:8]
        gain_out[:, cols] = small_out[n, 8:9]
    cp.arrived("back", full.at[:, :, 0:4], other)

    for n in range(NT):
        cols = slice(n * SLICE, (n + 1) * SLICE)
        for b in range(2):
            blocks = [full[n // NX, n % NX, b * 4 + r].astype(F32) for r in range(4)]
            for fr in range(2):
                rows = slice(fr * SITES, (fr + 1) * SITES)
                out[2 * b + fr, :, cols] = jnp.concatenate(
                    [block[rows] for block in blocks], 0
                ).astype(BF16)
    first = len(ACROSS)
    sent = {
        "w": wts.at[0:1984], "z": xu.at[0:7], "meta": meta.at[0:7], "t": tok.at[:, :, 0:7],
        "r": rin.at[0:7], "rx": rin.at[0:first], "ry": ry.at[0:first],
        "bz": zsend.at[0:7], "b": full.at[:, :, 0:7], "core": cin, "ring": wts.at[0:960],
        "m": m_in.at[0:7], "sz": zin.at[0:7], "ss": sin.at[0:3], "st": small_out.at[0:7],
    }
    for group in cp.groups:
        cp.drain(group, sent[group], other)


def finish_kernel(*refs):
    arrays, outs, held, sems = refs[:5], refs[5:10], refs[10:15], refs[15]
    parts = [(n, (slice(None),)) for n in range(1, 5)] + [(0, (n,)) for n in range(4)]
    taken = [
        pltpu.make_async_copy(arrays[n].at[at], held[n].at[at], sems.at[0, i])
        for i, (n, at) in enumerate(parts)
    ]
    given = [
        pltpu.make_async_copy(held[n].at[at], outs[n].at[at], sems.at[1, i])
        for i, (n, at) in enumerate(parts)
    ]
    for copy in taken:
        copy.start()
    for first, second in zip(taken, given):
        first.wait()
        second.start()
    for copy in given:
        copy.wait()


def on_device(inputs, upstream, action_ids, frame_time, action_table, gain, w_qkv, w_out):
    vmem = pl.BlockSpec(memory_space=pltpu.VMEM)
    hbm = pl.BlockSpec(memory_space=pl.ANY)
    smem = pl.BlockSpec(memory_space=pltpu.SMEM)
    chunk = (ROWS, SLICE)
    ring_shape = (4, 2, 64, 1024)
    scratch = [
        ((4, 144, WIDTH), BF16),
        ((4, 144, SLICE), BF16),
        ((4, WIDTH), F32),
        ((NZ, 2) + chunk, BF16),
        ((NZ, 8, 128), F32),
        ((NZ, 8, 128), F32),
        ((2, NX, NZ, 2) + chunk, BF16),
        ((WIDTH, 1024), BF16),
        ((TOKENS, WIDTH), BF16),
        ((TOKENS, WIDTH), BF16),
        ((TOKENS, TOKENS), F32),
        ((TOKENS, 1024), BF16),
        ((TOKENS, 256), BF16),
        ((TOKENS, 768), BF16),
        ((TOKENS, TOKENS), BF16),
        ((TOKENS, TOKENS), BF16),
        ((NZ, 128), F32),
        ((NT, NZ, 128), F32),
        ((NZ, 128), F32),
        ((2, NX, NZ) + chunk, BF16),
        ((NZ, 2, 2, 64, 1024), BF16),
        ((NZ,) + chunk, BF16),
        ((NZ,) + chunk, BF16),
        ((NZ,) + chunk, BF16),
        ((NZ,) + chunk, BF16),
        ((NZ, 2) + chunk, BF16),
        ((NZ, 2) + chunk, BF16),
        ((NZ,) + chunk, BF16),
        ((NZ,) + chunk, BF16),
        ((NZ,) + chunk, BF16),
        ((NZ, 2, 64, 1024), BF16),
        (ring_shape, BF16),
        (ring_shape, BF16),
        (ring_shape, BF16),
        (ring_shape, BF16),
        ((64, 1024), BF16),
        ((64, 1024), BF16),
        ((2, NX, NZ) + chunk, BF16),
        ((NZ, NX) + chunk, BF16),
        ((NZ, 3) + chunk, BF16),
        ((NZ, 3) + chunk, BF16),
        ((NT, 16, SLICE), F32),
        ((8, SLICE), F32),
        ((8, SLICE), F32),
        ((16, SLICE), F32),
        ((NZ, 16, SLICE), F32),
        ((16, SLICE), F32),
        ((4, 16, SLICE), F32),
        ((16, SLICE), F32),
    ]
    results = pl.pallas_call(
        kernel,
        out_shape=(
            jax.ShapeDtypeStruct((4, 144, WIDTH), BF16),
            jax.ShapeDtypeStruct((3, 64, 256), F32),
            jax.ShapeDtypeStruct((64, 256), F32),
            jax.ShapeDtypeStruct((1, WIDTH), F32),
            jax.ShapeDtypeStruct((8, WIDTH), F32),
        ),
        in_specs=[hbm] * 4 + [smem] * 2 + [vmem] * 2,
        out_specs=(vmem,) * 5,
        scratch_shapes=[pltpu.VMEM(shape, kind) for shape, kind in scratch]
        + [
            pltpu.SemaphoreType.DMA((SENT,)),
            pltpu.SemaphoreType.DMA((RECEIVED,)),
            pltpu.SemaphoreType.DMA((6,)),
        ],
        compiler_params=pltpu.CompilerParams(
            collective_id=0, has_side_effects=True, vmem_limit_bytes=VMEM_BYTES
        ),
    )(
        inputs.reshape(4, 144, WIDTH),
        upstream.reshape(4, 144, WIDTH),
        w_qkv.transpose(1, 0, 2),
        w_out,
        action_ids,
        frame_time,
        action_table,
        gain.reshape(1, WIDTH),
    )
    grad_inputs, wq_sum, wo_sum, grad_gain, grad_actions = pl.pallas_call(
        finish_kernel,
        out_shape=tuple(jax.ShapeDtypeStruct(a.shape, a.dtype) for a in results),
        in_specs=[hbm] * 5,
        out_specs=(hbm,) * 5,
        scratch_shapes=[pltpu.VMEM(a.shape, a.dtype) for a in results]
        + [pltpu.SemaphoreType.DMA((2, 8))],
        compiler_params=pltpu.CompilerParams(vmem_limit_bytes=VMEM_BYTES),
    )(*results)
    return (
        grad_inputs.reshape(inputs.shape),
        wq_sum.transpose(1, 0, 2),
        wo_sum,
        grad_gain.reshape(WIDTH),
        grad_actions,
    )


def solution(mesh):
    return jax.shard_map(
        on_device,
        mesh=mesh,
        in_specs=(
            P(None, "frame", "space", None),
            P(None, "frame", "space", None),
            P(None, "frame"),
            P(),
            P(),
            P(),
            P(("frame", "space"), None, "tensor"),
            P(("frame", "space"), "tensor"),
        ),
        out_specs=(
            P(None, "frame", "space", None),
            P(("frame", "space"), None, "tensor"),
            P(("frame", "space"), "tensor"),
            P(),
            P(),
        ),
        check_vma=False,
    )
```

```python
import math

import jax
import jax.numpy as jnp
from jax import lax
from jax.experimental import pallas as pl
from jax.experimental.pallas import tpu as pltpu
from jax.sharding import PartitionSpec as P

HEAD = 128
NORM_EPSILON = 1e-06
MESH = pl.DeviceIdType.MESH
BF16 = jnp.bfloat16
F32 = jnp.float32

NZ, NX, NT = 8, 4, 8
SITES = 36
ROWS = 72
TOKENS = NZ * ROWS
SLICE = 256
WIDTH = 2048
VMEM_BYTES = 58 * 1024 * 1024
ORDER = (0, 1, 7, 2, 6, 3, 5, 4)
RECEIVED, SENT = 144, 15
BACK = (0, 1, 7, 2, 6, 3, 5, 4)
ACROSS = (1, 3, 5, 7)
GATHER = (
    ("zsend",), ("w", 0, 0), ("t0a", 0), ("t1a", 0), ("t0a", 1), ("t1a", 1), ("t0a", 2), ("t1a", 2),
    ("t1b", 0), ("t1c", 0), ("w", 0, 1), ("t0b", 0), ("t0a", 3), ("t1a", 3), ("t0a", 4), ("t1a", 4),
    ("t1b", 1), ("t0b", 1), ("t1c", 1), ("t0b", 2), ("t1b", 2), ("t1c", 2), ("t0c", 0), ("t0a", 5),
    ("t1a", 5), ("t0a", 6), ("t1a", 6), ("t1b", 3), ("t0b", 3), ("t1c", 3), ("t0b", 4), ("t0a", 7),
    ("t1a", 7), ("t1b", 4), ("t1c", 4), ("t0c", 1), ("w", 1, 0), ("t0c", 2), ("t1b", 5), ("w", 1, 1),
    ("t1c", 5), ("t0b", 5), ("t1b", 6), ("t0b", 6), ("t1c", 6), ("w", 2, 0), ("t0c", 3), ("t0c", 4),
    ("w", 2, 1), ("t1b", 7), ("t0b", 7), ("t1c", 7), ("rp", 0), ("w", 3, 0), ("t0c", 5), ("t0c", 6),
    ("rp", 1), ("w", 3, 1), ("t0c", 7), ("rp", 2), ("w", 4, 0), ("w", 4, 1),
)
REDUCE = (
    ("np", 0), ("np0s",), ("wt", 0), ("np", 1), ("ra", 0), ("ra", 2), ("ra", 4), ("ra", 6), ("wt", 1),
    ("wt", 2), ("wt", 3), ("rg", 0), ("wt", 4), ("wt", 5), ("rx", 0), ("wt", 6), ("rx", 1), ("wt", 7), ("m",),
    ("rx", 2), ("rx", 4), ("rx", 3), ("rg", 1, 0), ("rg", 1, 1), ("rx", 6), ("sy", 0), ("rx", 5), ("tf", 1),
    ("sy", 2), ("rg", 2, 0), ("sy", 4), ("rx", 7), ("tf", 0), ("ba", 0), ("tf", 3), ("tf", 2), ("rg", 2, 1),
    ("sy", 6), ("tf", 4), ("ba", 1), ("tf", 5), ("bb", 0), ("tf", 7), ("tf", 6), ("rg", 3, 0), ("bb", 1),
    ("ba", 2), ("s0",), ("bc", 0), ("ba", 3), ("bc", 1), ("bb", 2), ("rg", 3, 1), ("ba", 4), ("bb", 3),
    ("bc", 2), ("ba", 5), ("bb", 4), ("bc", 3), ("ba", 6), ("ba", 7), ("bb", 5), ("s1",), ("bc", 4),
    ("bb", 6), ("bb", 7), ("rg", 4, 1), ("s2",), ("bc", 5), ("bc", 6), ("bc", 7), ("rg", 4, 0),
)


def mod(value, n):
    return lax.rem(value + 2 * n, n)


def nt(a, b):
    return lax.dot_general(a, b, (((1,), (1,)), ((), ())), preferred_element_type=F32)


def tn(a, b):
    return lax.dot_general(a, b, (((0,), (0,)), ((), ())), preferred_element_type=F32)


def nn(a, b):
    return jnp.dot(a, b, preferred_element_type=F32)


class Copies:
    def __init__(self, send_sems, recv_sems):
        self.send_sems, self.recv_sems = send_sems, recv_sems
        self.names, self.groups = {}, {}

    def copy(self, name, group, src, dst, device):
        return pltpu.make_async_remote_copy(
            src_ref=src,
            dst_ref=dst,
            send_sem=self.send_sems.at[self.groups.setdefault(group, len(self.groups))],
            recv_sem=self.recv_sems.at[self.names.setdefault(name, len(self.names))],
            device_id=device,
            device_id_type=MESH,
        )

    def send(self, name, src, dst, device, group):
        self.copy(name, group, src, dst, device).start()

    def arrived(self, name, landed, device):
        group = next(iter(self.groups))
        self.copy(name, group, landed, landed, device).wait_recv()

    def drain(self, group, sent, device):
        name = next(iter(self.names))
        self.copy(name, group, sent, sent, device).wait_send()


def kernel(
    inputs, upstream, w3, wo, ids, times, table, gain,
    out, wq_sum, wo_sum, gain_out, act_out,
    in_v, up_v, embedded, xu, meta, meta_in, tok, wts, normed, up, bias, qkv, mixed, grads, probs, dscore,
    m_part, m_in, m_sum, gn, gw, part_l, part_r, sum_l, sum_r, in_l, in_r, ysend, yin, zsend,
    cin, rs_up, rs_down, ri_up, ri_down, psend, pin, full, ry, rsend, rin, small_out,
    act, gterm, small, zin, sent, sin, total,
    send_sems, recv_sems, local_sems,
):
    f = lax.axis_index("frame")
    s = lax.axis_index("space")
    t = lax.axis_index("tensor")
    yl, c, yh, x = s // 2, s % 2, t // NX, t % NX
    xl, xr, xo = mod(x - 1, NX), mod(x + 1, NX), mod(x + 2, NX)
    right, left = {"tensor": yh * NX + xr}, {"tensor": yh * NX + xl}
    other = {"tensor": (1 - yh) * NX + x}
    opposite = {"tensor": yh * NX + xo}
    z_up, z_down = {"frame": mod(f + 1, NZ)}, {"frame": mod(f - 1, NZ)}
    ypeer = {"space": (1 - yl) * 2 + c}
    cpeer = {"space": yl * 2 + 1 - c}
    frames = [{"frame": mod(f + k, NZ)} for k in range(1, NZ)]
    spaces = [{"space": mod(s + k, 4)} for k in range(1, 4)]
    tensors = [{"tensor": mod(t + k, NT)} for k in range(1, NT)]
    peers = frames + spaces + tensors
    my_cols = pl.ds(pl.multiple_of(t * SLICE, SLICE), SLICE)

    greeted = pltpu.get_barrier_semaphore()
    for peer in peers:
        pl.semaphore_signal(greeted, inc=1, device_id=peer, device_id_type=MESH)

    cp = Copies(send_sems, recv_sems)

    def w_rows(z, row, plane):
        return wts.at[pl.ds(pl.multiple_of((z * 4 + row * 2 + plane) * 64, 64), 64), :]

    def local(src, dst, n):
        copy = pltpu.make_async_copy(src, dst, local_sems.at[n])
        copy.start()
        return copy

    load_in = local(inputs, in_v, 0)
    load_up = local(upstream.at[:, :, my_cols], up_v, 1)
    own_rows = pl.ds(pl.multiple_of((f * 4 + s) * 64, 64), 64)
    load_w = [
        local(w3.at[n], wts.at[own_rows, n * 256 : (n + 1) * 256], 2 + n) for n in range(3)
    ] + [local(wo, wts.at[own_rows, 768:1024], 5)]

    def source(p):
        return mod(f - ORDER[p], NZ)

    def target(p):
        return mod(f + ORDER[p], NZ)

    spot = lax.broadcasted_iota(jnp.int32, (ROWS, 128), 0)
    lane = lax.broadcasted_iota(jnp.int32, (8, TOKENS), 1)
    columns = []
    time_row = jnp.zeros((8, TOKENS), jnp.int32)
    for p in range(NZ):
        pair = [times[f // 4, 2 * source(p) + fr] for fr in range(2)]
        second = spot >= SITES
        columns.append(jnp.where(second, pair[1] + 64 * (spot - SITES), pair[0] + 64 * spot))
        for fr in range(2):
            start = p * ROWS + fr * SITES
            time_row = jnp.where((lane >= start) & (lane < start + SITES), pair[fr], time_row)
    site_row = lax.rem(lane, SITES)
    code_col = jnp.concatenate(columns, 0)[:, 0:1]
    code_row = (time_row + 64 * site_row)[0:1, :]
    apart = code_col - code_row
    bias[...] = jnp.where((apart >= 0) & (apart <= 15), 0.0, -1e30)

    names = lax.broadcasted_iota(jnp.int32, (8, WIDTH), 0)
    for i in range(4):
        embedded[i : i + 1] = jnp.sum(
            jnp.where(names == ids[i // 2, i % 2], table[...], 0.0), 0, keepdims=True
        )
    load_in.wait()

    lane = lax.broadcasted_iota(jnp.int32, (ROWS, 128), 1)
    eye = (lane == lax.broadcasted_iota(jnp.int32, (ROWS, 128), 0)).astype(F32)

    def to_row(column):
        return jnp.sum(eye * column, 0, keepdims=True)

    def to_column(row):
        return jnp.sum(eye * row, 1, keepdims=True)

    gain_t = gain[0:1, my_cols]
    gain_inv = 1.0 / gain_t
    pieces, inverses = [], []
    for i in range(4):
        squares = jnp.zeros((144, SLICE), F32)
        for n in range(NT):
            cols = slice(n * SLICE, (n + 1) * SLICE)
            hidden = in_v[i, :, cols].astype(F32) + embedded[i : i + 1, cols]
            squares = squares + hidden * hidden
        inverse = lax.rsqrt(jnp.sum(squares, -1, keepdims=True) * (1.0 / WIDTH) + NORM_EPSILON)
        hidden = in_v[i, :, my_cols].astype(F32) + embedded[i : i + 1, my_cols]
        pieces.append(hidden * inverse * gain_t)
        inverses.append(jnp.broadcast_to(inverse, (144, 128)))
    load_up.wait()
    for b in range(2):
        for r in range(4):
            rows = slice(r * SITES, (r + 1) * SITES)

            def chunk(a):
                return jnp.concatenate([a[2 * b][rows], a[2 * b + 1][rows]], 0)

            xu[b * 4 + r, 0] = chunk(pieces).astype(BF16)
            xu[b * 4 + r, 1] = jnp.concatenate(
                [up_v[2 * b].astype(F32)[rows], up_v[2 * b + 1].astype(F32)[rows]], 0
            ).astype(BF16)
            meta[b * 4 + r] = jnp.concatenate(
                [to_row(chunk(inverses))]
                + [jnp.full((1, 128), ids[b, fr].astype(F32), F32) for fr in range(2)]
                + [jnp.zeros((5, 128), F32)],
                0,
            )

    pl.semaphore_wait(greeted, len(peers))

    def tokens_send():
        for p in range(1, NZ):
            j = target(p)
            cp.send(("z", p), xu.at[j], tok.at[yh, x, f], {"frame": j}, "z")
            cp.send("meta", meta.at[j], meta_in.at[f], {"frame": j}, "meta")
        local(xu.at[f], tok.at[yh, x, f], 0).wait()
        meta_in[f] = meta[f]

    def normed_a(p):
        j = source(p)
        if p > 0:
            cp.arrived(("z", p), tok.at[yh, x, j], other)
        mine = tok.at[yh, x, j, 0]
        cp.send(("t0y", p), mine, mine, other, "t")
        cp.send(("t0x", p), mine, mine, right, "t")
        cp.send(("last", p // 2), mine, mine, left, "t")

    def normed_b(p):
        theirs = tok.at[1 - yh, x, source(p), 0]
        cp.arrived(("t0y", p), theirs, other)
        cp.send(("last", p // 2), theirs, theirs, right, "t")
        cp.send(("t0x", p), theirs, theirs, left, "t")

    def normed_c(p):
        j = source(p)
        cp.arrived(("t0x", p), tok.at[0, 0, 0], left)
        block = tok.at[yh, xl, j, 0]
        cp.send(("last", p // 2), block, block, right, "t")
        block = tok.at[1 - yh, xr, j, 0]
        cp.send(("last", p // 2), block, block, left, "t")

    def upstream_a(p):
        mine = tok.at[yh, x, source(p), 1]
        cp.send(("t1x", p), mine, mine, right, "t")
        cp.send(("t1x", p), mine, mine, left, "t")
        cp.send(("last", p // 2), mine, mine, other, "t")
        cp.send(("t1o", p), mine, mine, opposite, "t")

    def upstream_b(p):
        j = source(p)
        cp.arrived(("t1x", p), tok.at[0, 0, 0], left)
        for column in (xl, xr):
            block = tok.at[yh, column, j, 1]
            cp.send(("last", p // 2), block, block, other, "t")

    def upstream_c(p):
        block = tok.at[yh, xo, source(p), 1]
        cp.arrived(("t1o", p), block, opposite)
        cp.send(("last", p // 2), block, block, other, "t")

    def repack(pair):
        cp.arrived(("last", pair), tok.at[:, :, 0:1], other)
        rows = slice(pair * 2 * ROWS, (pair + 1) * 2 * ROWS)
        for n in range(NT):
            cols = slice(n * SLICE, (n + 1) * SLICE)
            for arr, dst in ((0, normed), (1, up)):
                dst[rows, cols] = jnp.concatenate(
                    [
                        tok[n // NX, n % NX, source(p), arr].astype(F32)
                        for p in (2 * pair, 2 * pair + 1)
                    ],
                    0,
                ).astype(BF16)

    def weights(step, o):
        row = yl if o == 0 else 1 - yl
        if step == 0:
            block = w_rows(f, row, c)
            if o == 0:
                for copy in load_w:
                    copy.wait()
                cp.send("wy", block, block, ypeer, "w")
            else:
                cp.arrived("wy", block, ypeer)
            cp.send(("wu", 0, o), block, block, z_up, "w")
            cp.send(("wd", 0, o), block, block, z_down, "w")
            cp.send("wc", block, block, cpeer, "w")
        elif step < 4:
            block = w_rows(mod(f - step, NZ), row, c)
            cp.arrived(("wu", step - 1, o), block, z_down)
            if step < 3 or o == 0:
                cp.send(("wu", step, o), block, block, z_up, "w")
            cp.send("wc", block, block, cpeer, "w")
            block = w_rows(mod(f + step, NZ), row, c)
            cp.arrived(("wd", step - 1, o), block, z_up)
            if step < 3 or o == 1:
                cp.send(("wd", step, o), block, block, z_down, "w")
            cp.send("wc", block, block, cpeer, "w")
        else:
            block = w_rows(mod(f + 4, NZ), row, c)
            if o == 0:
                cp.arrived(("wu", 3, o), block, z_down)
            else:
                cp.arrived(("wd", 3, o), block, z_up)
            cp.send("wc", block, block, cpeer, "w")

    actions = {
        "w": weights, "zsend": tokens_send, "t0a": normed_a, "t0b": normed_b, "t0c": normed_c,
        "t1a": upstream_a, "t1b": upstream_b, "t1c": upstream_c, "rp": repack,
    }
    for name, *where in GATHER:
        actions[name](*where)
    cp.arrived("wc", wts.at[0:1024], cpeer)

    def project(rows):
        @pl.loop(0, 3)
        def _(n):
            at = pl.ds(pl.multiple_of(n * 256, 256), 256)
            qkv[rows, at] = nn(normed[rows], wts[:, at]).astype(BF16)

        qkv[rows, 768:1024] = nn(up[rows], wts[:, 768:1024]).astype(BF16)

    project(slice(0, 6 * ROWS))
    repack(3)
    project(slice(6 * ROWS, TOKENS))

    scale = 1.0 / math.sqrt(HEAD)
    half = TOKENS // 2
    for h in range(2):
        q, k, v, g = (qkv[:, n * 256 + h * HEAD : n * 256 + (h + 1) * HEAD] for n in range(4))
        for part in range(2):
            rows = slice(part * half, (part + 1) * half)
            scores = nt(q[rows], k) * scale + bias[rows]
            exponent = jnp.exp(scores - jnp.max(scores, -1, keepdims=True))
            prob = exponent / jnp.sum(exponent, -1, keepdims=True)
            probs[rows] = prob.astype(BF16)
            grad_prob = nt(g[rows], v)
            grad_score = prob * (grad_prob - jnp.sum(grad_prob * prob, -1, keepdims=True))
            dscore[rows] = grad_score.astype(BF16)
        pb, db = probs[...], dscore[...]
        mixed[:, h * HEAD : (h + 1) * HEAD] = nn(pb, v).astype(BF16)
        grads[:, h * HEAD : (h + 1) * HEAD] = (nn(db, k) * scale).astype(BF16)
        grads[:, 256 + h * HEAD : 256 + (h + 1) * HEAD] = (tn(db, q) * scale).astype(BF16)
        grads[:, 512 + h * HEAD : 512 + (h + 1) * HEAD] = tn(pb, g).astype(BF16)

    def norm_part(plane, column):
        feature = pl.ds(pl.multiple_of((plane * NX + column) * SLICE, SLICE), SLICE)
        term = nt(grads[...], wts[feature, 0:768])
        for p in range(NZ):
            gn[plane, column, source(p)] = term[p * ROWS : (p + 1) * ROWS].astype(BF16)

    def back_source(p):
        return mod(f - BACK[p], NZ)

    def back_target(p):
        return mod(f + BACK[p], NZ)

    def norm_parts(which):
        plane = 1 - yh if which == 0 else yh
        for column in range(NX):
            norm_part(plane, column)

    def send_across():
        for p in ACROSS:
            cp.send(("ry", p), gn.at[1 - yh, :, back_target(p)], ry.at[p], other, "ry")

    def reduce_a(p):
        j = back_target(p)
        cp.send(("a", p), gn.at[1 - yh, xo, j], part_l.at[p], right, "r")
        cp.send(("b", p), gn.at[yh, xo, j], part_r.at[p], left, "r")
        cp.send(("in", p), gn.at[yh, xr, j], in_l.at[p, 0], right, "r")
        cp.send(("in", p), gn.at[1 - yh, xl, j], in_r.at[p, 1], left, "r")

    def reduce_x(p):
        j = back_target(p)
        if p in ACROSS:
            cp.arrived(("ry", p), ry.at[p], other)
            for i, (column, device) in enumerate(((xr, right), (xl, left), (xo, opposite))):
                rsend[p, i] = (
                    gn[yh, column, j].astype(F32) + ry[p, column].astype(F32)
                ).astype(BF16)
                cp.send(("rx", p), rsend.at[p, i], rin.at[p, i], device, "rx")
            return
        cp.arrived(("a", p), part_l.at[p], left)
        sum_r[p] = (gn[1 - yh, xr, j].astype(F32) + part_l[p].astype(F32)).astype(BF16)
        cp.send(("in", p), sum_r.at[p], in_l.at[p, 1], right, "r")
        cp.arrived(("b", p), part_r.at[p], right)
        sum_l[p] = (gn[yh, xl, j].astype(F32) + part_r[p].astype(F32)).astype(BF16)
        cp.send(("in", p), sum_l.at[p], in_r.at[p, 0], left, "r")

    def send_means():
        product = jnp.zeros((TOKENS, 128), F32)
        for n in range(6):
            cols = slice(n * 128, (n + 1) * 128)
            product = product + grads[:, cols].astype(F32) * qkv[:, cols].astype(F32)
        column = jnp.broadcast_to(jnp.sum(product, -1, keepdims=True), (TOKENS, 128))
        for p in range(NZ):
            m_part[pl.ds(source(p), 1), :] = to_row(column[p * ROWS : (p + 1) * ROWS])
        m_in[t] = m_part[...]
        for k, peer in enumerate(tensors):
            cp.send("m", m_part, m_in.at[t], peer, "m")

    def take_means():
        cp.arrived("meta", meta_in.at[0:7], other)
        cp.arrived("m", m_in.at[0:7], other)
        row_sum = m_in[0]
        for k in range(1, NT):
            row_sum = row_sum + m_in[k]
        m_sum[...] = row_sum * (1.0 / WIDTH)
        act[...] = jnp.zeros((8, SLICE), F32)
        gterm[...] = jnp.zeros((8, SLICE), F32)

    blocks = [mod(f + k, NZ) for k in (4, 3, -3, 2, -2, 1, -1, 0)]
    shared = set()

    def weight_terms(i):
        n = blocks[i]
        cols = pl.ds(pl.multiple_of(n * SLICE, SLICE), SLICE)
        term = tn(normed[:, cols], grads[...]).astype(BF16)
        term_out = tn(up[:, cols], mixed[...]).astype(BF16)
        for r in range(4):
            gw[n, r // 2, r % 2, :, 0:768] = term[64 * r : 64 * r + 64]
            gw[n, r // 2, r % 2, :, 768:1024] = term_out[64 * r : 64 * r + 64]
        cp.send(("core", i), gw.at[n, :, 1 - c], cin.at[n], cpeer, "core")

    def partner_terms(*which):
        for i in which:
            if i not in shared:
                shared.add(i)
                cp.arrived(("core", i), cin.at[blocks[i]], cpeer)

    def sum_y(p):
        j = back_target(p)
        cp.arrived(("in", p), ry.at[0], left)
        theirs = (
            gn[1 - yh, x, j].astype(F32) + in_l[p, 1].astype(F32) + in_r[p, 1].astype(F32)
        )
        ysend[p] = theirs.astype(BF16)
        cp.send(("sy", p), ysend.at[p], yin.at[p], other, "r")

    def to_frames(p):
        j = back_target(p)
        if not shared.issuperset(("mean",)):
            shared.add("mean")
            take_means()
        grad_norm = gn[yh, x, j].astype(F32)
        if p in ACROSS:
            cp.arrived(("rx", p), rin.at[p], left)
            for i in range(3):
                grad_norm = grad_norm + rin[p, i].astype(F32)
            grad_norm = grad_norm + ry[p, x].astype(F32)
        else:
            cp.arrived(("sy", p), yin.at[p], other)
            grad_norm = (
                grad_norm
                + in_l[p, 0].astype(F32)
                + in_r[p, 0].astype(F32)
                + yin[p].astype(F32)
            )
        rows = tok[yh, x, j, 0].astype(F32)
        inverse = to_column(meta_in[j, 0:1, :])
        mean = to_column(m_sum[pl.ds(j, 1), :])
        grad_hidden = tok[yh, x, j, 1].astype(F32) + inverse * (
            gain_t * grad_norm - rows * (gain_inv * mean)
        )
        zsend[p] = grad_hidden.astype(BF16)
        if BACK[p] == 0:
            local(zsend.at[p], full.at[yh, x, f], 0).wait()
        else:
            cp.send(("bz", p), zsend.at[p], full.at[yh, x, f], {"frame": j}, "bz")
        gterm[0:1] += jnp.sum(grad_norm * rows, 0, keepdims=True)
        labels = lax.broadcasted_iota(jnp.int32, (8, SLICE), 0).astype(F32)
        for fr in range(2):
            name = jnp.concatenate([meta_in[j, 1 + fr : 2 + fr, :]] * 2, 1)
            frame_sum = jnp.sum(grad_hidden[fr * SITES : (fr + 1) * SITES], 0, keepdims=True)
            act[...] += jnp.where(labels == name, frame_sum, 0.0)

    def back_y(p):
        j = back_source(p)
        mine = full.at[yh, x, j]
        if BACK[p] > 0:
            cp.arrived(("bz", p), mine, other)
        cp.send(("by", p), mine, mine, other, "b")
        cp.send(("bx", p), mine, mine, right, "b")
        cp.send("back", mine, mine, left, "b")

    def back_x(p):
        j = back_source(p)
        theirs = full.at[1 - yh, x, j]
        cp.arrived(("by", p), theirs, other)
        cp.send("back", theirs, theirs, right, "b")
        cp.send(("bx", p), theirs, theirs, left, "b")

    def back_forward(p):
        j = back_source(p)
        cp.arrived(("bx", p), full.at[0, 0, 0:2], left)
        block = full.at[yh, xl, j]
        cp.send("back", block, block, right, "b")
        block = full.at[1 - yh, xr, j]
        cp.send("back", block, block, left, "b")

    def term(j, o):
        row = yl if o == 0 else 1 - yl
        return gw[j, row, c].astype(F32) + cin[j, row].astype(F32)

    def ring(step, o=None):
        if step == 0:
            partner_terms(0)
            far = blocks[0]
            rs_up[0, 0] = term(far, 0).astype(BF16)
            cp.send(("ru", 0, 0), rs_up.at[0, 0], ri_up.at[0, 0], z_up, "ring")
            rs_down[0, 1] = term(far, 1).astype(BF16)
            cp.send(("rd", 0, 1), rs_down.at[0, 1], ri_down.at[0, 1], z_down, "ring")
        elif step < 4:
            partner_terms(2 * step - 1, 2 * step)
            value = term(blocks[2 * step - 1], o)
            if step > 1 or o == 0:
                cp.arrived(("ru", step - 1, o), ri_up.at[step - 1, o], z_down)
                value = value + ri_up[step - 1, o].astype(F32)
            rs_up[step, o] = value.astype(BF16)
            cp.send(("ru", step, o), rs_up.at[step, o], ri_up.at[step, o], z_up, "ring")
            value = term(blocks[2 * step], o)
            if step > 1 or o == 1:
                cp.arrived(("rd", step - 1, o), ri_down.at[step - 1, o], z_up)
                value = value + ri_down[step - 1, o].astype(F32)
            rs_down[step, o] = value.astype(BF16)
            cp.send(("rd", step, o), rs_down.at[step, o], ri_down.at[step, o], z_down, "ring")
        else:
            partner_terms(7)
            cp.arrived(("ru", 3, o), ri_up.at[3, o], z_down)
            cp.arrived(("rd", 3, o), ri_down.at[3, o], z_up)
            value = term(f, o) + ri_up[3, o].astype(F32) + ri_down[3, o].astype(F32)
            if o == 1:
                psend[...] = value.astype(BF16)
                cp.send("py", psend, pin, ypeer, "ring")
                return
            cp.arrived("py", pin, ypeer)
            value = value + pin[...].astype(F32)
            for n in range(3):
                wq_sum[n] = value[:, n * 256 : (n + 1) * 256]
            wo_sum[...] = value[:, 768:1024]

    def small_z_send():
        small[0:8] = act[...]
        small[8:16] = gterm[...] * gain_inv
        zin[f] = small[...]
        for k, peer in enumerate(frames):
            cp.send("sz", small, zin.at[f], peer, "sz")

    def small_z_recv():
        cp.arrived("sz", zin.at[0:7], other)
        acc = zin[0]
        for k in range(1, NZ):
            acc = acc + zin[k]
        sent[...] = acc
        sin[s] = acc
        for k, peer in enumerate(spaces):
            cp.send("ss", sent, sin.at[s], peer, "ss")

    def small_s_recv():
        cp.arrived("ss", sin.at[0:3], other)
        acc = sin[0]
        for k in range(1, 4):
            acc = acc + sin[k]
        total[...] = acc
        small_out[t] = acc
        for k, peer in enumerate(tensors):
            cp.send("st", total, small_out.at[t], peer, "st")

    def small_t_recv():
        cp.arrived("st", small_out.at[0:7], other)

    actions = {
        "np": norm_parts, "np0s": send_across, "ra": reduce_a, "rx": reduce_x, "m": send_means,
        "wt": weight_terms, "rg": ring, "sy": sum_y, "tf": to_frames, "ba": back_y, "bb": back_x,
        "bc": back_forward, "s0": small_z_send, "s1": small_z_recv, "s2": small_s_recv,
    }
    for name, *where in REDUCE:
        actions[name](*where)
    small_t_recv()
    for n in range(NT):
        cols = slice(n * SLICE, (n + 1) * SLICE)
        act_out[:, cols] = small_out[n, 0:8]
        gain_out[:, cols] = small_out[n, 8:9]
    cp.arrived("back", full.at[:, :, 0:4], other)

    for n in range(NT):
        cols = slice(n * SLICE, (n + 1) * SLICE)
        for b in range(2):
            blocks = [full[n // NX, n % NX, b * 4 + r].astype(F32) for r in range(4)]
            for fr in range(2):
                rows = slice(fr * SITES, (fr + 1) * SITES)
                out[2 * b + fr, :, cols] = jnp.concatenate(
                    [block[rows] for block in blocks], 0
                ).astype(BF16)
    first = len(ACROSS)
    sent = {
        "w": wts.at[0:1984], "z": xu.at[0:7], "meta": meta.at[0:7], "t": tok.at[:, :, 0:7],
        "r": {3: rin.at[0:7], 4: ry.at[0:7], 6: full.at[:, 0:3, 0:7]}.get(NZ - first), "rx": rin.at[0:first], "ry": ry.at[0:first],
        "bz": zsend.at[0:7], "b": full.at[:, :, 0:7], "core": cin, "ring": wts.at[0:960],
        "m": m_in.at[0:7], "sz": zin.at[0:7], "ss": sin.at[0:3], "st": small_out.at[0:7],
    }
    for group in cp.groups:
        cp.drain(group, sent[group], other)


def finish_kernel(*refs):
    arrays, outs, held, sems = refs[:5], refs[5:10], refs[10:15], refs[15]
    parts = [(n, (slice(None),)) for n in range(1, 5)] + [(0, (n,)) for n in range(4)]
    taken = [
        pltpu.make_async_copy(arrays[n].at[at], held[n].at[at], sems.at[0, i])
        for i, (n, at) in enumerate(parts)
    ]
    given = [
        pltpu.make_async_copy(held[n].at[at], outs[n].at[at], sems.at[1, i])
        for i, (n, at) in enumerate(parts)
    ]
    for copy in taken:
        copy.start()
    for first, second in zip(taken, given):
        first.wait()
        second.start()
    for copy in given:
        copy.wait()


def on_device(inputs, upstream, action_ids, frame_time, action_table, gain, w_qkv, w_out):
    vmem = pl.BlockSpec(memory_space=pltpu.VMEM)
    hbm = pl.BlockSpec(memory_space=pl.ANY)
    smem = pl.BlockSpec(memory_space=pltpu.SMEM)
    chunk = (ROWS, SLICE)
    ring_shape = (4, 2, 64, 1024)
    scratch = [
        ((4, 144, WIDTH), BF16),
        ((4, 144, SLICE), BF16),
        ((4, WIDTH), F32),
        ((NZ, 2) + chunk, BF16),
        ((NZ, 8, 128), F32),
        ((NZ, 8, 128), F32),
        ((2, NX, NZ, 2) + chunk, BF16),
        ((WIDTH, 1024), BF16),
        ((TOKENS, WIDTH), BF16),
        ((TOKENS, WIDTH), BF16),
        ((TOKENS, TOKENS), F32),
        ((TOKENS, 1024), BF16),
        ((TOKENS, 256), BF16),
        ((TOKENS, 768), BF16),
        ((TOKENS, TOKENS), BF16),
        ((TOKENS, TOKENS), BF16),
        ((NZ, 128), F32),
        ((NT, NZ, 128), F32),
        ((NZ, 128), F32),
        ((2, NX, NZ) + chunk, BF16),
        ((NZ, 2, 2, 64, 1024), BF16),
        ((NZ,) + chunk, BF16),
        ((NZ,) + chunk, BF16),
        ((NZ,) + chunk, BF16),
        ((NZ,) + chunk, BF16),
        ((NZ, 2) + chunk, BF16),
        ((NZ, 2) + chunk, BF16),
        ((NZ,) + chunk, BF16),
        ((NZ,) + chunk, BF16),
        ((NZ,) + chunk, BF16),
        ((NZ, 2, 64, 1024), BF16),
        (ring_shape, BF16),
        (ring_shape, BF16),
        (ring_shape, BF16),
        (ring_shape, BF16),
        ((64, 1024), BF16),
        ((64, 1024), BF16),
        ((2, NX, NZ) + chunk, BF16),
        ((NZ, NX) + chunk, BF16),
        ((NZ, 3) + chunk, BF16),
        ((NZ, 3) + chunk, BF16),
        ((NT, 16, SLICE), F32),
        ((8, SLICE), F32),
        ((8, SLICE), F32),
        ((16, SLICE), F32),
        ((NZ, 16, SLICE), F32),
        ((16, SLICE), F32),
        ((4, 16, SLICE), F32),
        ((16, SLICE), F32),
    ]
    results = pl.pallas_call(
        kernel,
        out_shape=(
            jax.ShapeDtypeStruct((4, 144, WIDTH), BF16),
            jax.ShapeDtypeStruct((3, 64, 256), F32),
            jax.ShapeDtypeStruct((64, 256), F32),
            jax.ShapeDtypeStruct((1, WIDTH), F32),
            jax.ShapeDtypeStruct((8, WIDTH), F32),
        ),
        in_specs=[hbm] * 4 + [smem] * 2 + [vmem] * 2,
        out_specs=(vmem,) * 5,
        scratch_shapes=[pltpu.VMEM(shape, kind) for shape, kind in scratch]
        + [
            pltpu.SemaphoreType.DMA((SENT,)),
            pltpu.SemaphoreType.DMA((RECEIVED,)),
            pltpu.SemaphoreType.DMA((6,)),
        ],
        compiler_params=pltpu.CompilerParams(
            collective_id=0, has_side_effects=True, vmem_limit_bytes=VMEM_BYTES
        ),
    )(
        inputs.reshape(4, 144, WIDTH),
        upstream.reshape(4, 144, WIDTH),
        w_qkv.transpose(1, 0, 2),
        w_out,
        action_ids,
        frame_time,
        action_table,
        gain.reshape(1, WIDTH),
    )
    grad_inputs, wq_sum, wo_sum, grad_gain, grad_actions = pl.pallas_call(
        finish_kernel,
        out_shape=tuple(jax.ShapeDtypeStruct(a.shape, a.dtype) for a in results),
        in_specs=[hbm] * 5,
        out_specs=(hbm,) * 5,
        scratch_shapes=[pltpu.VMEM(a.shape, a.dtype) for a in results]
        + [pltpu.SemaphoreType.DMA((2, 8))],
        compiler_params=pltpu.CompilerParams(vmem_limit_bytes=VMEM_BYTES),
    )(*results)
    return (
        grad_inputs.reshape(inputs.shape),
        wq_sum.transpose(1, 0, 2),
        wo_sum,
        grad_gain.reshape(WIDTH),
        grad_actions,
    )


def solution(mesh):
    return jax.shard_map(
        on_device,
        mesh=mesh,
        in_specs=(
            P(None, "frame", "space", None),
            P(None, "frame", "space", None),
            P(None, "frame"),
            P(),
            P(),
            P(),
            P(("frame", "space"), None, "tensor"),
            P(("frame", "space"), "tensor"),
        ),
        out_specs=(
            P(None, "frame", "space", None),
            P(("frame", "space"), None, "tensor"),
            P(("frame", "space"), "tensor"),
            P(),
            P(),
        ),
        check_vma=False,
    )
```

```python
import math

import jax
import jax.numpy as jnp
from jax import lax
from jax.experimental import pallas as pl
from jax.experimental.pallas import tpu as pltpu
from jax.sharding import PartitionSpec as P

HEAD = 128
NORM_EPSILON = 1e-06
MESH = pl.DeviceIdType.MESH
BF16 = jnp.bfloat16
F32 = jnp.float32

NZ, NX, NT = 8, 4, 8
SITES = 36
ROWS = 72
TOKENS = NZ * ROWS
SLICE = 256
WIDTH = 2048
VMEM_BYTES = 58 * 1024 * 1024
ORDER = (0, 1, 7, 2, 6, 3, 5, 4)
RECEIVED, SENT = 144, 15
BACK = (0, 1, 7, 2, 6, 3, 5, 4)
ACROSS = (1, 3, 5, 7)
GATHER = (
    ("zsend",), ("w", 0, 0), ("t0a", 0), ("t1a", 0), ("t0a", 1), ("t1a", 1), ("t0a", 2), ("t1a", 2),
    ("t1b", 0), ("t1c", 0), ("w", 0, 1), ("t0b", 0), ("t0a", 3), ("t1a", 3), ("t0a", 4), ("t1a", 4),
    ("t1b", 1), ("t0b", 1), ("t1c", 1), ("t0b", 2), ("t1b", 2), ("t1c", 2), ("t0c", 0), ("t0a", 5),
    ("t1a", 5), ("t0a", 6), ("t1a", 6), ("t1b", 3), ("t0b", 3), ("t1c", 3), ("t0b", 4), ("t0a", 7),
    ("t1a", 7), ("t1b", 4), ("t1c", 4), ("t0c", 1), ("w", 1, 0), ("t0c", 2), ("t1b", 5), ("w", 1, 1),
    ("t1c", 5), ("t0b", 5), ("t1b", 6), ("t0b", 6), ("t1c", 6), ("w", 2, 0), ("t0c", 3), ("t0c", 4),
    ("w", 2, 1), ("t1b", 7), ("t0b", 7), ("t1c", 7), ("rp", 0), ("w", 3, 0), ("t0c", 5), ("t0c", 6),
    ("rp", 1), ("w", 3, 1), ("t0c", 7), ("rp", 2), ("w", 4, 0), ("w", 4, 1),
)
REDUCE = (
    ("np", 0), ("np0s",), ("wt", 0), ("np", 1), ("ra", 0), ("ra", 2), ("ra", 4), ("ra", 6), ("wt", 1),
    ("wt", 2), ("wt", 3), ("rg", 0), ("wt", 4), ("wt", 5), ("rx", 0), ("wt", 6), ("rx", 1), ("wt", 7), ("m",),
    ("rx", 2), ("rx", 4), ("rx", 3), ("rg", 1, 0), ("rg", 1, 1), ("rx", 6), ("sy", 0), ("rx", 5), ("tf", 1),
    ("sy", 2), ("rg", 2, 0), ("sy", 4), ("rx", 7), ("tf", 0), ("ba", 0), ("tf", 3), ("tf", 2), ("rg", 2, 1),
    ("sy", 6), ("tf", 4), ("ba", 1), ("tf", 5), ("bb", 0), ("tf", 7), ("tf", 6), ("rg", 3, 0), ("bb", 1),
    ("ba", 2), ("s0",), ("bc", 0), ("ba", 3), ("bc", 1), ("bb", 2), ("rg", 3, 1), ("ba", 4), ("bb", 3),
    ("bc", 2), ("ba", 5), ("bb", 4), ("bc", 3), ("ba", 6), ("ba", 7), ("bb", 5), ("s1",), ("bc", 4),
    ("bb", 6), ("bb", 7), ("rg", 4, 1), ("s2",), ("bc", 5), ("bc", 6), ("bc", 7), ("rg", 4, 0),
)


def mod(value, n):
    return lax.rem(value + 2 * n, n)


def nt(a, b):
    return lax.dot_general(a, b, (((1,), (1,)), ((), ())), preferred_element_type=F32)


def tn(a, b):
    return lax.dot_general(a, b, (((0,), (0,)), ((), ())), preferred_element_type=F32)


def nn(a, b):
    return jnp.dot(a, b, preferred_element_type=F32)


class Copies:
    def __init__(self, send_sems, recv_sems):
        self.send_sems, self.recv_sems = send_sems, recv_sems
        self.names, self.groups = {}, {}

    def copy(self, name, group, src, dst, device):
        return pltpu.make_async_remote_copy(
            src_ref=src,
            dst_ref=dst,
            send_sem=self.send_sems.at[self.groups.setdefault(group, len(self.groups))],
            recv_sem=self.recv_sems.at[self.names.setdefault(name, len(self.names))],
            device_id=device,
            device_id_type=MESH,
        )

    def send(self, name, src, dst, device, group):
        self.copy(name, group, src, dst, device).start()

    def arrived(self, name, landed, device):
        group = next(iter(self.groups))
        self.copy(name, group, landed, landed, device).wait_recv()

    def drain(self, group, sent, device):
        name = next(iter(self.names))
        self.copy(name, group, sent, sent, device).wait_send()


def kernel(
    inputs, upstream, w3, wo, ids, times, table, gain,
    out, wq_sum, wo_sum, gain_out, act_out,
    in_v, up_v, embedded, out_v, xu, meta, meta_in, tok, wts, normed, up, bias, qkv, mixed, grads, probs, dscore,
    m_part, m_in, m_sum, gn, gw, part_l, part_r, sum_l, sum_r, in_l, in_r, ysend, yin, zsend,
    cin, rs_up, rs_down, ri_up, ri_down, psend, pin, full, ry, rsend, rin, small_out,
    act, gterm, small, zin, sent, sin, total,
    send_sems, recv_sems, local_sems,
):
    f = lax.axis_index("frame")
    s = lax.axis_index("space")
    t = lax.axis_index("tensor")
    yl, c, yh, x = s // 2, s % 2, t // NX, t % NX
    xl, xr, xo = mod(x - 1, NX), mod(x + 1, NX), mod(x + 2, NX)
    right, left = {"tensor": yh * NX + xr}, {"tensor": yh * NX + xl}
    other = {"tensor": (1 - yh) * NX + x}
    opposite = {"tensor": yh * NX + xo}
    z_up, z_down = {"frame": mod(f + 1, NZ)}, {"frame": mod(f - 1, NZ)}
    ypeer = {"space": (1 - yl) * 2 + c}
    cpeer = {"space": yl * 2 + 1 - c}
    frames = [{"frame": mod(f + k, NZ)} for k in range(1, NZ)]
    spaces = [{"space": mod(s + k, 4)} for k in range(1, 4)]
    tensors = [{"tensor": mod(t + k, NT)} for k in range(1, NT)]
    peers = frames + spaces + tensors
    my_cols = pl.ds(pl.multiple_of(t * SLICE, SLICE), SLICE)

    greeted = pltpu.get_barrier_semaphore()
    for peer in peers:
        pl.semaphore_signal(greeted, inc=1, device_id=peer, device_id_type=MESH)

    cp = Copies(send_sems, recv_sems)

    def w_rows(z, row, plane):
        return wts.at[pl.ds(pl.multiple_of((z * 4 + row * 2 + plane) * 64, 64), 64), :]

    def local(src, dst, n):
        copy = pltpu.make_async_copy(src, dst, local_sems.at[n])
        copy.start()
        return copy

    load_in = local(inputs, in_v, 0)
    load_up = local(upstream.at[:, :, my_cols], up_v, 1)
    own_rows = pl.ds(pl.multiple_of((f * 4 + s) * 64, 64), 64)
    load_w = [
        local(w3.at[n], wts.at[own_rows, n * 256 : (n + 1) * 256], 2 + n) for n in range(3)
    ] + [local(wo, wts.at[own_rows, 768:1024], 5)]

    def source(p):
        return mod(f - ORDER[p], NZ)

    def target(p):
        return mod(f + ORDER[p], NZ)

    spot = lax.broadcasted_iota(jnp.int32, (ROWS, 128), 0)
    lane = lax.broadcasted_iota(jnp.int32, (8, TOKENS), 1)
    columns = []
    time_row = jnp.zeros((8, TOKENS), jnp.int32)
    for p in range(NZ):
        pair = [times[f // 4, 2 * source(p) + fr] for fr in range(2)]
        second = spot >= SITES
        columns.append(jnp.where(second, pair[1] + 64 * (spot - SITES), pair[0] + 64 * spot))
        for fr in range(2):
            start = p * ROWS + fr * SITES
            time_row = jnp.where((lane >= start) & (lane < start + SITES), pair[fr], time_row)
    site_row = lax.rem(lane, SITES)
    code_col = jnp.concatenate(columns, 0)[:, 0:1]
    code_row = (time_row + 64 * site_row)[0:1, :]
    apart = code_col - code_row
    bias[...] = jnp.where((apart >= 0) & (apart <= 15), 0.0, -1e30)

    names = lax.broadcasted_iota(jnp.int32, (8, WIDTH), 0)
    for i in range(4):
        embedded[i : i + 1] = jnp.sum(
            jnp.where(names == ids[i // 2, i % 2], table[...], 0.0), 0, keepdims=True
        )
    load_in.wait()

    lane = lax.broadcasted_iota(jnp.int32, (ROWS, 128), 1)
    eye = (lane == lax.broadcasted_iota(jnp.int32, (ROWS, 128), 0)).astype(F32)

    def to_row(column):
        return jnp.sum(eye * column, 0, keepdims=True)

    def to_column(row):
        return jnp.sum(eye * row, 1, keepdims=True)

    gain_t = gain[0:1, my_cols]
    gain_inv = 1.0 / gain_t
    pieces, inverses = [], []
    for i in range(4):
        squares = jnp.zeros((144, SLICE), F32)
        for n in range(NT):
            cols = slice(n * SLICE, (n + 1) * SLICE)
            hidden = in_v[i, :, cols].astype(F32) + embedded[i : i + 1, cols]
            squares = squares + hidden * hidden
        inverse = lax.rsqrt(jnp.sum(squares, -1, keepdims=True) * (1.0 / WIDTH) + NORM_EPSILON)
        hidden = in_v[i, :, my_cols].astype(F32) + embedded[i : i + 1, my_cols]
        pieces.append(hidden * inverse * gain_t)
        inverses.append(jnp.broadcast_to(inverse, (144, 128)))
    load_up.wait()
    for b in range(2):
        for r in range(4):
            rows = slice(r * SITES, (r + 1) * SITES)

            def chunk(a):
                return jnp.concatenate([a[2 * b][rows], a[2 * b + 1][rows]], 0)

            xu[b * 4 + r, 0] = chunk(pieces).astype(BF16)
            xu[b * 4 + r, 1] = jnp.concatenate(
                [up_v[2 * b].astype(F32)[rows], up_v[2 * b + 1].astype(F32)[rows]], 0
            ).astype(BF16)
            meta[b * 4 + r] = jnp.concatenate(
                [to_row(chunk(inverses))]
                + [jnp.full((1, 128), ids[b, fr].astype(F32), F32) for fr in range(2)]
                + [jnp.zeros((5, 128), F32)],
                0,
            )

    pl.semaphore_wait(greeted, len(peers))

    def tokens_send():
        for p in range(1, NZ):
            j = target(p)
            cp.send(("z", p), xu.at[j], tok.at[yh, x, f], {"frame": j}, "z")
            cp.send("meta", meta.at[j], meta_in.at[f], {"frame": j}, "meta")
        local(xu.at[f], tok.at[yh, x, f], 0).wait()
        meta_in[f] = meta[f]

    def normed_a(p):
        j = source(p)
        if p > 0:
            cp.arrived(("z", p), tok.at[yh, x, j], other)
        mine = tok.at[yh, x, j, 0]
        cp.send(("t0y", p), mine, mine, other, "t")
        cp.send(("t0x", p), mine, mine, right, "t")
        cp.send(("last", p // 2), mine, mine, left, "t")

    def normed_b(p):
        theirs = tok.at[1 - yh, x, source(p), 0]
        cp.arrived(("t0y", p), theirs, other)
        cp.send(("last", p // 2), theirs, theirs, right, "t")
        cp.send(("t0x", p), theirs, theirs, left, "t")

    def normed_c(p):
        j = source(p)
        cp.arrived(("t0x", p), tok.at[0, 0, 0], left)
        block = tok.at[yh, xl, j, 0]
        cp.send(("last", p // 2), block, block, right, "t")
        block = tok.at[1 - yh, xr, j, 0]
        cp.send(("last", p // 2), block, block, left, "t")

    def upstream_a(p):
        mine = tok.at[yh, x, source(p), 1]
        cp.send(("t1x", p), mine, mine, right, "t")
        cp.send(("t1x", p), mine, mine, left, "t")
        cp.send(("last", p // 2), mine, mine, other, "t")
        cp.send(("t1o", p), mine, mine, opposite, "t")

    def upstream_b(p):
        j = source(p)
        cp.arrived(("t1x", p), tok.at[0, 0, 0], left)
        for column in (xl, xr):
            block = tok.at[yh, column, j, 1]
            cp.send(("last", p // 2), block, block, other, "t")

    def upstream_c(p):
        block = tok.at[yh, xo, source(p), 1]
        cp.arrived(("t1o", p), block, opposite)
        cp.send(("last", p // 2), block, block, other, "t")

    def repack(pair):
        cp.arrived(("last", pair), tok.at[:, :, 0:1], other)
        rows = slice(pair * 2 * ROWS, (pair + 1) * 2 * ROWS)
        for n in range(NT):
            cols = slice(n * SLICE, (n + 1) * SLICE)
            for arr, dst in ((0, normed), (1, up)):
                dst[rows, cols] = jnp.concatenate(
                    [
                        tok[n // NX, n % NX, source(p), arr].astype(F32)
                        for p in (2 * pair, 2 * pair + 1)
                    ],
                    0,
                ).astype(BF16)

    def weights(step, o):
        row = yl if o == 0 else 1 - yl
        if step == 0:
            block = w_rows(f, row, c)
            if o == 0:
                for copy in load_w:
                    copy.wait()
                cp.send("wy", block, block, ypeer, "w")
            else:
                cp.arrived("wy", block, ypeer)
            cp.send(("wu", 0, o), block, block, z_up, "w")
            cp.send(("wd", 0, o), block, block, z_down, "w")
            cp.send("wc", block, block, cpeer, "w")
        elif step < 4:
            block = w_rows(mod(f - step, NZ), row, c)
            cp.arrived(("wu", step - 1, o), block, z_down)
            if step < 3 or o == 0:
                cp.send(("wu", step, o), block, block, z_up, "w")
            cp.send("wc", block, block, cpeer, "w")
            block = w_rows(mod(f + step, NZ), row, c)
            cp.arrived(("wd", step - 1, o), block, z_up)
            if step < 3 or o == 1:
                cp.send(("wd", step, o), block, block, z_down, "w")
            cp.send("wc", block, block, cpeer, "w")
        else:
            block = w_rows(mod(f + 4, NZ), row, c)
            if o == 0:
                cp.arrived(("wu", 3, o), block, z_down)
            else:
                cp.arrived(("wd", 3, o), block, z_up)
            cp.send("wc", block, block, cpeer, "w")

    actions = {
        "w": weights, "zsend": tokens_send, "t0a": normed_a, "t0b": normed_b, "t0c": normed_c,
        "t1a": upstream_a, "t1b": upstream_b, "t1c": upstream_c, "rp": repack,
    }
    for name, *where in GATHER:
        actions[name](*where)
    cp.arrived("wc", wts.at[0:1024], cpeer)

    def project(rows):
        @pl.loop(0, 3)
        def _(n):
            at = pl.ds(pl.multiple_of(n * 256, 256), 256)
            qkv[rows, at] = nn(normed[rows], wts[:, at]).astype(BF16)

        qkv[rows, 768:1024] = nn(up[rows], wts[:, 768:1024]).astype(BF16)

    project(slice(0, 6 * ROWS))
    repack(3)
    project(slice(6 * ROWS, TOKENS))

    scale = 1.0 / math.sqrt(HEAD)
    half = TOKENS // 2
    for h in range(2):
        q, k, v, g = (qkv[:, n * 256 + h * HEAD : n * 256 + (h + 1) * HEAD] for n in range(4))
        for part in range(2):
            rows = slice(part * half, (part + 1) * half)
            scores = nt(q[rows], k) * scale + bias[rows]
            exponent = jnp.exp(scores - jnp.max(scores, -1, keepdims=True))
            prob = exponent / jnp.sum(exponent, -1, keepdims=True)
            probs[rows] = prob.astype(BF16)
            grad_prob = nt(g[rows], v)
            grad_score = prob * (grad_prob - jnp.sum(grad_prob * prob, -1, keepdims=True))
            dscore[rows] = grad_score.astype(BF16)
        pb, db = probs[...], dscore[...]
        mixed[:, h * HEAD : (h + 1) * HEAD] = nn(pb, v).astype(BF16)
        grads[:, h * HEAD : (h + 1) * HEAD] = (nn(db, k) * scale).astype(BF16)
        grads[:, 256 + h * HEAD : 256 + (h + 1) * HEAD] = (tn(db, q) * scale).astype(BF16)
        grads[:, 512 + h * HEAD : 512 + (h + 1) * HEAD] = tn(pb, g).astype(BF16)

    def norm_part(plane, column):
        feature = pl.ds(pl.multiple_of((plane * NX + column) * SLICE, SLICE), SLICE)
        term = nt(grads[...], wts[feature, 0:768])
        for p in range(NZ):
            gn[plane, column, source(p)] = term[p * ROWS : (p + 1) * ROWS].astype(BF16)

    def back_source(p):
        return mod(f - BACK[p], NZ)

    def back_target(p):
        return mod(f + BACK[p], NZ)

    def norm_parts(which):
        plane = 1 - yh if which == 0 else yh
        for column in range(NX):
            norm_part(plane, column)

    def send_across():
        for p in ACROSS:
            cp.send(("ry", p), gn.at[1 - yh, :, back_target(p)], ry.at[p], other, "ry")

    def reduce_a(p):
        j = back_target(p)
        cp.send(("a", p), gn.at[1 - yh, xo, j], part_l.at[p], right, "r")
        cp.send(("b", p), gn.at[yh, xo, j], part_r.at[p], left, "r")
        cp.send(("in", p), gn.at[yh, xr, j], in_l.at[p, 0], right, "r")
        cp.send(("in", p), gn.at[1 - yh, xl, j], in_r.at[p, 1], left, "r")

    def reduce_x(p):
        j = back_target(p)
        if p in ACROSS:
            cp.arrived(("ry", p), ry.at[p], other)
            for i, (column, device) in enumerate(((xr, right), (xl, left), (xo, opposite))):
                rsend[p, i] = (
                    gn[yh, column, j].astype(F32) + ry[p, column].astype(F32)
                ).astype(BF16)
                cp.send(("rx", p), rsend.at[p, i], rin.at[p, i], device, "rx")
            return
        cp.arrived(("a", p), part_l.at[p], left)
        sum_r[p] = (gn[1 - yh, xr, j].astype(F32) + part_l[p].astype(F32)).astype(BF16)
        cp.send(("in", p), sum_r.at[p], in_l.at[p, 1], right, "r")
        cp.arrived(("b", p), part_r.at[p], right)
        sum_l[p] = (gn[yh, xl, j].astype(F32) + part_r[p].astype(F32)).astype(BF16)
        cp.send(("in", p), sum_l.at[p], in_r.at[p, 0], left, "r")

    def send_means():
        product = jnp.zeros((TOKENS, 128), F32)
        for n in range(6):
            cols = slice(n * 128, (n + 1) * 128)
            product = product + grads[:, cols].astype(F32) * qkv[:, cols].astype(F32)
        column = jnp.broadcast_to(jnp.sum(product, -1, keepdims=True), (TOKENS, 128))
        for p in range(NZ):
            m_part[pl.ds(source(p), 1), :] = to_row(column[p * ROWS : (p + 1) * ROWS])
        m_in[t] = m_part[...]
        for k, peer in enumerate(tensors):
            cp.send("m", m_part, m_in.at[t], peer, "m")

    def take_means():
        cp.arrived("meta", meta_in.at[0:7], other)
        cp.arrived("m", m_in.at[0:7], other)
        row_sum = m_in[0]
        for k in range(1, NT):
            row_sum = row_sum + m_in[k]
        m_sum[...] = row_sum * (1.0 / WIDTH)
        act[...] = jnp.zeros((8, SLICE), F32)
        gterm[...] = jnp.zeros((8, SLICE), F32)

    blocks = [mod(f + k, NZ) for k in (4, 3, -3, 2, -2, 1, -1, 0)]
    shared = set()

    def weight_terms(i):
        n = blocks[i]
        cols = pl.ds(pl.multiple_of(n * SLICE, SLICE), SLICE)
        term = tn(normed[:, cols], grads[...]).astype(BF16)
        term_out = tn(up[:, cols], mixed[...]).astype(BF16)
        for r in range(4):
            gw[n, r // 2, r % 2, :, 0:768] = term[64 * r : 64 * r + 64]
            gw[n, r // 2, r % 2, :, 768:1024] = term_out[64 * r : 64 * r + 64]
        cp.send(("core", i), gw.at[n, :, 1 - c], cin.at[n], cpeer, "core")

    def partner_terms(*which):
        for i in which:
            if i not in shared:
                shared.add(i)
                cp.arrived(("core", i), cin.at[blocks[i]], cpeer)

    def sum_y(p):
        j = back_target(p)
        cp.arrived(("in", p), ry.at[0], left)
        theirs = (
            gn[1 - yh, x, j].astype(F32) + in_l[p, 1].astype(F32) + in_r[p, 1].astype(F32)
        )
        ysend[p] = theirs.astype(BF16)
        cp.send(("sy", p), ysend.at[p], yin.at[p], other, "r")

    def to_frames(p):
        j = back_target(p)
        if not shared.issuperset(("mean",)):
            shared.add("mean")
            take_means()
        grad_norm = gn[yh, x, j].astype(F32)
        if p in ACROSS:
            cp.arrived(("rx", p), rin.at[p], left)
            for i in range(3):
                grad_norm = grad_norm + rin[p, i].astype(F32)
            grad_norm = grad_norm + ry[p, x].astype(F32)
        else:
            cp.arrived(("sy", p), yin.at[p], other)
            grad_norm = (
                grad_norm
                + in_l[p, 0].astype(F32)
                + in_r[p, 0].astype(F32)
                + yin[p].astype(F32)
            )
        rows = tok[yh, x, j, 0].astype(F32)
        inverse = to_column(meta_in[j, 0:1, :])
        mean = to_column(m_sum[pl.ds(j, 1), :])
        grad_hidden = tok[yh, x, j, 1].astype(F32) + inverse * (
            gain_t * grad_norm - rows * (gain_inv * mean)
        )
        zsend[p] = grad_hidden.astype(BF16)
        if BACK[p] == 0:
            local(zsend.at[p], full.at[yh, x, f], 0).wait()
        else:
            cp.send(("bz", p), zsend.at[p], full.at[yh, x, f], {"frame": j}, "bz")
        gterm[0:1] += jnp.sum(grad_norm * rows, 0, keepdims=True)
        labels = lax.broadcasted_iota(jnp.int32, (8, SLICE), 0).astype(F32)
        for fr in range(2):
            name = jnp.concatenate([meta_in[j, 1 + fr : 2 + fr, :]] * 2, 1)
            frame_sum = jnp.sum(grad_hidden[fr * SITES : (fr + 1) * SITES], 0, keepdims=True)
            act[...] += jnp.where(labels == name, frame_sum, 0.0)

    def back_y(p):
        j = back_source(p)
        mine = full.at[yh, x, j]
        if BACK[p] > 0:
            cp.arrived(("bz", p), mine, other)
        cp.send(("by", p), mine, mine, other, "b")
        cp.send(("bx", p), mine, mine, right, "b")
        cp.send("back", mine, mine, left, "b")

    def back_x(p):
        j = back_source(p)
        theirs = full.at[1 - yh, x, j]
        cp.arrived(("by", p), theirs, other)
        cp.send("back", theirs, theirs, right, "b")
        cp.send(("bx", p), theirs, theirs, left, "b")

    def back_forward(p):
        j = back_source(p)
        cp.arrived(("bx", p), full.at[0, 0, 0:2], left)
        block = full.at[yh, xl, j]
        cp.send("back", block, block, right, "b")
        block = full.at[1 - yh, xr, j]
        cp.send("back", block, block, left, "b")

    def term(j, o):
        row = yl if o == 0 else 1 - yl
        return gw[j, row, c].astype(F32) + cin[j, row].astype(F32)

    def ring(step, o=None):
        if step == 0:
            partner_terms(0)
            far = blocks[0]
            rs_up[0, 0] = term(far, 0).astype(BF16)
            cp.send(("ru", 0, 0), rs_up.at[0, 0], ri_up.at[0, 0], z_up, "ring")
            rs_down[0, 1] = term(far, 1).astype(BF16)
            cp.send(("rd", 0, 1), rs_down.at[0, 1], ri_down.at[0, 1], z_down, "ring")
        elif step < 4:
            partner_terms(2 * step - 1, 2 * step)
            value = term(blocks[2 * step - 1], o)
            if step > 1 or o == 0:
                cp.arrived(("ru", step - 1, o), ri_up.at[step - 1, o], z_down)
                value = value + ri_up[step - 1, o].astype(F32)
            rs_up[step, o] = value.astype(BF16)
            cp.send(("ru", step, o), rs_up.at[step, o], ri_up.at[step, o], z_up, "ring")
            value = term(blocks[2 * step], o)
            if step > 1 or o == 1:
                cp.arrived(("rd", step - 1, o), ri_down.at[step - 1, o], z_up)
                value = value + ri_down[step - 1, o].astype(F32)
            rs_down[step, o] = value.astype(BF16)
            cp.send(("rd", step, o), rs_down.at[step, o], ri_down.at[step, o], z_down, "ring")
        else:
            partner_terms(7)
            cp.arrived(("ru", 3, o), ri_up.at[3, o], z_down)
            cp.arrived(("rd", 3, o), ri_down.at[3, o], z_up)
            value = term(f, o) + ri_up[3, o].astype(F32) + ri_down[3, o].astype(F32)
            if o == 1:
                psend[...] = value.astype(BF16)
                cp.send("py", psend, pin, ypeer, "ring")
                return
            cp.arrived("py", pin, ypeer)
            value = value + pin[...].astype(F32)
            for n in range(3):
                wq_sum[n] = value[:, n * 256 : (n + 1) * 256]
            wo_sum[...] = value[:, 768:1024]

    def small_z_send():
        small[0:8] = act[...]
        small[8:16] = gterm[...] * gain_inv
        zin[f] = small[...]
        for k, peer in enumerate(frames):
            cp.send("sz", small, zin.at[f], peer, "sz")

    def small_z_recv():
        cp.arrived("sz", zin.at[0:7], other)
        acc = zin[0]
        for k in range(1, NZ):
            acc = acc + zin[k]
        sent[...] = acc
        sin[s] = acc
        for k, peer in enumerate(spaces):
            cp.send("ss", sent, sin.at[s], peer, "ss")

    def small_s_recv():
        cp.arrived("ss", sin.at[0:3], other)
        acc = sin[0]
        for k in range(1, 4):
            acc = acc + sin[k]
        total[...] = acc
        small_out[t] = acc
        for k, peer in enumerate(tensors):
            cp.send("st", total, small_out.at[t], peer, "st")

    def small_t_recv():
        cp.arrived("st", small_out.at[0:7], other)

    actions = {
        "np": norm_parts, "np0s": send_across, "ra": reduce_a, "rx": reduce_x, "m": send_means,
        "wt": weight_terms, "rg": ring, "sy": sum_y, "tf": to_frames, "ba": back_y, "bb": back_x,
        "bc": back_forward, "s0": small_z_send, "s1": small_z_recv, "s2": small_s_recv,
    }
    for name, *where in REDUCE:
        actions[name](*where)
    small_t_recv()
    for n in range(NT):
        cols = slice(n * SLICE, (n + 1) * SLICE)
        act_out[:, cols] = small_out[n, 0:8]
        gain_out[:, cols] = small_out[n, 8:9]
    cp.arrived("back", full.at[:, :, 0:4], other)

    written = []
    for b in range(2):
        for n in range(NT):
            cols = slice(n * SLICE, (n + 1) * SLICE)
            blocks = [full[n // NX, n % NX, b * 4 + r].astype(F32) for r in range(4)]
            for fr in range(2):
                rows = slice(fr * SITES, (fr + 1) * SITES)
                out_v[2 * b + fr, :, cols] = jnp.concatenate(
                    [block[rows] for block in blocks], 0
                ).astype(BF16)
        for fr in range(2):
            written.append(local(out_v.at[2 * b + fr], out.at[2 * b + fr], 2 * b + fr))
    first = len(ACROSS)
    sent = {
        "w": wts.at[0:1984], "z": xu.at[0:7], "meta": meta.at[0:7], "t": tok.at[:, :, 0:7],
        "r": {3: rin.at[0:7], 4: ry.at[0:7], 6: full.at[:, 0:3, 0:7]}.get(NZ - first), "rx": rin.at[0:first], "ry": ry.at[0:first],
        "bz": zsend.at[0:7], "b": full.at[:, :, 0:7], "core": cin, "ring": wts.at[0:960],
        "m": m_in.at[0:7], "sz": zin.at[0:7], "ss": sin.at[0:3], "st": small_out.at[0:7],
    }
    for group in cp.groups:
        cp.drain(group, sent[group], other)
    for copy in written:
        copy.wait()


def finish_kernel(*refs):
    arrays, outs, held, sems = refs[:5], refs[5:10], refs[10:15], refs[15]
    parts = [(n, (slice(None),)) for n in range(1, 5)] + [(0, (n,)) for n in range(4)]
    taken = [
        pltpu.make_async_copy(arrays[n].at[at], held[n].at[at], sems.at[0, i])
        for i, (n, at) in enumerate(parts)
    ]
    given = [
        pltpu.make_async_copy(held[n].at[at], outs[n].at[at], sems.at[1, i])
        for i, (n, at) in enumerate(parts)
    ]
    for copy in taken:
        copy.start()
    for first, second in zip(taken, given):
        first.wait()
        second.start()
    for copy in given:
        copy.wait()


def on_device(inputs, upstream, action_ids, frame_time, action_table, gain, w_qkv, w_out):
    vmem = pl.BlockSpec(memory_space=pltpu.VMEM)
    hbm = pl.BlockSpec(memory_space=pl.ANY)
    smem = pl.BlockSpec(memory_space=pltpu.SMEM)
    chunk = (ROWS, SLICE)
    ring_shape = (4, 2, 64, 1024)
    scratch = [
        ((4, 144, WIDTH), BF16),
        ((4, 144, SLICE), BF16),
        ((4, WIDTH), F32),
        ((4, 144, WIDTH), BF16),
        ((NZ, 2) + chunk, BF16),
        ((NZ, 8, 128), F32),
        ((NZ, 8, 128), F32),
        ((2, NX, NZ, 2) + chunk, BF16),
        ((WIDTH, 1024), BF16),
        ((TOKENS, WIDTH), BF16),
        ((TOKENS, WIDTH), BF16),
        ((TOKENS, TOKENS), F32),
        ((TOKENS, 1024), BF16),
        ((TOKENS, 256), BF16),
        ((TOKENS, 768), BF16),
        ((TOKENS, TOKENS), BF16),
        ((TOKENS, TOKENS), BF16),
        ((NZ, 128), F32),
        ((NT, NZ, 128), F32),
        ((NZ, 128), F32),
        ((2, NX, NZ) + chunk, BF16),
        ((NZ, 2, 2, 64, 1024), BF16),
        ((NZ,) + chunk, BF16),
        ((NZ,) + chunk, BF16),
        ((NZ,) + chunk, BF16),
        ((NZ,) + chunk, BF16),
        ((NZ, 2) + chunk, BF16),
        ((NZ, 2) + chunk, BF16),
        ((NZ,) + chunk, BF16),
        ((NZ,) + chunk, BF16),
        ((NZ,) + chunk, BF16),
        ((NZ, 2, 64, 1024), BF16),
        (ring_shape, BF16),
        (ring_shape, BF16),
        (ring_shape, BF16),
        (ring_shape, BF16),
        ((64, 1024), BF16),
        ((64, 1024), BF16),
        ((2, NX, NZ) + chunk, BF16),
        ((NZ, NX) + chunk, BF16),
        ((NZ, 3) + chunk, BF16),
        ((NZ, 3) + chunk, BF16),
        ((NT, 16, SLICE), F32),
        ((8, SLICE), F32),
        ((8, SLICE), F32),
        ((16, SLICE), F32),
        ((NZ, 16, SLICE), F32),
        ((16, SLICE), F32),
        ((4, 16, SLICE), F32),
        ((16, SLICE), F32),
    ]
    results = pl.pallas_call(
        kernel,
        out_shape=(
            jax.ShapeDtypeStruct((4, 144, WIDTH), BF16),
            jax.ShapeDtypeStruct((3, 64, 256), F32),
            jax.ShapeDtypeStruct((64, 256), F32),
            jax.ShapeDtypeStruct((1, WIDTH), F32),
            jax.ShapeDtypeStruct((8, WIDTH), F32),
        ),
        in_specs=[hbm] * 4 + [smem] * 2 + [vmem] * 2,
        out_specs=(hbm,) + (vmem,) * 4,
        scratch_shapes=[pltpu.VMEM(shape, kind) for shape, kind in scratch]
        + [
            pltpu.SemaphoreType.DMA((SENT,)),
            pltpu.SemaphoreType.DMA((RECEIVED,)),
            pltpu.SemaphoreType.DMA((6,)),
        ],
        compiler_params=pltpu.CompilerParams(
            collective_id=0, has_side_effects=True, vmem_limit_bytes=VMEM_BYTES
        ),
    )(
        inputs.reshape(4, 144, WIDTH),
        upstream.reshape(4, 144, WIDTH),
        w_qkv.transpose(1, 0, 2),
        w_out,
        action_ids,
        frame_time,
        action_table,
        gain.reshape(1, WIDTH),
    )
    grad_inputs, wq_sum, wo_sum, grad_gain, grad_actions = pl.pallas_call(
        finish_kernel,
        out_shape=tuple(jax.ShapeDtypeStruct(a.shape, a.dtype) for a in results),
        in_specs=[hbm] * 5,
        out_specs=(hbm,) * 5,
        scratch_shapes=[pltpu.VMEM(a.shape, a.dtype) for a in results]
        + [pltpu.SemaphoreType.DMA((2, 8))],
        compiler_params=pltpu.CompilerParams(vmem_limit_bytes=VMEM_BYTES),
    )(*results)
    return (
        grad_inputs.reshape(inputs.shape),
        wq_sum.transpose(1, 0, 2),
        wo_sum,
        grad_gain.reshape(WIDTH),
        grad_actions,
    )


def solution(mesh):
    return jax.shard_map(
        on_device,
        mesh=mesh,
        in_specs=(
            P(None, "frame", "space", None),
            P(None, "frame", "space", None),
            P(None, "frame"),
            P(),
            P(),
            P(),
            P(("frame", "space"), None, "tensor"),
            P(("frame", "space"), "tensor"),
        ),
        out_specs=(
            P(None, "frame", "space", None),
            P(("frame", "space"), None, "tensor"),
            P(("frame", "space"), "tensor"),
            P(),
            P(),
        ),
        check_vma=False,
    )
```
